512 devices in a mesh: blk: 16 (over z), uly: 8 (over x, core), dp: 4 (over y).
Axes of the slice: x: 4, y: 4, z: 16, core: 2. Of those that a mesh axis runs over, the one named last changes fastest.
Arguments:
- queries: bfloat16 [32768, 3072], P(('dp', 'blk', 'uly')), parts along dimension 0, may hold values from -6 to 6, as said below
- keys: bfloat16 [32768, 3072], P(('dp', 'blk', 'uly')), parts along dimension 0, may hold values from -6 to 6, as said below
- values: bfloat16 [32768, 3072], P(('dp', 'blk', 'uly')), parts along dimension 0, may hold values from -6 to 6
- tile_order: int32 [128], P('dp'), parts along dimension 0, may hold values from 0 to 31, as said below
- neighbors: int32 [128, 9], P('dp'), parts along dimension 0, may hold values from 0 to 31, as said below
Outputs:
- attended: bfloat16 [32768, 3072], P(('dp', 'blk', 'uly')), parts along dimension 0
The draws below stay inside these ranges and needn't reach their ends.
There are 4 independent parts, one for each index of `dp`. The reference program is written for one: setup_inputs(seed, part) draws one part's arguments, and reference() takes and returns one part's arrays. A program takes and returns all parts, laid end to end along the dimension named above; each array names one. Nothing has to cross between parts.
Inputs may be any that keep to these rules, and one draw needn't show every extreme that they name: `queries`: of order one; a few tokens carry larger entries. `keys`: of order one; a few tokens carry larger entries. `tile_order`: A permutation of the tile ids. The slots k * 4 to (k + 1) * 4 - 1 hold all tiles of one tile column w, and w = (k + r) % 8 with r drawn from the seed; index b of blk stores slots b * 2 to (b + 1) * 2 - 1. `neighbors`: row s lists, without repeats, the slots of all tiles with any time index, height index ch - 1, ch, ch + 1 and width index cw - 1, cw, cw + 1, where ch and cw are the height and width indices of the tile in slot s clamped to 1 .. 2 and 1 .. 6. Every listed slot lies in a shard (slot // 2) within cyclic distance 5 of shard s // 2, and distance 5 occurs.
All inputs are finite; a program needn't handle non-finite values.
Results may differ from the reference program's by a relative error of at most 0.0096.
Values may be sent and summed in bfloat16 or wider, within the bound.
No kernel may reach another device: no remote copies, remote signals or barrier semaphores. Data moves between devices by JAX's collectives and lax.ppermute only.
A program may use at most 64 MiB of HBM per device.

```python
import jax
import jax.numpy as jnp
from jax import lax

HEADS = 24
HD = 128
TILE_T = 4
TILE_H = 8
TILE_W = 8
TT = 1
TH = 4
TW = 8
NTILES = 32
TOK_TILE = 256
TOKENS = 8192
WIN = 9


def tile_layout(key):
    base = jax.random.fold_in(key, 7)
    first_key, second_key = jax.random.split(base)
    turn = jax.random.randint(first_key, (), 0, TW)
    column_keys = jax.random.split(second_key, TW)
    inner = jax.vmap(lambda single: jax.random.permutation(single, TT * TH))(column_keys)
    unit = jnp.arange(TW, dtype=jnp.int32)
    column = (unit + turn) % TW
    order = (inner.astype(jnp.int32) * TW + column[:, None]).reshape(-1)
    slot_of = jnp.zeros((NTILES,), jnp.int32).at[order].set(jnp.arange(NTILES, dtype=jnp.int32))
    centre_w = jnp.clip(order % TW, 1, TW - 2)
    centre_h = jnp.clip(order // TW % TH, 1, TH - 2)
    listed = []
    for frame_tile in range(TT):
        for step_h in range(-1, 2):
            for step_w in range(-1, 2):
                ident = (frame_tile * TH + centre_h + step_h) * TW + centre_w + step_w
                listed.append(jnp.take(slot_of, ident))
    return (order, jnp.stack(listed, axis=1).astype(jnp.int32))


def draw_tile_order(key, part):
    return tile_layout(key)[0]


def draw_neighbors(key, part):
    return tile_layout(key)[1]


def drawn_pair(key):
    width = HEADS * HD
    base_q = jnp.clip(jax.random.normal(jax.random.fold_in(key, 11), (TOKENS, width), jnp.float32), -5.0, 5.0)
    base_k = jnp.clip(jax.random.normal(jax.random.fold_in(key, 12), (TOKENS, width), jnp.float32), -5.0, 5.0)
    return (base_q, base_k)


def draw_queries(key, part):
    return drawn_pair(key)[0].astype(jnp.bfloat16)


def draw_keys(key, part):
    return drawn_pair(key)[1].astype(jnp.bfloat16)


def shard_levels(rng, extent, shards, low, top_value):
    gain = 1.0
    for position, parts in shards:
        steps = jax.random.uniform(jax.random.fold_in(jax.random.fold_in(rng, 6), position), (parts,), jnp.float32, low / len(shards), top_value / len(shards))
        gain = gain * jnp.repeat(jnp.exp(steps), extent[position] // parts).reshape((-1,) + (1,) * (len(extent) - 1 - position))
    return gain


def noise(own_key, dims, scale, limit, shards=(), held_as=jnp.bfloat16):
    values = jax.random.normal(own_key, dims, jnp.float32) * scale
    if len(shards) > 0:
        values = shard_levels(own_key, dims, shards, -0.22, 0.18) * values
    return jnp.clip(values, min=-limit, max=limit).astype(held_as)


def setup_inputs(seed: int = 0, part: int = 0) -> dict:
    splits = jax.random.split(jax.random.key(seed), 6)
    part_splits = jax.random.split(jax.random.fold_in(splits[5], part), 6)
    return {
        "queries": draw_queries(jax.random.fold_in(jax.random.fold_in(splits[5], part), 71), part),
        "keys": draw_keys(jax.random.fold_in(jax.random.fold_in(splits[5], part), 71), part),
        "values": noise(part_splits[2], (TOKENS, HEADS * HD), 1.0, 6.0, ((0, 128),)),
        "tile_order": draw_tile_order(jax.random.fold_in(jax.random.fold_in(splits[5], part), 71), part),
        "neighbors": draw_neighbors(jax.random.fold_in(jax.random.fold_in(splits[5], part), 71), part),
    }


def angle_tables(tokens, tile_order):
    slot = tokens // TOK_TILE
    local = tokens % TOK_TILE
    tile = jnp.take(tile_order, slot)
    frame = (tile // (TH * TW)) * TILE_T + local // (TILE_H * TILE_W)
    row = ((tile // TW) % TH) * TILE_H + (local // TILE_W) % TILE_H
    column = (tile % TW) * TILE_W + local % TILE_W
    dt = HD - 4 * (HD // 6)
    dhw = 2 * (HD // 6)
    freq_t = jnp.power(10000.0, -2.0 * jnp.arange(dt // 2, dtype=jnp.float32) / dt)
    freq_s = jnp.power(10000.0, -2.0 * jnp.arange(dhw // 2, dtype=jnp.float32) / dhw)
    angles = jnp.concatenate([frame.astype(jnp.float32)[:, None] * freq_t[None, :],
                              row.astype(jnp.float32)[:, None] * freq_s[None, :],
                              column.astype(jnp.float32)[:, None] * freq_s[None, :]], axis=1)
    return jnp.cos(angles), jnp.sin(angles)


def rotate(field, cosine, sine):
    rows = field.shape[0]
    pairs = field.astype(jnp.float32).reshape(rows, -1, HD // 2, 2)
    first = pairs[..., 0]
    second = pairs[..., 1]
    cosine = cosine[:, None, :]
    sine = sine[:, None, :]
    turned = jnp.stack([first * cosine - second * sine, first * sine + second * cosine], axis=-1)
    return turned.reshape(rows, -1).astype(jnp.bfloat16)


def reference(queries, keys, values, tile_order, neighbors):
    tokens = jnp.arange(TOKENS, dtype=jnp.int32)
    cosine, sine = angle_tables(tokens, tile_order)
    q_rot = rotate(queries, cosine, sine).reshape(NTILES, TOK_TILE, HEADS, HD)
    k_rot = rotate(keys, cosine, sine).reshape(NTILES, TOK_TILE, HEADS, HD)
    v_all = values.reshape(NTILES, TOK_TILE, HEADS, HD)
    scale = HD ** -0.5

    def one_tile(slot):
        picks = lax.dynamic_index_in_dim(neighbors, slot, 0, keepdims=False).astype(jnp.int32)
        q_tile = lax.dynamic_index_in_dim(q_rot, slot, 0, keepdims=False).astype(jnp.float32)
        k_tile = jnp.take(k_rot, picks, axis=0).reshape(WIN * TOK_TILE, HEADS, HD).astype(jnp.float32)
        v_tile = jnp.take(v_all, picks, axis=0).reshape(WIN * TOK_TILE, HEADS, HD).astype(jnp.float32)
        scores = jnp.einsum('qhd,khd->hqk', q_tile, k_tile) * scale
        top = jnp.max(scores, axis=-1, keepdims=True)
        weights = jnp.exp(scores - top)
        total = jnp.sum(weights, axis=-1)
        weights_bf = weights.astype(jnp.bfloat16).astype(jnp.float32)
        summed = jnp.einsum('hqk,khd->qhd', weights_bf, v_tile)
        result = summed / jnp.transpose(total)[:, :, None]
        return result.reshape(TOK_TILE, HEADS * HD).astype(jnp.bfloat16)

    attended = lax.map(one_tile, jnp.arange(NTILES, dtype=jnp.int32))
    return attended.reshape(TOKENS, HEADS * HD)
```

```python
import functools

import jax
import jax.numpy as jnp
import numpy as np
from jax import lax
from jax.experimental import pallas as pl
from jax.experimental.pallas import tpu as pltpu
from jax.sharding import Mesh
from jax.sharding import PartitionSpec as P

HD = 128
TOK_TILE = 256
WIN = 9
COLS = 8
GROUP = ("half", "x", "core")
VMEM = pl.BlockSpec(memory_space=pltpu.VMEM)
SMEM = pl.BlockSpec(memory_space=pltpu.SMEM)
BF = jnp.bfloat16
F32 = jnp.float32
LIMIT = 48 * 1024 * 1024


def frequencies():
    pair = np.arange(HD) // 2
    dt = HD - 4 * (HD // 6)
    dhw = 2 * (HD // 6)
    nt, ns = dt // 2, dhw // 2
    kind = np.where(pair < nt, 0, np.where(pair < nt + ns, 1, 2))
    within = np.where(kind == 0, pair, np.where(kind == 1, pair - nt, pair - nt - ns))
    freq = np.power(10000.0, -2.0 * within / np.where(kind == 0, dt, dhw))
    table = np.zeros((8, HD), np.float32)
    table[0] = freq
    for which in range(3):
        table[1 + which] = np.where(kind == which, freq, 0.0)
    return table


def rotate_kernel(meta, freq, q_ref, k_ref, v_ref, out_ref):
    tile = meta[2]
    frame = (tile // 32 * 4 + meta[3]).astype(F32)
    row0 = (tile // 8 % 4 * 8).astype(F32)
    col0 = (tile % 8 * 8).astype(F32)
    rows = q_ref.shape[0]
    token = lax.broadcasted_iota(jnp.int32, (rows, HD), 0)
    row = row0 + (token // 8).astype(F32)
    col = col0 + (token % 8).astype(F32)
    angle = frame * freq[1:2, :] + row * freq[2:3, :] + col * freq[3:4, :]
    cosine = jnp.cos(angle)
    sine = jnp.sin(angle)
    even = lax.broadcasted_iota(jnp.int32, (rows, HD), 1) % 2 == 0
    from_next = jnp.where(even, -sine, 0.0)
    from_last = jnp.where(even, 0.0, sine)
    scale = HD ** (-0.5) * 1.4426950408889634

    def turned(x, c, n, l):
        x = x.astype(F32)
        return (x * c + pltpu.roll(x, HD - 1, 1) * n + pltpu.roll(x, 1, 1) * l).astype(BF)

    qc, qn, ql = cosine * scale, from_next * scale, from_last * scale
    for which, ref in enumerate((q_ref, k_ref, v_ref)):
        for g in range(8):
            for h in range(3):
                x = ref[:, (3 * g + h) * HD : (3 * g + h + 1) * HD]
                if which == 0:
                    x = turned(x, qc, qn, ql)
                elif which == 1:
                    x = turned(x, cosine, from_next, from_last)
                if h < 2:
                    out_ref[2 * g + h, which, 0:64, :] = x
                else:
                    out_ref[2 * g, which, 64:96, :] = x[0:32]
                    out_ref[2 * g + 1, which, 64:96, :] = x[32:64]


def attend(q, kp, vp, picks, s_ref):
    rows = q.shape[0]
    top = None
    for j in range(WIN):
        s = lax.dot_general(q, kp[picks[j]], (((1,), (1,)), ((), ())), preferred_element_type=F32)
        s_ref[j, 0:rows, :] = s
        top = s if top is None else jnp.maximum(top, s)
    top = jnp.max(top, axis=1, keepdims=True)
    total = jnp.zeros((rows, TOK_TILE), F32)
    acc = jnp.zeros((rows, HD), F32)
    for j in range(WIN):
        p = jnp.exp2(s_ref[j, 0:rows, :] - top)
        total = total + p
        acc = acc + jnp.dot(p.astype(BF), vp[picks[j]], preferred_element_type=F32)
    return (acc / jnp.sum(total, axis=1, keepdims=True)).astype(BF)


def attention_kernel(
    meta, nb, own, r1, r2, r3, l1, l2, l3, s0, sx, sy, o_own, o_oth, kh, vh, k2, v2, s_ref
):
    k = meta[0]
    w = meta[1]
    for t in range(4):
        rows = slice(t * TOK_TILE, (t + 1) * TOK_TILE)
        kh[t] = own[4 * t : 4 * t + 4, 1, 0:64, :].reshape(TOK_TILE, HD)
        vh[t] = own[4 * t : 4 * t + 4, 2, 0:64, :].reshape(TOK_TILE, HD)
        kh[4 + t] = r2[rows]
        vh[4 + t] = r3[rows]
        kh[8 + t] = l2[rows]
        vh[8 + t] = l3[rows]

    def shared(base, mine, other):
        for t in range(4):
            rk = slice(t * 128, (t + 1) * 128)
            rv = slice(512 + t * 128, 512 + (t + 1) * 128)
            k2[base + t, 128:256] = other[rk]
            v2[base + t, 128:256] = other[rv]
            k2[base + t, 0:128] = mine[rk]
            v2[base + t, 0:128] = mine[rv]

    for t in range(4):
        k2[t, 0:128] = own[4 * t : 4 * t + 4, 1, 64:96, :].reshape(128, HD)
        v2[t, 0:128] = own[4 * t : 4 * t + 4, 2, 64:96, :].reshape(128, HD)
        k2[t, 128:256] = s0[t * 128 : (t + 1) * 128]
        v2[t, 128:256] = s0[512 + t * 128 : 512 + (t + 1) * 128]

    @pl.when(w != 7)
    def _():
        shared(4, r1, sx)

    @pl.when(w == 7)
    def _():
        shared(4, l1, sx)
        shared(8, l2, sy)

    @pl.when(w == 0)
    def _():
        shared(8, r2, sy)

    @pl.when((w != 0) & (w != 7))
    def _():
        shared(8, l1, sy)

    from_left = (w == 1) | (w == 7)
    k_oth = lax.rem(jnp.where(from_left, k + 7, k + 1), 8)
    near = jnp.where(w == 7, 7, 1)

    def picks_of(slot, one):
        picks = []
        for j in range(WIN):
            n = nb[slot, j]
            d = lax.rem(n // 4 - k + 8, 8)
            picks.append(jnp.where(d == 0, 0, jnp.where(d == one, 4, 8)) + lax.rem(n, 4))
        return picks

    edge = (w == 0) | (w == 7)
    inner = (w == 1) | (w == 6)

    @pl.when(inner)
    def _():
        @pl.loop(0, 4)
        def _(t):
            rows = pl.ds(pl.multiple_of(t * TOK_TILE, TOK_TILE), TOK_TILE)
            q = jnp.where(from_left, l1[rows], r1[rows])
            o_oth[rows] = attend(q, kh, vh, picks_of(k_oth * 4 + t, 1), s_ref)

    @pl.when(edge)
    def _():
        @pl.loop(0, 4)
        def _(t):
            rows = pl.ds(pl.multiple_of(t * 128, 128), 128)
            q = jnp.where(from_left, l3[rows], r3[rows])
            o_oth[rows] = attend(q, k2, v2, picks_of(k_oth * 4 + t, near), s_ref)

    @pl.when(jnp.logical_not(edge))
    def _():
        @pl.loop(0, 4)
        def _(t):
            q = own[pl.ds(t * 4, 4), 0, 0:64, :].reshape(TOK_TILE, HD)
            o = attend(q, kh, vh, picks_of(k * 4 + t, 1), s_ref)
            o_own[pl.ds(t * 4, 4), 0:64, :] = o.reshape(4, 64, HD)

    @pl.when(jnp.logical_not(inner))
    def _():
        @pl.loop(0, 4)
        def _(t):
            q = own[pl.ds(t * 4, 4), 0, 64:96, :].reshape(128, HD)
            o = attend(q, k2, v2, picks_of(k * 4 + t, near), s_ref)
            o_own[pl.ds(t * 4, 4), 64:96, :] = o.reshape(4, 32, HD)


def unpack_kernel(in_ref, out_ref):
    for g in range(8):
        for h in range(2):
            out_ref[:, (3 * g + h) * HD : (3 * g + h + 1) * HD] = in_ref[2 * g + h, 0:64, :]
        last = slice((3 * g + 2) * HD, (3 * g + 3) * HD)
        out_ref[0:32, last] = in_ref[2 * g, 64:96, :]
        out_ref[32:64, last] = in_ref[2 * g + 1, 64:96, :]


def along_columns(block, distance):
    n = 2 * COLS
    return lax.ppermute(block, ("col", "half"), [(i, (i + 2 * distance) % n) for i in range(n)])


def swapped(block):
    return lax.ppermute(block, "core", [(0, 1), (1, 0)])


def shards(freq, queries, keys, values, tile_order, neighbors):
    col = lax.axis_index("col")
    half = lax.axis_index("half")
    x = lax.axis_index("x")
    core = lax.axis_index("core")
    slot = col * 4 + half * 2 + x // 2
    w = tile_order[col * 4] % COLS
    meta = jnp.stack([col, w, tile_order[slot], (x % 2) * 2 + core]).astype(jnp.int32)
    packed = pl.pallas_call(
        rotate_kernel,
        out_shape=jax.ShapeDtypeStruct((16, 3, 96, HD), BF),
        in_specs=[SMEM, VMEM, VMEM, VMEM, VMEM],
        out_specs=VMEM,
        compiler_params=pltpu.CompilerParams(vmem_limit_bytes=LIMIT),
        name="rotate",
    )(meta, freq, queries, keys, values)
    own = lax.all_to_all(packed, GROUP, split_axis=0, concat_axis=0, tiled=True)
    q_head = own[:, 0, 0:64].reshape(1024, HD)
    k_head = own[:, 1, 0:64].reshape(1024, HD)
    v_head = own[:, 2, 0:64].reshape(1024, HD)
    q_shared = own[:, 0, 64:96].reshape(512, HD)
    kv_shared = jnp.concatenate(
        [own[:, 1, 64:96].reshape(512, HD), own[:, 2, 64:96].reshape(512, HD)]
    )
    q_shared = jnp.concatenate([q_shared, q_shared])
    s0 = swapped(kv_shared)
    r1 = along_columns(jnp.where(w == 7, q_head, kv_shared), -1)
    l1 = along_columns(jnp.where(w == 0, q_head, kv_shared), 1)
    r3 = along_columns(jnp.where(w == 1, q_shared, v_head), -1)
    l3 = along_columns(jnp.where(w == 6, q_shared, v_head), 1)
    r2 = along_columns(jnp.where(w == 1, r1, k_head), -1)
    l2 = along_columns(jnp.where(w == 6, l1, k_head), 1)
    sx = swapped(jnp.where(w == 7, l1, r1))
    sy = swapped(jnp.where(w == 0, r2, jnp.where(w == 7, l2, l1)))
    o_own, o_oth = pl.pallas_call(
        attention_kernel,
        out_shape=(
            jax.ShapeDtypeStruct((16, 96, HD), BF),
            jax.ShapeDtypeStruct((1024, HD), BF),
        ),
        in_specs=[SMEM, SMEM] + [VMEM] * 10,
        out_specs=(VMEM, VMEM),
        scratch_shapes=[pltpu.VMEM((12, TOK_TILE, HD), BF)] * 4
        + [pltpu.VMEM((WIN, TOK_TILE, TOK_TILE), F32)],
        compiler_params=pltpu.CompilerParams(vmem_limit_bytes=LIMIT),
        name="attend",
    )(meta, neighbors, own, r1, r2, r3, l1, l2, l3, s0, sx, sy)
    o_right = along_columns(o_oth, -1)
    o_left = along_columns(o_oth, 1)
    o_head = jnp.where(
        w == 0,
        o_right.reshape(16, 64, HD),
        jnp.where(w == 7, o_left.reshape(16, 64, HD), o_own[:, 0:64]),
    )
    o_shared = jnp.where(
        w == 1,
        o_left[0:512].reshape(16, 32, HD),
        jnp.where(w == 6, o_right[0:512].reshape(16, 32, HD), o_own[:, 64:96]),
    )
    sent = jnp.concatenate([o_head, o_shared], axis=1)
    back = lax.all_to_all(sent, GROUP, split_axis=0, concat_axis=0, tiled=True)
    return pl.pallas_call(
        unpack_kernel,
        out_shape=jax.ShapeDtypeStruct(queries.shape, BF),
        in_specs=[VMEM],
        out_specs=VMEM,
        compiler_params=pltpu.CompilerParams(vmem_limit_bytes=LIMIT),
        name="unpack",
    )(back)


def solution(mesh):
    blk, uly, dp = (mesh.shape[name] for name in ("blk", "uly", "dp"))
    fine = Mesh(
        mesh.devices.reshape(blk // 2, 2, uly // 2, 2, dp), ("col", "half", "x", "core", "dp")
    )
    tokens = ("dp", "col", "half", "x", "core")
    placed = (P(), P(tokens, None), P(tokens, None), P(tokens, None), P("dp"), P("dp", None))
    body = jax.shard_map(
        shards, mesh=fine, in_specs=placed, out_specs=P(tokens, None), check_vma=False
    )

    def run(queries, keys, values, tile_order, neighbors):
        return body(jnp.asarray(frequencies()), queries, keys, values, tile_order, neighbors)

    return run
```

```python
import functools

import jax
import jax.numpy as jnp
import numpy as np
from jax import lax
from jax.experimental import pallas as pl
from jax.experimental.pallas import tpu as pltpu
from jax.sharding import Mesh
from jax.sharding import PartitionSpec as P

HD = 128
TOK_TILE = 256
WIN = 9
COLS = 8
GROUP = ("half", "x", "core")
VMEM = pl.BlockSpec(memory_space=pltpu.VMEM)
SMEM = pl.BlockSpec(memory_space=pltpu.SMEM)
BF = jnp.bfloat16
F32 = jnp.float32
LIMIT = 48 * 1024 * 1024


def frequency_rows():
    pair = lax.broadcasted_iota(jnp.int32, (8, HD), 1) // 2
    nt = (HD - 4 * (HD // 6)) // 2
    ns = HD // 6
    rows = []
    for first, count in ((0, nt), (nt, ns), (nt + ns, ns)):
        within = (pair - first).astype(F32)
        freq = jnp.exp(within * float(-np.log(10000.0) / count))
        rows.append(jnp.where((pair >= first) & (pair < first + count), freq, 0.0)[0:1])
    return rows


def rotate_kernel(order, q_hbm, k_hbm, v_hbm, kv_ref, qv_ref, held, sems):
    x = lax.axis_index("x")
    frame_in_tile = lax.rem(x, 2) * 2 + lax.axis_index("core")
    slot = lax.axis_index("col") * 4 + lax.axis_index("half") * 2 + x // 2
    rows = held.shape[1]
    width = 2 * 3 * HD
    copies = []
    for part in range(4):
        for which, ref in enumerate((k_hbm, q_hbm, v_hbm)):
            columns = pl.ds(part * width, width)
            copies.append(
                pltpu.make_async_copy(
                    ref.at[:, columns], held.at[which, :, columns], sems.at[3 * part + which]
                )
            )
    for copy in copies:
        copy.start()
    tile = order[slot]
    frame = (tile // 32 * 4 + frame_in_tile).astype(F32)
    row0 = (tile // 8 % 4 * 8).astype(F32)
    col0 = (tile % 8 * 8).astype(F32)
    token = lax.broadcasted_iota(jnp.int32, (rows, HD), 0)
    row = row0 + (token // 8).astype(F32)
    col = col0 + (token % 8).astype(F32)
    by_frame, by_row, by_col = frequency_rows()
    angle = frame * by_frame + row * by_row + col * by_col
    cosine = jnp.cos(angle)
    sine = jnp.sin(angle)
    even = lax.broadcasted_iota(jnp.int32, (rows, HD), 1) % 2 == 0
    from_next = jnp.where(even, -sine, 0.0)
    from_last = jnp.where(even, 0.0, sine)
    scale = HD ** (-0.5) * 1.4426950408889634

    def turned(x, c, n, l):
        x = x.astype(F32)
        return (x * c + pltpu.roll(x, HD - 1, 1) * n + pltpu.roll(x, 1, 1) * l).astype(BF)

    qc, qn, ql = cosine * scale, from_next * scale, from_last * scale
    for part in range(4):
        for which in range(3):
            copies[3 * part + which].wait()
            for g in range(2 * part, 2 * part + 2):
                for h in range(3):
                    y = held[which, :, (3 * g + h) * HD : (3 * g + h + 1) * HD]
                    if which == 0:
                        y = turned(y, cosine, from_next, from_last)
                        out, head_row, shared_row = kv_ref, 0, 64
                    elif which == 1:
                        y = turned(y, qc, qn, ql)
                        out, head_row, shared_row = qv_ref, 0, 64
                    else:
                        out, head_row, shared_row = qv_ref, 96, 96
                    if h < 2:
                        out[2 * g + h, head_row : head_row + 64, :] = y
                    else:
                        if which == 2:
                            out = kv_ref
                        out[2 * g, shared_row : shared_row + 32, :] = y[0:32]
                        out[2 * g + 1, shared_row : shared_row + 32, :] = y[32:64]


def attend(q, kp, vp, picks, s_ref):
    rows = q.shape[0]
    top = None
    for j in range(WIN):
        s = lax.dot_general(q, kp[picks[j]], (((1,), (1,)), ((), ())), preferred_element_type=F32)
        s_ref[j, 0:rows, :] = s
        top = s if top is None else jnp.maximum(top, s)
    top = jnp.max(top, axis=1, keepdims=True)
    total = jnp.zeros((rows, TOK_TILE), F32)
    acc = jnp.zeros((rows, HD), F32)
    for j in range(WIN):
        p = jnp.exp2(s_ref[j, 0:rows, :] - top)
        total = total + p
        acc = acc + jnp.dot(p.astype(BF), vp[picks[j]], preferred_element_type=F32)
    return (acc / jnp.sum(total, axis=1, keepdims=True)).astype(BF)


def place(order):
    k = lax.axis_index("col")
    w = lax.rem(order[k * 4], COLS)
    from_left = (w == 1) | (w == 7)
    k_oth = lax.rem(jnp.where(from_left, k + 7, k + 1), COLS)
    return k, w, k_oth


def picks_of(nb, k, slot, one):
    picks = []
    for j in range(WIN):
        n = nb[slot, j]
        d = lax.rem(n // 4 - k + 8, 8)
        picks.append(jnp.where(d == 0, 0, jnp.where(d == one, 4, 8)) + lax.rem(n, 4))
    return picks


def whole(ref, *index):
    return ref[index].reshape(-1, HD)


def fill_head(w, kv, qv, r1, r2, l1, l2, kh, vh):
    for t in range(4):
        four = slice(4 * t, 4 * t + 4)
        kh[t] = whole(kv, four, slice(0, 64))
        vh[t] = whole(qv, four, slice(96, 160))
        vh[4 + t] = whole(r2, 1, four)
        vh[8 + t] = whole(l2, 1, four)

    for base, special, early, late in ((4, 6, r1, r2), (8, 1, l1, l2)):
        for condition, first in ((w == special, True), (w != special, False)):

            @pl.when(condition)
            def _(base=base, first=first, early=early, late=late):
                for t in range(4):
                    four = slice(4 * t, 4 * t + 4)
                    kh[base + t] = whole(early, four) if first else whole(late, 0, four)


def fill_shared(w, kv, r1, r2, l1, l2, sw, se, k2, v2):
    def put(base, mine, other):
        for t in range(4):
            four = slice(4 * t, 4 * t + 4)
            for pool, part in ((k2, slice(0, 32)), (v2, slice(32, 64))):
                pool[base + t, 0:128] = mine(four, part)
                pool[base + t, 128:256] = other(four, part)

    put(
        0,
        lambda f, p: whole(kv, f, slice(64 + p.start, 64 + p.stop)),
        lambda f, p: whole(sw, 0, f, p),
    )

    @pl.when(w != 7)
    def _():
        put(4, lambda f, p: whole(r1, f, p), lambda f, p: whole(sw, 2, f, p))

    @pl.when(w == 7)
    def _():
        put(4, lambda f, p: whole(l1, f, p), lambda f, p: whole(sw, 1, f, p))
        put(8, lambda f, p: whole(l2, 0, f, p), lambda f, p: whole(se, f, p))

    @pl.when(w == 0)
    def _():
        put(8, lambda f, p: whole(r2, 0, f, p), lambda f, p: whole(se, f, p))

    @pl.when((w != 0) & (w != 7))
    def _():
        put(8, lambda f, p: whole(l1, f, p), lambda f, p: whole(sw, 1, f, p))


def first_kernel(order, nb, kv, qv, r1, r2, l1, l2, o_head, o_oth, kh, vh, s_ref):
    k, w, k_oth = place(order)
    inner = (w == 1) | (w == 6)
    edge = (w == 0) | (w == 7)

    @pl.when(jnp.logical_not(edge))
    def _():
        fill_head(w, kv, qv, r1, r2, l1, l2, kh, vh)

    @pl.when(inner)
    def _():
        @pl.loop(0, 4)
        def _(t):
            four = pl.ds(t * 4, 4)
            q = jnp.where(w == 1, whole(l2, 0, four), whole(r2, 0, four))
            o = attend(q, kh, vh, picks_of(nb, k, k_oth * 4 + t, 1), s_ref)
            o_oth[four] = o.reshape(4, 64, HD)

    @pl.when(jnp.logical_not(inner | edge))
    def _():
        @pl.loop(0, 4)
        def _(t):
            four = pl.ds(t * 4, 4)
            q = whole(qv, four, slice(0, 64))
            o = attend(q, kh, vh, picks_of(nb, k, k * 4 + t, 1), s_ref)
            o_head[four] = o.reshape(4, 64, HD)


def edge_kernel(order, nb, kv, r1, r2, l1, l2, sw, se, o_in, o_oth, k2, v2, s_ref):
    del o_in
    k, w, k_oth = place(order)
    near = jnp.where(w == 7, 7, 1)

    @pl.when((w == 0) | (w == 7))
    def _():
        fill_shared(w, kv, r1, r2, l1, l2, sw, se, k2, v2)

        @pl.loop(0, 4)
        def _(t):
            four = pl.ds(t * 4, 4)
            q = jnp.where(
                w == 7, whole(l2, 1, four, slice(0, 32)), whole(r2, 1, four, slice(0, 32))
            )
            o = attend(q, k2, v2, picks_of(nb, k, k_oth * 4 + t, near), s_ref)
            o_oth[four, 0:32] = o.reshape(4, 32, HD)


def last_kernel(
    order, nb, kv, qv, r1, r2, l1, l2, sw, se, o_first, o_head, o_shared, kh, vh, k2, v2, s_ref
):
    k, w, _ = place(order)
    inner = (w == 1) | (w == 6)
    near = jnp.where(w == 7, 7, 1)

    @pl.when(inner)
    def _():
        fill_head(w, kv, qv, r1, r2, l1, l2, kh, vh)

        @pl.loop(0, 4)
        def _(t):
            four = pl.ds(t * 4, 4)
            q = whole(qv, four, slice(0, 64))
            o = attend(q, kh, vh, picks_of(nb, k, k * 4 + t, 1), s_ref)
            o_head[four] = o.reshape(4, 64, HD)

    @pl.when(jnp.logical_not(inner))
    def _():
        o_head[...] = o_first[...]
        fill_shared(w, kv, r1, r2, l1, l2, sw, se, k2, v2)

        @pl.loop(0, 4)
        def _(t):
            four = pl.ds(t * 4, 4)
            q = whole(qv, four, slice(64, 96))
            o = attend(q, k2, v2, picks_of(nb, k, k * 4 + t, near), s_ref)
            o_shared[four] = o.reshape(4, 32, HD)


def unpack_kernel(in_ref, out_ref):
    for g in range(8):
        for h in range(2):
            out_ref[:, (3 * g + h) * HD : (3 * g + h + 1) * HD] = in_ref[2 * g + h, 0:64, :]
        last = slice((3 * g + 2) * HD, (3 * g + 3) * HD)
        out_ref[0:32, last] = in_ref[2 * g, 64:96, :]
        out_ref[32:64, last] = in_ref[2 * g + 1, 64:96, :]


def along_columns(block, distance):
    n = 2 * COLS
    return lax.ppermute(block, ("col", "half"), [(i, (i + 2 * distance) % n) for i in range(n)])


def swapped(block):
    return lax.ppermute(block, "core", [(0, 1), (1, 0)])


POOL = pltpu.VMEM((12, TOK_TILE, HD), BF)
SCORES = pltpu.VMEM((WIN, TOK_TILE, TOK_TILE), F32)


def kernel(body, name, shapes, inputs, scratch=(), memory=None, aliases={}, limit=LIMIT):
    specs = [SMEM] * sum(i.dtype == jnp.int32 for i in inputs)
    specs += [memory or VMEM] * (len(inputs) - len(specs))
    return pl.pallas_call(
        body,
        out_shape=tuple(jax.ShapeDtypeStruct(shape, BF) for shape in shapes),
        in_specs=specs,
        out_specs=(VMEM,) * len(shapes),
        scratch_shapes=list(scratch),
        input_output_aliases=aliases,
        compiler_params=pltpu.CompilerParams(vmem_limit_bytes=limit),
        name=name,
    )(*inputs)


def shards(queries, keys, values, order, nb):
    w = order[lax.axis_index("col") * 4] % COLS
    kv, qv = kernel(
        rotate_kernel,
        "rotate",
        ((16, 128, HD), (16, 160, HD)),
        (order, queries, keys, values),
        (pltpu.VMEM((3,) + queries.shape, BF), pltpu.SemaphoreType.DMA((12,))),
        memory=pl.BlockSpec(memory_space=pl.ANY),
        limit=60 * 1024 * 1024,
    )
    kv = lax.all_to_all(kv, GROUP, split_axis=0, concat_axis=0, tiled=True)
    k_head, shared = kv[:, 0:64], kv[:, 64:128]
    r1 = along_columns(jnp.where(w == 7, k_head, shared), -1)
    l1 = along_columns(jnp.where(w == 0, k_head, shared), 1)
    qv = lax.all_to_all(qv, GROUP, split_axis=0, concat_axis=0, tiled=True)
    q_head, q_shared, v_head = qv[:, 0:64], qv[:, 64:128], qv[:, 96:160]

    def second(early, near_edge, far_edge):
        return jnp.stack(
            [
                jnp.where(w == near_edge, early, jnp.where(w == far_edge, q_head, k_head)),
                jnp.where(w == near_edge, q_shared, v_head),
            ]
        )

    r2 = along_columns(second(r1, 1, 7), -1)
    l2 = along_columns(second(l1, 6, 0), 1)
    sw = swapped(jnp.stack([shared, l1, r1]))
    se = swapped(jnp.where(w == 0, r2[0], l2[0]))
    o_first, o_oth = kernel(
        first_kernel,
        "attend_first",
        ((16, 64, HD), (16, 64, HD)),
        (order, nb, kv, qv, r1, r2, l1, l2),
        (POOL, POOL, SCORES),
    )
    (o_oth,) = kernel(
        edge_kernel,
        "attend_edge",
        ((16, 64, HD),),
        (order, nb, kv, r1, r2, l1, l2, sw, se, o_oth),
        (POOL, POOL, SCORES),
        aliases={9: 0},
    )
    o_right = along_columns(o_oth, -1)
    o_left = along_columns(o_oth, 1)
    o_head, o_shared = kernel(
        last_kernel,
        "attend_last",
        ((16, 64, HD), (16, 32, HD)),
        (order, nb, kv, qv, r1, r2, l1, l2, sw, se, o_first),
        (POOL, POOL, POOL, POOL, SCORES),
    )
    o_head = jnp.where(w == 0, o_right, jnp.where(w == 7, o_left, o_head))
    o_shared = jnp.where(
        w == 1, o_left[:, 0:32], jnp.where(w == 6, o_right[:, 0:32], o_shared)
    )
    sent = jnp.concatenate([o_head, o_shared], axis=1)
    back = lax.all_to_all(sent, GROUP, split_axis=0, concat_axis=0, tiled=True)
    return kernel(unpack_kernel, "unpack", (queries.shape,), (back,))[0]


def solution(mesh):
    blk, uly, dp = (mesh.shape[name] for name in ("blk", "uly", "dp"))
    fine = Mesh(
        mesh.devices.reshape(blk // 2, 2, uly // 2, 2, dp), ("col", "half", "x", "core", "dp")
    )
    tokens = ("dp", "col", "half", "x", "core")
    placed = (P(tokens, None), P(tokens, None), P(tokens, None), P("dp"), P("dp", None))
    return jax.shard_map(
        shards, mesh=fine, in_specs=placed, out_specs=P(tokens, None), check_vma=False
    )
```

```python
import jax
import jax.numpy as jnp
import numpy as np
from jax import lax
from jax.experimental import pallas as pl
from jax.experimental.pallas import tpu as pltpu
from jax.sharding import Mesh
from jax.sharding import PartitionSpec as P

HD = 128
TOK_TILE = 256
WIN = 9
COLS = 8
GROUP = ("half", "x", "core")
VMEM = pl.BlockSpec(memory_space=pltpu.VMEM)
SMEM = pl.BlockSpec(memory_space=pltpu.SMEM)
ANY = pl.BlockSpec(memory_space=pl.ANY)
BF = jnp.bfloat16
F32 = jnp.float32
MIB = 1024 * 1024
MAIN, VALUE, QUERY, REST = slice(0, 64), slice(64, 128), slice(128, 160), slice(160, 224)
AT_W, AT_HEAD, AT_SHARED = 0, 16, 96


def frequency_rows():
    pair = lax.broadcasted_iota(jnp.int32, (8, HD), 1) // 2
    nt = (HD - 4 * (HD // 6)) // 2
    ns = HD // 6
    rows = []
    for first, count in ((0, nt), (nt, ns), (nt + ns, ns)):
        within = (pair - first).astype(F32)
        freq = jnp.exp(within * float(-np.log(10000.0) / count))
        rows.append(jnp.where((pair >= first) & (pair < first + count), freq, 0.0)[0:1])
    return rows


def plan(order, nb, table):
    k = lax.axis_index("col")
    w = lax.rem(order[k * 4], COLS)
    table[AT_W] = w
    k_oth = lax.rem(jnp.where((w == 1) | (w == 7), k + 7, k + 1), COLS)
    near = jnp.where(w == 7, 7, 1)
    for u in range(8):
        slot = k_oth * 4 + u if u < 4 else k * 4 + u - 4
        for j in range(WIN):
            n = nb[j, slot]
            d = lax.rem(n // 4 - k + COLS, COLS)
            t = lax.rem(n, 4)
            table[AT_HEAD + WIN * u + j] = jnp.where(d == 0, 0, jnp.where(d == 1, 4, 8)) + t
            table[AT_SHARED + WIN * u + j] = jnp.where(d == 0, 0, jnp.where(d == near, 4, 8)) + t
    return w


def rotate_kernel(order, nb, q_hbm, k_hbm, v_hbm, one, two, table, held, sems):
    x = lax.axis_index("x")
    frame_in_tile = lax.rem(x, 2) * 2 + lax.axis_index("core")
    slot = lax.axis_index("col") * 4 + lax.axis_index("half") * 2 + x // 2
    rows = held.shape[1]
    width = 2 * 3 * HD
    copies = []
    for part in range(4):
        for which, ref in enumerate((k_hbm, q_hbm, v_hbm)):
            columns = pl.ds(part * width, width)
            copies.append(
                pltpu.make_async_copy(
                    ref.at[:, columns], held.at[which, :, columns], sems.at[3 * part + which]
                )
            )
    for copy in copies:
        copy.start()
    w = plan(order, nb, table)
    edge = (w == 0) | (w == 7)
    tile = order[slot]
    frame = (tile // 32 * 4 + frame_in_tile).astype(F32)
    row0 = (tile // 8 % 4 * 8).astype(F32)
    col0 = (tile % 8 * 8).astype(F32)
    token = lax.broadcasted_iota(jnp.int32, (rows, HD), 0)
    row = row0 + (token // 8).astype(F32)
    col = col0 + (token % 8).astype(F32)
    by_frame, by_row, by_col = frequency_rows()
    angle = frame * by_frame + row * by_row + col * by_col
    cosine = jnp.cos(angle)
    sine = jnp.sin(angle)
    even = lax.broadcasted_iota(jnp.int32, (rows, HD), 1) % 2 == 0
    from_next = jnp.where(even, -sine, 0.0)
    from_last = jnp.where(even, 0.0, sine)
    scale = HD ** (-0.5) * 1.4426950408889634

    def turned(x, c, n, l):
        x = x.astype(F32)
        return (x * c + pltpu.roll(x, HD - 1, 1) * n + pltpu.roll(x, 1, 1) * l).astype(BF)

    qc, qn, ql = cosine * scale, from_next * scale, from_last * scale
    for part in range(4):
        for which in range(3):
            copies[3 * part + which].wait()
        for g in range(2 * part, 2 * part + 2):
            for h in range(3):
                at = slice((3 * g + h) * HD, (3 * g + h + 1) * HD)
                key = turned(held[0, :, at], cosine, from_next, from_last)
                query = turned(held[1, :, at], qc, qn, ql)
                value = held[2, :, at]
                if h < 2:
                    to = 2 * g + h
                    two[to, VALUE, :] = value

                    @pl.when(edge)
                    def _(to=to, key=key, query=query):
                        one[to] = key
                        two[to, MAIN, :] = query

                    @pl.when(jnp.logical_not(edge))
                    def _(to=to, key=key, query=query):
                        two[to, MAIN, :] = key
                        two[to, REST, :] = query

                else:
                    for c in range(2):
                        to = 2 * g + c
                        part_of = slice(32 * c, 32 * c + 32)
                        two[to, QUERY, :] = query[part_of]

                        @pl.when(edge)
                        def _(to=to, part_of=part_of, key=key, value=value):
                            two[to, REST.start : REST.start + 32, :] = key[part_of]
                            two[to, REST.start + 32 : REST.stop, :] = value[part_of]

                        @pl.when(jnp.logical_not(edge))
                        def _(to=to, part_of=part_of, key=key, value=value):
                            one[to, 0:32, :] = key[part_of]
                            one[to, 32:64, :] = value[part_of]


def second_kernel(table, one, two, l1, r1, main_left, main_right, value_left, value_right, swap):
    w = table[AT_W]

    @pl.when(w == 1)
    def _():
        main_left[...] = r1[...]
        value_left[:, 0:32] = two[:, QUERY]
        value_left[:, 32:64] = two[:, QUERY]

    @pl.when(w != 1)
    def _():
        main_left[...] = two[:, MAIN]
        value_left[...] = two[:, VALUE]

    @pl.when(w == 6)
    def _():
        main_right[...] = l1[...]
        value_right[:, 0:32] = two[:, QUERY]
        value_right[:, 32:64] = two[:, QUERY]

    @pl.when(w != 6)
    def _():
        main_right[...] = two[:, MAIN]
        value_right[...] = two[:, VALUE]

    @pl.when((w == 0) | (w == 7))
    def _():
        swap[0] = two[:, REST]

    @pl.when((w != 0) & (w != 7))
    def _():
        swap[0] = one[...]

    swap[1] = l1[...]
    swap[2] = r1[...]


def attend(q, kp, vp, picks, s_ref):
    rows = q.shape[0]
    top = None
    for j in range(WIN):
        s = lax.dot_general(q, kp[picks[j]], (((1,), (1,)), ((), ())), preferred_element_type=F32)
        s_ref[j, 0:rows, :] = s
        top = s if top is None else jnp.maximum(top, s)
    top = jnp.max(top, axis=1, keepdims=True)
    total = jnp.zeros((rows, TOK_TILE), F32)
    acc = jnp.zeros((rows, HD), F32)
    for j in range(WIN):
        p = jnp.exp2(s_ref[j, 0:rows, :] - top)
        total = total + p
        acc = acc + jnp.dot(p.astype(BF), vp[picks[j]], preferred_element_type=F32)
    return (acc / jnp.sum(total, axis=1, keepdims=True)).astype(BF)


def picks_of(table, at, u):
    return [table[at + u * WIN + j] for j in range(WIN)]


def whole(ref, *index):
    return ref[index].reshape(-1, HD)


def fill_shared(base, mine, other, k2, v2):
    for t in range(4):
        four = slice(4 * t, 4 * t + 4)
        for pool, part in ((k2, slice(0, 32)), (v2, slice(32, 64))):
            pool[base + t, 0:128] = mine(four, part)
            pool[base + t, 128:256] = other(four, part)


def first_kernel(
    table, two, l1, r1, l2, r2, l3, r3, sw, se, sent, o_oth, kh, vh, k2, v2, s_ref
):
    w = table[AT_W]
    inner = (w == 1) | (w == 6)
    edge = (w == 0) | (w == 7)

    @pl.when(jnp.logical_not(edge))
    def _():
        for t in range(4):
            four = slice(4 * t, 4 * t + 4)
            kh[t] = whole(two, four, MAIN)
            vh[t] = whole(two, four, VALUE)
            vh[4 + t] = whole(r3, four)
            vh[8 + t] = whole(l3, four)
        for base, special, early, late in ((4, 6, r1, r2), (8, 1, l1, l2)):
            for condition, source in ((w == special, early), (w != special, late)):

                @pl.when(condition)
                def _(base=base, source=source):
                    for t in range(4):
                        kh[base + t] = whole(source, slice(4 * t, 4 * t + 4))

    @pl.when(inner)
    def _():
        @pl.loop(0, 4)
        def _(t):
            four = pl.ds(t * 4, 4)
            q = jnp.where(w == 1, whole(l2, four), whole(r2, four))
            o = attend(q, kh, vh, picks_of(table, AT_HEAD, t), s_ref)
            o_oth[four] = o.reshape(4, 64, HD)

    @pl.when(jnp.logical_not(inner | edge))
    def _():
        @pl.loop(0, 4)
        def _(t):
            four = pl.ds(t * 4, 4)
            o = attend(whole(two, four, REST), kh, vh, picks_of(table, AT_HEAD, 4 + t), s_ref)
            sent[four, 0:64] = o.reshape(4, 64, HD)

    @pl.when(edge)
    def _():
        fill_shared(
            0,
            lambda f, p: whole(two, f, slice(REST.start + p.start, REST.start + p.stop)),
            lambda f, p: whole(sw, 0, f, p),
            k2,
            v2,
        )

        @pl.when(w == 0)
        def _():
            fill_shared(4, lambda f, p: whole(r1, f, p), lambda f, p: whole(sw, 2, f, p), k2, v2)
            fill_shared(8, lambda f, p: whole(r2, f, p), lambda f, p: whole(se, f, p), k2, v2)

        @pl.when(w == 7)
        def _():
            fill_shared(4, lambda f, p: whole(l1, f, p), lambda f, p: whole(sw, 1, f, p), k2, v2)
            fill_shared(8, lambda f, p: whole(l2, f, p), lambda f, p: whole(se, f, p), k2, v2)

        @pl.loop(0, 4)
        def _(t):
            four = pl.ds(t * 4, 4)
            half = slice(0, 32)
            q = jnp.where(w == 7, whole(l3, four, half), whole(r3, four, half))
            o = attend(q, k2, v2, picks_of(table, AT_SHARED, t), s_ref)
            o_oth[four, 0:32] = o.reshape(4, 32, HD)

        @pl.loop(0, 4)
        def _(t):
            four = pl.ds(t * 4, 4)
            o = attend(whole(two, four, QUERY), k2, v2, picks_of(table, AT_SHARED, 4 + t), s_ref)
            sent[four, 64:96] = o.reshape(4, 32, HD)


def last_kernel(table, one, two, l1, r1, sw, kh, vh, sent_in, sent, k2, v2, s_ref):
    del sent_in
    w = table[AT_W]
    inner = (w == 1) | (w == 6)
    edge = (w == 0) | (w == 7)

    @pl.when(inner)
    def _():
        @pl.loop(0, 4)
        def _(t):
            four = pl.ds(t * 4, 4)
            o = attend(whole(two, four, REST), kh, vh, picks_of(table, AT_HEAD, 4 + t), s_ref)
            sent[four, 0:64] = o.reshape(4, 64, HD)

    @pl.when(jnp.logical_not(inner | edge))
    def _():
        fill_shared(0, lambda f, p: whole(one, f, p), lambda f, p: whole(sw, 0, f, p), k2, v2)
        fill_shared(4, lambda f, p: whole(r1, f, p), lambda f, p: whole(sw, 2, f, p), k2, v2)
        fill_shared(8, lambda f, p: whole(l1, f, p), lambda f, p: whole(sw, 1, f, p), k2, v2)

        @pl.loop(0, 4)
        def _(t):
            four = pl.ds(t * 4, 4)
            o = attend(whole(two, four, QUERY), k2, v2, picks_of(table, AT_SHARED, 4 + t), s_ref)
            sent[four, 64:96] = o.reshape(4, 32, HD)


def merge_kernel(table, o_left, o_right, sent_in, sent):
    del sent_in
    w = table[AT_W]

    @pl.when(w == 0)
    def _():
        sent[:, 0:64] = o_right[...]

    @pl.when(w == 7)
    def _():
        sent[:, 0:64] = o_left[...]

    @pl.when(w == 1)
    def _():
        sent[:, 64:96] = o_left[:, 0:32]

    @pl.when(w == 6)
    def _():
        sent[:, 64:96] = o_right[:, 0:32]


def unpack_kernel(in_ref, out_ref):
    for g in range(8):
        for h in range(2):
            out_ref[:, (3 * g + h) * HD : (3 * g + h + 1) * HD] = in_ref[2 * g + h, 0:64, :]
        last = slice((3 * g + 2) * HD, (3 * g + 3) * HD)
        out_ref[0:32, last] = in_ref[2 * g, 64:96, :]
        out_ref[32:64, last] = in_ref[2 * g + 1, 64:96, :]


def along_columns(block, distance):
    n = 2 * COLS
    return lax.ppermute(block, ("col", "half"), [(i, (i + 2 * distance) % n) for i in range(n)])


def swapped(block):
    return lax.ppermute(block, "core", [(0, 1), (1, 0)])


def exchanged(block):
    return lax.all_to_all(block, GROUP, split_axis=0, concat_axis=0, tiled=True)


POOL = (12, TOK_TILE, HD)
SCRATCH = [pltpu.VMEM(POOL, BF), pltpu.VMEM(POOL, BF), pltpu.VMEM((WIN, TOK_TILE, TOK_TILE), F32)]
SLOT = (16, 64, HD)


def kernel(body, name, outs, inputs, scratch=(), space=VMEM, limit=32, aliases={}):
    return pl.pallas_call(
        body,
        out_shape=tuple(
            jax.ShapeDtypeStruct(shape, BF if len(shape) > 1 else jnp.int32) for shape in outs
        ),
        in_specs=[SMEM if i.dtype == jnp.int32 else space for i in inputs],
        out_specs=tuple(VMEM if len(shape) > 1 else SMEM for shape in outs),
        scratch_shapes=list(scratch),
        input_output_aliases=aliases,
        compiler_params=pltpu.CompilerParams(vmem_limit_bytes=limit * MIB),
        name=name,
    )(*inputs)


def shards(queries, keys, values, order, nb):
    one, two, table = kernel(
        rotate_kernel,
        "rotate",
        (SLOT, (16, 224, HD), (256,)),
        (order, nb.T, queries, keys, values),
        (pltpu.VMEM((3,) + queries.shape, BF), pltpu.SemaphoreType.DMA((12,))),
        space=ANY,
        limit=60,
    )
    one = exchanged(one)
    l1, r1 = along_columns(one, 1), along_columns(one, -1)
    two = exchanged(two)
    main_left, main_right, value_left, value_right, swap = kernel(
        second_kernel, "second", (SLOT,) * 4 + ((3,) + SLOT,), (table, one, two, l1, r1)
    )
    l2, r2 = along_columns(main_right, 1), along_columns(main_left, -1)
    l3, r3 = along_columns(value_right, 1), along_columns(value_left, -1)
    sw = swapped(swap)
    se = swapped(jnp.where(table[AT_W] == 0, r2, l2))
    sent, o_oth, kh, vh = kernel(
        first_kernel,
        "attend_first",
        ((16, 96, HD), SLOT, POOL, POOL),
        (table, two, l1, r1, l2, r2, l3, r3, sw, se),
        SCRATCH,
    )
    o_left, o_right = along_columns(o_oth, 1), along_columns(o_oth, -1)
    (sent,) = kernel(
        last_kernel,
        "attend_last",
        ((16, 96, HD),),
        (table, one, two, l1, r1, sw, kh, vh, sent),
        SCRATCH,
        aliases={8: 0},
    )
    (sent,) = kernel(
        merge_kernel, "merge", ((16, 96, HD),), (table, o_left, o_right, sent), aliases={3: 0}
    )
    return kernel(unpack_kernel, "unpack", (queries.shape,), (exchanged(sent),))[0]


def solution(mesh):
    blk, uly, dp = (mesh.shape[name] for name in ("blk", "uly", "dp"))
    fine = Mesh(
        mesh.devices.reshape(blk // 2, 2, uly // 2, 2, dp), ("col", "half", "x", "core", "dp")
    )
    tokens = ("dp", "col", "half", "x", "core")
    placed = (P(tokens, None), P(tokens, None), P(tokens, None), P("dp"), P("dp", None))
    return jax.shard_map(
        shards, mesh=fine, in_specs=placed, out_specs=P(tokens, None), check_vma=False
    )
```

```python
import jax
import jax.numpy as jnp
import numpy as np
from jax import lax
from jax.experimental import pallas as pl
from jax.experimental.pallas import tpu as pltpu
from jax.sharding import Mesh
from jax.sharding import PartitionSpec as P

HD = 128
TOK_TILE = 256
WIN = 9
COLS = 8
GROUP = ("half", "x", "core")
VMEM = pl.BlockSpec(memory_space=pltpu.VMEM)
SMEM = pl.BlockSpec(memory_space=pltpu.SMEM)
ANY = pl.BlockSpec(memory_space=pl.ANY)
BF = jnp.bfloat16
F32 = jnp.float32
MIB = 1024 * 1024
ONE, MAIN, VALUE = slice(0, 64), slice(64, 128), slice(128, 192)
QUERY, REST = slice(192, 224), slice(224, 288)
AT_W, AT_HEAD, AT_SHARED = 0, 16, 96


def frequency_rows():
    pair = lax.broadcasted_iota(jnp.int32, (8, HD), 1) // 2
    nt = (HD - 4 * (HD // 6)) // 2
    ns = HD // 6
    rows = []
    for first, count in ((0, nt), (nt, ns), (nt + ns, ns)):
        within = (pair - first).astype(F32)
        freq = jnp.exp(within * float(-np.log(10000.0) / count))
        rows.append(jnp.where((pair >= first) & (pair < first + count), freq, 0.0)[0:1])
    return rows


def plan(order, nb, table):
    k = lax.axis_index("col")
    w = lax.rem(order[k * 4], COLS)
    table[AT_W] = w
    k_oth = lax.rem(jnp.where((w == 1) | (w == 7), k + 7, k + 1), COLS)
    near = jnp.where(w == 7, 7, 1)
    for u in range(8):
        slot = k_oth * 4 + u if u < 4 else k * 4 + u - 4
        for j in range(WIN):
            n = nb[j, slot]
            d = lax.rem(n // 4 - k + COLS, COLS)
            t = lax.rem(n, 4)
            table[AT_HEAD + WIN * u + j] = jnp.where(d == 0, 0, jnp.where(d == 1, 4, 8)) + t
            table[AT_SHARED + WIN * u + j] = jnp.where(d == 0, 0, jnp.where(d == near, 4, 8)) + t
    return w


def rotate_kernel(order, nb, q_hbm, k_hbm, v_hbm, two, table, held, sems):
    x = lax.axis_index("x")
    frame_in_tile = lax.rem(x, 2) * 2 + lax.axis_index("core")
    slot = lax.axis_index("col") * 4 + lax.axis_index("half") * 2 + x // 2
    rows = held.shape[1]
    width = 2 * 3 * HD
    copies = []
    for part in range(4):
        for which, ref in enumerate((k_hbm, q_hbm, v_hbm)):
            columns = pl.ds(part * width, width)
            copies.append(
                pltpu.make_async_copy(
                    ref.at[:, columns], held.at[which, :, columns], sems.at[3 * part + which]
                )
            )
    for copy in copies:
        copy.start()
    w = plan(order, nb, table)
    edge = (w == 0) | (w == 7)
    tile = order[slot]
    frame = (tile // 32 * 4 + frame_in_tile).astype(F32)
    row0 = (tile // 8 % 4 * 8).astype(F32)
    col0 = (tile % 8 * 8).astype(F32)
    token = lax.broadcasted_iota(jnp.int32, (rows, HD), 0)
    row = row0 + (token // 8).astype(F32)
    col = col0 + (token % 8).astype(F32)
    by_frame, by_row, by_col = frequency_rows()
    angle = frame * by_frame + row * by_row + col * by_col
    cosine = jnp.cos(angle)
    sine = jnp.sin(angle)
    even = lax.broadcasted_iota(jnp.int32, (rows, HD), 1) % 2 == 0
    from_next = jnp.where(even, -sine, 0.0)
    from_last = jnp.where(even, 0.0, sine)
    scale = HD ** (-0.5) * 1.4426950408889634

    def turned(x, c, n, l):
        x = x.astype(F32)
        return (x * c + pltpu.roll(x, HD - 1, 1) * n + pltpu.roll(x, 1, 1) * l).astype(BF)

    qc, qn, ql = cosine * scale, from_next * scale, from_last * scale
    for part in range(4):
        for which in range(3):
            copies[3 * part + which].wait()
        for g in range(2 * part, 2 * part + 2):
            for h in range(3):
                at = slice((3 * g + h) * HD, (3 * g + h + 1) * HD)
                key = turned(held[0, :, at], cosine, from_next, from_last)
                query = turned(held[1, :, at], qc, qn, ql)
                value = held[2, :, at]
                if h < 2:
                    to = 2 * g + h
                    two[to, VALUE, :] = value

                    @pl.when(edge)
                    def _(to=to, key=key, query=query):
                        two[to, ONE, :] = key
                        two[to, MAIN, :] = query

                    @pl.when(jnp.logical_not(edge))
                    def _(to=to, key=key, query=query):
                        two[to, MAIN, :] = key
                        two[to, REST, :] = query

                else:
                    for c in range(2):
                        to = 2 * g + c
                        part_of = slice(32 * c, 32 * c + 32)
                        two[to, QUERY, :] = query[part_of]

                        @pl.when(edge)
                        def _(to=to, part_of=part_of, key=key, value=value):
                            two[to, REST.start : REST.start + 32, :] = key[part_of]
                            two[to, REST.start + 32 : REST.stop, :] = value[part_of]

                        @pl.when(jnp.logical_not(edge))
                        def _(to=to, part_of=part_of, key=key, value=value):
                            two[to, 0:32, :] = key[part_of]
                            two[to, 32:64, :] = value[part_of]


def early_kernel(table, two, one, value_left, value_right):
    w = table[AT_W]
    one[...] = two[:, ONE]
    for out, special in ((value_left, 1), (value_right, 6)):

        @pl.when(w == special)
        def _(out=out):
            out[:, 0:32] = two[:, QUERY]
            out[:, 32:64] = two[:, QUERY]

        @pl.when(w != special)
        def _(out=out):
            out[...] = two[:, VALUE]


def late_kernel(table, two, l1, r1, main_left, main_right, swap):
    w = table[AT_W]
    for out, special, source in ((main_left, 1, r1), (main_right, 6, l1)):

        @pl.when(w == special)
        def _(out=out, source=source):
            out[...] = source[...]

        @pl.when(w != special)
        def _(out=out):
            out[...] = two[:, MAIN]

    @pl.when((w == 0) | (w == 7))
    def _():
        swap[0] = two[:, REST]

    @pl.when((w != 0) & (w != 7))
    def _():
        swap[0] = two[:, ONE]

    swap[1] = l1[...]
    swap[2] = r1[...]


def attend(q, kp, vp, picks, s_ref):
    rows = q.shape[0]
    top = None
    for j in range(WIN):
        s = lax.dot_general(q, kp[picks[j]], (((1,), (1,)), ((), ())), preferred_element_type=F32)
        s_ref[j, 0:rows, :] = s
        top = s if top is None else jnp.maximum(top, s)
    top = jnp.max(top, axis=1, keepdims=True)
    total = jnp.zeros((rows, TOK_TILE), F32)
    acc = jnp.zeros((rows, HD), F32)
    for j in range(WIN):
        p = jnp.exp2(s_ref[j, 0:rows, :] - top)
        total = total + p
        acc = acc + jnp.dot(p.astype(BF), vp[picks[j]], preferred_element_type=F32)
    return (acc / jnp.sum(total, axis=1, keepdims=True)).astype(BF)


def picks_of(table, at, u):
    return [table[at + u * WIN + j] for j in range(WIN)]


def whole(ref, *index):
    return ref[index].reshape(-1, HD)


def fill_shared(base, mine, other, k2, v2):
    for t in range(4):
        four = slice(4 * t, 4 * t + 4)
        for pool, part in ((k2, slice(0, 32)), (v2, slice(32, 64))):
            pool[base + t, 0:128] = mine(four, part)
            pool[base + t, 128:256] = other(four, part)


def value_kernel(two, l3, r3, vh):
    for t in range(4):
        four = slice(4 * t, 4 * t + 4)
        vh[t] = whole(two, four, VALUE)
        vh[4 + t] = whole(r3, four)
        vh[8 + t] = whole(l3, four)


def forwarded_kernel(table, l2, r2, vh, out):
    del vh
    w = table[AT_W]

    @pl.when(w == 0)
    def _():
        out[...] = r2[...]

    @pl.when(w == 7)
    def _():
        out[...] = l2[...]


def first_kernel(table, two, l1, r1, l2, r2, vh, sent, o_oth, kh, s_ref):
    w = table[AT_W]
    inner = (w == 1) | (w == 6)
    edge = (w == 0) | (w == 7)

    @pl.when(jnp.logical_not(edge))
    def _():
        for t in range(4):
            four = slice(4 * t, 4 * t + 4)
            kh[t] = whole(two, four, MAIN)
        for base, special, early, late in ((4, 6, r1, r2), (8, 1, l1, l2)):
            for condition, source in ((w == special, early), (w != special, late)):

                @pl.when(condition)
                def _(base=base, source=source):
                    for t in range(4):
                        kh[base + t] = whole(source, slice(4 * t, 4 * t + 4))

    @pl.when(inner)
    def _():
        @pl.loop(0, 4)
        def _(t):
            four = pl.ds(t * 4, 4)
            q = jnp.where(w == 1, whole(l2, four), whole(r2, four))
            o = attend(q, kh, vh, picks_of(table, AT_HEAD, t), s_ref)
            o_oth[four] = o.reshape(4, 64, HD)

    @pl.when(jnp.logical_not(inner | edge))
    def _():
        @pl.loop(0, 4)
        def _(t):
            four = pl.ds(t * 4, 4)
            o = attend(whole(two, four, REST), kh, vh, picks_of(table, AT_HEAD, 4 + t), s_ref)
            sent[four, 0:64] = o.reshape(4, 64, HD)


def edge_kernel(
    table, two, l1, r1, l2, r2, l3, r3, sw, se, sent_in, oth_in, sent, o_oth, k2, v2, s_ref
):
    del sent_in, oth_in
    w = table[AT_W]

    @pl.when((w == 0) | (w == 7))
    def _():
        fill_shared(
            0,
            lambda f, p: whole(two, f, slice(REST.start + p.start, REST.start + p.stop)),
            lambda f, p: whole(sw, 0, f, p),
            k2,
            v2,
        )

        @pl.when(w == 0)
        def _():
            fill_shared(4, lambda f, p: whole(r1, f, p), lambda f, p: whole(sw, 2, f, p), k2, v2)
            fill_shared(8, lambda f, p: whole(r2, f, p), lambda f, p: whole(se, f, p), k2, v2)

        @pl.when(w == 7)
        def _():
            fill_shared(4, lambda f, p: whole(l1, f, p), lambda f, p: whole(sw, 1, f, p), k2, v2)
            fill_shared(8, lambda f, p: whole(l2, f, p), lambda f, p: whole(se, f, p), k2, v2)

        @pl.loop(0, 4)
        def _(t):
            four = pl.ds(t * 4, 4)
            half = slice(0, 32)
            q = jnp.where(w == 7, whole(l3, four, half), whole(r3, four, half))
            o = attend(q, k2, v2, picks_of(table, AT_SHARED, t), s_ref)
            o_oth[four, 0:32] = o.reshape(4, 32, HD)

        @pl.loop(0, 4)
        def _(t):
            four = pl.ds(t * 4, 4)
            o = attend(whole(two, four, QUERY), k2, v2, picks_of(table, AT_SHARED, 4 + t), s_ref)
            sent[four, 64:96] = o.reshape(4, 32, HD)


def last_kernel(table, two, l1, r1, sw, kh, vh, sent_in, sent, k2, v2, s_ref):
    del sent_in
    w = table[AT_W]
    inner = (w == 1) | (w == 6)
    edge = (w == 0) | (w == 7)

    @pl.when(inner)
    def _():
        @pl.loop(0, 4)
        def _(t):
            four = pl.ds(t * 4, 4)
            o = attend(whole(two, four, REST), kh, vh, picks_of(table, AT_HEAD, 4 + t), s_ref)
            sent[four, 0:64] = o.reshape(4, 64, HD)

    @pl.when(jnp.logical_not(inner | edge))
    def _():
        fill_shared(0, lambda f, p: whole(two, f, p), lambda f, p: whole(sw, 0, f, p), k2, v2)
        fill_shared(4, lambda f, p: whole(r1, f, p), lambda f, p: whole(sw, 2, f, p), k2, v2)
        fill_shared(8, lambda f, p: whole(l1, f, p), lambda f, p: whole(sw, 1, f, p), k2, v2)

        @pl.loop(0, 4)
        def _(t):
            four = pl.ds(t * 4, 4)
            o = attend(whole(two, four, QUERY), k2, v2, picks_of(table, AT_SHARED, 4 + t), s_ref)
            sent[four, 64:96] = o.reshape(4, 32, HD)


def merge_kernel(table, o_left, o_right, sent_in, sent):
    del sent_in
    w = table[AT_W]

    @pl.when(w == 0)
    def _():
        sent[:, 0:64] = o_right[...]

    @pl.when(w == 7)
    def _():
        sent[:, 0:64] = o_left[...]

    @pl.when(w == 1)
    def _():
        sent[:, 64:96] = o_left[:, 0:32]

    @pl.when(w == 6)
    def _():
        sent[:, 64:96] = o_right[:, 0:32]


def unpack_kernel(in_ref, out_ref):
    for g in range(8):
        for h in range(2):
            out_ref[:, (3 * g + h) * HD : (3 * g + h + 1) * HD] = in_ref[2 * g + h, 0:64, :]
        last = slice((3 * g + 2) * HD, (3 * g + 3) * HD)
        out_ref[0:32, last] = in_ref[2 * g, 64:96, :]
        out_ref[32:64, last] = in_ref[2 * g + 1, 64:96, :]


def along_columns(block, distance):
    n = 2 * COLS
    return lax.ppermute(block, ("col", "half"), [(i, (i + 2 * distance) % n) for i in range(n)])


def swapped(block):
    return lax.ppermute(block, "core", [(0, 1), (1, 0)])


def exchanged(block):
    return lax.all_to_all(block, GROUP, split_axis=0, concat_axis=0, tiled=True)


POOL = (12, TOK_TILE, HD)
SCRATCH = [pltpu.VMEM(POOL, BF), pltpu.VMEM(POOL, BF), pltpu.VMEM((WIN, TOK_TILE, TOK_TILE), F32)]
SLOT = (16, 64, HD)
FLOPS = 20_000_000_000


def kernel(body, name, outs, inputs, scratch=(), space=VMEM, limit=32, aliases={}, flops=None):
    return pl.pallas_call(
        body,
        out_shape=tuple(
            jax.ShapeDtypeStruct(shape, BF if len(shape) > 1 else jnp.int32) for shape in outs
        ),
        in_specs=[SMEM if i.dtype == jnp.int32 else space for i in inputs],
        out_specs=tuple(VMEM if len(shape) > 1 else SMEM for shape in outs),
        scratch_shapes=list(scratch),
        input_output_aliases=aliases,
        compiler_params=pltpu.CompilerParams(vmem_limit_bytes=limit * MIB),
        cost_estimate=flops and pl.CostEstimate(flops=flops, bytes_accessed=0, transcendentals=0),
        name=name,
    )(*inputs)


def shards(queries, keys, values, order, nb):
    two, table = kernel(
        rotate_kernel,
        "rotate",
        ((16, 288, HD), (256,)),
        (order, nb.T, queries, keys, values),
        (pltpu.VMEM((3,) + queries.shape, BF), pltpu.SemaphoreType.DMA((12,))),
        space=ANY,
        limit=60,
    )
    two = exchanged(two)
    one, value_left, value_right = kernel(early_kernel, "early", (SLOT,) * 3, (table, two))
    l1, r1 = along_columns(one, 1), along_columns(one, -1)
    l3, r3 = along_columns(value_right, 1), along_columns(value_left, -1)
    main_left, main_right, swap = kernel(
        late_kernel, "late", (SLOT, SLOT, (3,) + SLOT), (table, two, l1, r1)
    )
    l2, r2 = along_columns(main_right, 1), along_columns(main_left, -1)
    sw = swapped(swap)
    (vh,) = kernel(value_kernel, "values", (POOL,), (two, l3, r3), flops=FLOPS)
    (se,) = kernel(forwarded_kernel, "forwarded", (SLOT,), (table, l2, r2, vh))
    se = swapped(se)
    sent, o_oth, kh = kernel(
        first_kernel,
        "attend_first",
        ((16, 96, HD), SLOT, POOL),
        (table, two, l1, r1, l2, r2, vh),
        SCRATCH[2:],
        flops=FLOPS,
    )
    sent, o_oth = kernel(
        edge_kernel,
        "attend_edge",
        ((16, 96, HD), SLOT),
        (table, two, l1, r1, l2, r2, l3, r3, sw, se, sent, o_oth),
        SCRATCH,
        aliases={10: 0, 11: 1},
    )
    o_left, o_right = along_columns(o_oth, 1), along_columns(o_oth, -1)
    (sent,) = kernel(
        last_kernel,
        "attend_last",
        ((16, 96, HD),),
        (table, two, l1, r1, sw, kh, vh, sent),
        SCRATCH,
        aliases={7: 0},
    )
    (sent,) = kernel(
        merge_kernel, "merge", ((16, 96, HD),), (table, o_left, o_right, sent), aliases={3: 0}
    )
    return kernel(unpack_kernel, "unpack", (queries.shape,), (exchanged(sent),))[0]


def solution(mesh):
    blk, uly, dp = (mesh.shape[name] for name in ("blk", "uly", "dp"))
    fine = Mesh(
        mesh.devices.reshape(blk // 2, 2, uly // 2, 2, dp), ("col", "half", "x", "core", "dp")
    )
    tokens = ("dp", "col", "half", "x", "core")
    placed = (P(tokens, None), P(tokens, None), P(tokens, None), P("dp"), P("dp", None))
    return jax.shard_map(
        shards, mesh=fine, in_specs=placed, out_specs=P(tokens, None), check_vma=False
    )
```

```python
import jax
import jax.numpy as jnp
import numpy as np
from jax import lax
from jax.experimental import pallas as pl
from jax.experimental.pallas import tpu as pltpu
from jax.sharding import Mesh
from jax.sharding import PartitionSpec as P

HD = 128
TOK_TILE = 256
WIN = 9
COLS = 8
GROUP = ("half", "x", "core")
VMEM = pl.BlockSpec(memory_space=pltpu.VMEM)
SMEM = pl.BlockSpec(memory_space=pltpu.SMEM)
ANY = pl.BlockSpec(memory_space=pl.ANY)
BF = jnp.bfloat16
F32 = jnp.float32
MIB = 1024 * 1024
ONE, MAIN, VALUE = slice(0, 64), slice(64, 128), slice(128, 192)
QUERY, REST = slice(192, 224), slice(224, 288)
VALUE_A, VALUE_B = slice(128, 160), slice(160, 192)
AT_W, AT_TILE, AT_HEAD, AT_SHARED = 0, 8, 16, 64
OTHER, THIS = 0, 1


def frequency_rows():
    pair = lax.broadcasted_iota(jnp.int32, (8, HD), 1) // 2
    nt = (HD - 4 * (HD // 6)) // 2
    ns = HD // 6
    rows = []
    for first, count in ((0, nt), (nt, ns), (nt + ns, ns)):
        within = (pair - first).astype(F32)
        freq = jnp.exp(within * float(-np.log(10000.0) / count))
        rows.append(jnp.where((pair >= first) & (pair < first + count), freq, 0.0)[0:1])
    return rows


def plan(order, nb, table):
    k = lax.axis_index("col")
    w = lax.rem(order[k * 4], COLS)
    table[AT_W] = w
    k_oth = lax.rem(jnp.where((w == 1) | (w == 7), k + 7, k + 1), COLS)
    near = jnp.where(w == 7, 7, 1)
    for column, base in ((OTHER, k_oth), (THIS, k)):
        low, high = 0, 2
        first = [0, 0]
        for t in range(4):
            upper = lax.rem(order[base * 4 + t] // 8, 4) < 2
            table[AT_TILE + 4 * column + jnp.where(upper, low, high)] = t
            first = [jnp.where(upper, t, first[0]), jnp.where(upper, first[1], t)]
            low, high = low + upper.astype(jnp.int32), high + 1 - upper.astype(jnp.int32)
        for p in range(2):
            for j in range(WIN):
                n = nb[j, base * 4 + first[p]]
                d = lax.rem(n // 4 - k + COLS, COLS)
                t = lax.rem(n, 4)
                at = WIN * (2 * column + p) + j
                table[AT_HEAD + at] = jnp.where(d == 0, 0, jnp.where(d == 1, 4, 8)) + t
                table[AT_SHARED + at] = jnp.where(d == 0, 0, jnp.where(d == near, 4, 8)) + t
    return w


def rotate_kernel(order, nb, q_hbm, k_hbm, v_hbm, out_hbm, table, held, packed, sems, out_sems):
    x = lax.axis_index("x")
    frame_in_tile = lax.rem(x, 2) * 2 + lax.axis_index("core")
    slot = lax.axis_index("col") * 4 + lax.axis_index("half") * 2 + x // 2
    rows = held.shape[1]
    width = 2 * 3 * HD
    copies = []
    for part in range(4):
        for which, ref in enumerate((k_hbm, q_hbm, v_hbm)):
            columns = pl.ds(part * width, width)
            copies.append(
                pltpu.make_async_copy(
                    ref.at[:, columns], held.at[which, :, columns], sems.at[3 * part + which]
                )
            )
    for copy in copies:
        copy.start()
    w = plan(order, nb, table)
    edge = (w == 0) | (w == 7)
    tile = order[slot]
    frame = (tile // 32 * 4 + frame_in_tile).astype(F32)
    row0 = (tile // 8 % 4 * 8).astype(F32)
    col0 = (tile % 8 * 8).astype(F32)
    token = lax.broadcasted_iota(jnp.int32, (rows, HD), 0)
    row = row0 + (token // 8).astype(F32)
    col = col0 + (token % 8).astype(F32)
    by_frame, by_row, by_col = frequency_rows()
    angle = frame * by_frame + row * by_row + col * by_col
    cosine = jnp.cos(angle)
    sine = jnp.sin(angle)
    even = lax.broadcasted_iota(jnp.int32, (rows, HD), 1) % 2 == 0
    from_next = jnp.where(even, -sine, 0.0)
    from_last = jnp.where(even, 0.0, sine)
    scale = HD ** (-0.5) * 1.4426950408889634

    def turned(x, c, n, l):
        x = x.astype(F32)
        return (x * c + pltpu.roll(x, HD - 1, 1) * n + pltpu.roll(x, 1, 1) * l).astype(BF)

    qc, qn, ql = cosine * scale, from_next * scale, from_last * scale
    outs = []
    for part in range(4):
        for which in range(3):
            copies[3 * part + which].wait()
        for g in range(2 * part, 2 * part + 2):
            at = [slice((3 * g + h) * HD, (3 * g + h + 1) * HD) for h in range(3)]
            key = [turned(held[0, :, a], cosine, from_next, from_last) for a in at]
            query = [turned(held[1, :, a], qc, qn, ql) for a in at]
            value = [held[2, :, a] for a in at]
            for c in range(2):
                to = 2 * g + c
                mine = slice(32 * c, 32 * c + 32)
                shared = jnp.concatenate([key[2][mine], value[2][mine]])
                packed[to, ONE, :] = jnp.where(edge, key[c], shared)
                packed[to, MAIN, :] = jnp.where(edge, query[c], key[c])
                packed[to, VALUE, :] = value[c]
                packed[to, QUERY, :] = query[2][mine]
                packed[to, REST, :] = jnp.where(edge, shared, query[c])
        four = pl.ds(4 * part, 4)
        outs.append(
            pltpu.make_async_copy(packed.at[four], out_hbm.at[four], out_sems.at[part])
        )
        outs[-1].start()
    for out in outs:
        out.wait()


def early_kernel(table, two, one, value_left, value_right):
    w = table[AT_W]
    one[...] = two[:, ONE]
    for out, special in ((value_left, 1), (value_right, 6)):

        @pl.when(w == special)
        def _(out=out):
            out[...] = two[:, QUERY]

        @pl.when(w != special)
        def _(out=out):
            out[...] = two[:, VALUE_A]


def late_kernel(table, two, l1, r1, main_left, main_right, swap):
    w = table[AT_W]
    for out, special, source in ((main_left, 1, r1), (main_right, 6, l1)):
        out[:, 64:96] = two[:, VALUE_B]

        @pl.when(w == special)
        def _(out=out, source=source):
            out[:, 0:64] = source[...]

        @pl.when(w != special)
        def _(out=out):
            out[:, 0:64] = two[:, MAIN]

    @pl.when((w == 0) | (w == 7))
    def _():
        swap[0] = two[:, REST]

    @pl.when((w != 0) & (w != 7))
    def _():
        swap[0] = two[:, ONE]

    swap[1] = l1[...]
    swap[2] = r1[...]


def attend(q, kp, vp, picks):
    top = weights = acc = None
    for pick in picks:
        s = lax.dot_general(q, kp[pick], (((1,), (1,)), ((), ())), preferred_element_type=F32)
        high = jnp.max(s, axis=1, keepdims=True)
        new = high if top is None else jnp.maximum(top, high)
        p = jnp.exp2(s - new)
        part = jnp.dot(p.astype(BF), whole(vp, pick), preferred_element_type=F32)
        if top is None:
            weights, acc = p, part
        else:
            shrink = jnp.exp2(top - new)
            weights, acc = weights * shrink + p, acc * shrink + part
        top = new
    return (acc / jnp.sum(weights, axis=1, keepdims=True)).astype(BF)


def whole(ref, *index):
    return ref[index].reshape(-1, HD)


def attend_column(table, column, at, query, kp, vp, store):
    @pl.loop(0, 2)
    def _(p):
        fours = [pl.ds(table[AT_TILE + 4 * column + 2 * p + i] * 4, 4) for i in range(2)]
        picks = [table[at + (2 * column + p) * WIN + j] for j in range(WIN)]
        o = attend(jnp.concatenate([query(four) for four in fours]), kp, vp, picks)
        half = o.shape[0] // 2
        for i, four in enumerate(fours):
            store(four, o[i * half : (i + 1) * half].reshape(4, -1, HD))


def fill_shared(base, mine, other, k2, v2):
    for t in range(4):
        four = slice(4 * t, 4 * t + 4)
        for pool, part in ((k2, slice(0, 32)), (v2, slice(32, 64))):
            pool[base + t, 0:128] = mine(four, part)
            pool[base + t, 128:256] = other(four, part)


def value_kernel(two, l3, r3, vh):
    for t in range(4):
        four = slice(4 * t, 4 * t + 4)
        vh[t] = two[four, VALUE]
        vh[4 + t, :, 0:32] = r3[four]
        vh[8 + t, :, 0:32] = l3[four]


def forwarded_kernel(table, l2, r2, vh, out):
    del vh
    w = table[AT_W]

    @pl.when(w == 0)
    def _():
        out[...] = r2[:, 0:64]

    @pl.when(w == 7)
    def _():
        out[...] = l2[:, 0:64]


def first_kernel(table, two, l1, r1, l2, r2, vh_in, sent, o_oth, kh, vh):
    del vh_in
    w = table[AT_W]
    inner = (w == 1) | (w == 6)
    edge = (w == 0) | (w == 7)

    @pl.when(jnp.logical_not(edge))
    def _():
        for t in range(4):
            four = slice(4 * t, 4 * t + 4)
            kh[t] = whole(two, four, MAIN)
            vh[4 + t, :, 32:64] = r2[four, 64:96]
            vh[8 + t, :, 32:64] = l2[four, 64:96]
        for base, special, early, late in ((4, 6, r1, r2), (8, 1, l1, l2)):

            @pl.when(w == special)
            def _(base=base, early=early):
                for t in range(4):
                    kh[base + t] = whole(early, slice(4 * t, 4 * t + 4))

            @pl.when(w != special)
            def _(base=base, late=late):
                for t in range(4):
                    kh[base + t] = whole(late, slice(4 * t, 4 * t + 4), slice(0, 64))

    def to_other(four, o):
        o_oth[four] = o

    def to_sent(four, o):
        sent[four, 0:64] = o

    for special, source in ((1, l2), (6, r2)):

        @pl.when(w == special)
        def _(source=source):
            query = lambda four: whole(source, four, slice(0, 64))
            attend_column(table, OTHER, AT_HEAD, query, kh, vh, to_other)

    @pl.when(jnp.logical_not(inner | edge))
    def _():
        query = lambda four: whole(two, four, REST)
        attend_column(table, THIS, AT_HEAD, query, kh, vh, to_sent)


def edge_kernel(table, two, l1, r1, l2, r2, l3, r3, sw, se, oth_in, o_oth, k2, v2):
    del oth_in
    w = table[AT_W]

    def to_other(four, o):
        o_oth[four, 0:32] = o

    for special, near, far, asked, swapped_near in ((0, r1, r2, r3, 2), (7, l1, l2, l3, 1)):

        @pl.when(w == special)
        def _(near=near, far=far, asked=asked, swapped_near=swapped_near):
            own = lambda f, p: whole(two, f, slice(REST.start + p.start, REST.start + p.stop))
            fill_shared(0, own, lambda f, p: whole(sw, 0, f, p), k2, v2)
            fill_shared(
                4, lambda f, p: whole(near, f, p), lambda f, p: whole(sw, swapped_near, f, p), k2, v2
            )
            fill_shared(8, lambda f, p: whole(far, f, p), lambda f, p: whole(se, f, p), k2, v2)
            query = lambda four: whole(asked, four)
            attend_column(table, OTHER, AT_SHARED, query, k2, v2, to_other)


def last_kernel(table, two, l1, r1, sw, kh, vh, k2, v2, sent_in, sent, k3, v3):
    del sent_in
    w = table[AT_W]
    inner = (w == 1) | (w == 6)
    edge = (w == 0) | (w == 7)

    def to_head(four, o):
        sent[four, 0:64] = o

    def to_shared(four, o):
        sent[four, 64:96] = o

    shared_query = lambda four: whole(two, four, QUERY)

    @pl.when(inner)
    def _():
        query = lambda four: whole(two, four, REST)
        attend_column(table, THIS, AT_HEAD, query, kh, vh, to_head)

    @pl.when(edge)
    def _():
        attend_column(table, THIS, AT_SHARED, shared_query, k2, v2, to_shared)

    @pl.when(jnp.logical_not(inner | edge))
    def _():
        fill_shared(0, lambda f, p: whole(two, f, p), lambda f, p: whole(sw, 0, f, p), k3, v3)
        fill_shared(4, lambda f, p: whole(r1, f, p), lambda f, p: whole(sw, 2, f, p), k3, v3)
        fill_shared(8, lambda f, p: whole(l1, f, p), lambda f, p: whole(sw, 1, f, p), k3, v3)
        attend_column(table, THIS, AT_SHARED, shared_query, k3, v3, to_shared)


def merge_kernel(table, o_left, o_right, sent_in, sent):
    del sent_in
    w = table[AT_W]

    @pl.when(w == 0)
    def _():
        sent[:, 0:64] = o_right[...]

    @pl.when(w == 7)
    def _():
        sent[:, 0:64] = o_left[...]

    @pl.when(w == 1)
    def _():
        sent[:, 64:96] = o_left[:, 0:32]

    @pl.when(w == 6)
    def _():
        sent[:, 64:96] = o_right[:, 0:32]


def unpack_kernel(in_ref, out_ref):
    for g in range(8):
        for h in range(2):
            out_ref[:, (3 * g + h) * HD : (3 * g + h + 1) * HD] = in_ref[2 * g + h, 0:64, :]
        last = slice((3 * g + 2) * HD, (3 * g + 3) * HD)
        out_ref[0:32, last] = in_ref[2 * g, 64:96, :]
        out_ref[32:64, last] = in_ref[2 * g + 1, 64:96, :]


def along_columns(block, distance):
    n = 2 * COLS
    return lax.ppermute(block, ("col", "half"), [(i, (i + 2 * distance) % n) for i in range(n)])


def swapped(block):
    return lax.ppermute(block, "core", [(0, 1), (1, 0)])


def exchanged(block):
    return lax.all_to_all(block, GROUP, split_axis=0, concat_axis=0, tiled=True)


SLOT = (16, 64, HD)
SENT = (16, 96, HD)
POOL = (12, TOK_TILE, HD)
PARTS = (12, 4, 64, HD)
FLOPS = 20_000_000_000


def kernel(body, name, outs, inputs, scratch=(), limit=32, aliases={}, flops=None, space=VMEM):
    return pl.pallas_call(
        body,
        out_shape=tuple(
            jax.ShapeDtypeStruct(shape, BF if len(shape) > 1 else jnp.int32) for shape in outs
        ),
        in_specs=[SMEM if i.dtype == jnp.int32 else space for i in inputs],
        out_specs=tuple(space if len(shape) > 1 else SMEM for shape in outs),
        scratch_shapes=list(scratch),
        input_output_aliases=aliases,
        compiler_params=pltpu.CompilerParams(vmem_limit_bytes=limit * MIB),
        cost_estimate=flops and pl.CostEstimate(flops=flops, bytes_accessed=0, transcendentals=0),
        name=name,
    )(*inputs)


def shards(queries, keys, values, order, nb):
    two, table = kernel(
        rotate_kernel,
        "rotate",
        ((16, 288, HD), (128,)),
        (order, nb.T, queries, keys, values),
        (
            pltpu.VMEM((3,) + queries.shape, BF),
            pltpu.VMEM((16, 288, HD), BF),
            pltpu.SemaphoreType.DMA((12,)),
            pltpu.SemaphoreType.DMA((4,)),
        ),
        limit=60,
        space=ANY,
    )
    two = exchanged(two)
    one, value_left, value_right = kernel(
        early_kernel, "early", (SLOT, (16, 32, HD), (16, 32, HD)), (table, two)
    )
    l1, r1 = along_columns(one, 1), along_columns(one, -1)
    l3, r3 = along_columns(value_right, 1), along_columns(value_left, -1)
    main_left, main_right, swap = kernel(
        late_kernel, "late", (SENT, SENT, (3,) + SLOT), (table, two, l1, r1)
    )
    l2, r2 = along_columns(main_right, 1), along_columns(main_left, -1)
    sw = swapped(swap)
    (vh,) = kernel(value_kernel, "values", (PARTS,), (two, l3, r3), flops=FLOPS)
    (se,) = kernel(forwarded_kernel, "forwarded", (SLOT,), (table, l2, r2, vh))
    se = swapped(se)
    sent, o_oth, kh, vh = kernel(
        first_kernel,
        "attend_first",
        (SENT, SLOT, POOL, PARTS),
        (table, two, l1, r1, l2, r2, vh),
        aliases={6: 3},
        flops=FLOPS,
    )
    o_oth, k2, v2 = kernel(
        edge_kernel,
        "attend_edge",
        (SLOT, POOL, POOL),
        (table, two, l1, r1, l2, r2, l3, r3, sw, se, o_oth),
        aliases={10: 0},
    )
    o_left, o_right = along_columns(o_oth, 1), along_columns(o_oth, -1)
    (sent,) = kernel(
        last_kernel,
        "attend_last",
        (SENT,),
        (table, two, l1, r1, sw, kh, vh, k2, v2, sent),
        (pltpu.VMEM(POOL, BF), pltpu.VMEM(POOL, BF)),
        aliases={9: 0},
    )
    (sent,) = kernel(merge_kernel, "merge", (SENT,), (table, o_left, o_right, sent), aliases={3: 0})
    return kernel(unpack_kernel, "unpack", (queries.shape,), (exchanged(sent),))[0]


def solution(mesh):
    blk, uly, dp = (mesh.shape[name] for name in ("blk", "uly", "dp"))
    fine = Mesh(
        mesh.devices.reshape(blk // 2, 2, uly // 2, 2, dp), ("col", "half", "x", "core", "dp")
    )
    tokens = ("dp", "col", "half", "x", "core")
    placed = (P(tokens, None), P(tokens, None), P(tokens, None), P("dp"), P("dp", None))
    return jax.shard_map(
        shards, mesh=fine, in_specs=placed, out_specs=P(tokens, None), check_vma=False
    )
```

```python
import jax
import jax.numpy as jnp
import numpy as np
from jax import lax
from jax.experimental import pallas as pl
from jax.experimental.pallas import tpu as pltpu
from jax.sharding import Mesh
from jax.sharding import PartitionSpec as P

HD = 128
TOK_TILE = 256
WIN = 9
COLS = 8
GROUP = ("half", "x", "core")
VMEM = pl.BlockSpec(memory_space=pltpu.VMEM)
SMEM = pl.BlockSpec(memory_space=pltpu.SMEM)
ANY = pl.BlockSpec(memory_space=pl.ANY)
BF = jnp.bfloat16
F32 = jnp.float32
MIB = 1024 * 1024
ONE, MAIN, VALUE = slice(0, 64), slice(64, 128), slice(128, 192)
QUERY, REST = slice(192, 224), slice(224, 288)
AT_W, AT_TILE, AT_HEAD, AT_SHARED = 0, 8, 16, 64
OTHER, THIS = 0, 1


def frequency_rows():
    pair = lax.broadcasted_iota(jnp.int32, (8, HD), 1) // 2
    nt = (HD - 4 * (HD // 6)) // 2
    ns = HD // 6
    rows = []
    for first, count in ((0, nt), (nt, ns), (nt + ns, ns)):
        within = (pair - first).astype(F32)
        freq = jnp.exp(within * float(-np.log(10000.0) / count))
        rows.append(jnp.where((pair >= first) & (pair < first + count), freq, 0.0)[0:1])
    return rows


def turns(tile, frame_in_tile, scale):
    frame = (tile // 32 * 4 + frame_in_tile).astype(F32)
    row0 = (tile // 8 % 4 * 8).astype(F32)
    col0 = (tile % 8 * 8).astype(F32)
    token = lax.broadcasted_iota(jnp.int32, (64, HD), 0)
    row = row0 + (token // 8).astype(F32)
    col = col0 + (token % 8).astype(F32)
    by_frame, by_row, by_col = frequency_rows()
    angle = frame * by_frame + row * by_row + col * by_col
    cosine = jnp.cos(angle) * scale
    sine = jnp.sin(angle) * scale
    even = lax.broadcasted_iota(jnp.int32, (64, HD), 1) % 2 == 0
    return cosine, jnp.where(even, -sine, 0.0), jnp.where(even, 0.0, sine)


def turned(x, factors):
    here, after, before = factors
    x = x.astype(F32)
    return (x * here + pltpu.roll(x, HD - 1, 1) * after + pltpu.roll(x, 1, 1) * before).astype(BF)


def plan(order, nb, table):
    k = lax.axis_index("col")
    w = lax.rem(order[k * 4], COLS)
    table[AT_W] = w
    k_oth = lax.rem(jnp.where((w == 1) | (w == 7), k + 7, k + 1), COLS)
    near = jnp.where(w == 7, 7, 1)
    for column, base in ((OTHER, k_oth), (THIS, k)):
        low, high = 0, 2
        first = [0, 0]
        for t in range(4):
            upper = lax.rem(order[base * 4 + t] // 8, 4) < 2
            table[AT_TILE + 4 * column + jnp.where(upper, low, high)] = t
            first = [jnp.where(upper, t, first[0]), jnp.where(upper, first[1], t)]
            low, high = low + upper.astype(jnp.int32), high + 1 - upper.astype(jnp.int32)
        for p in range(2):
            for j in range(WIN):
                n = nb[j, base * 4 + first[p]]
                d = lax.rem(n // 4 - k + COLS, COLS)
                t = lax.rem(n, 4)
                at = WIN * (2 * column + p) + j
                table[AT_HEAD + at] = jnp.where(d == 0, 0, jnp.where(d == 1, 4, 8)) + t
                table[AT_SHARED + at] = jnp.where(d == 0, 0, jnp.where(d == near, 4, 8)) + t
    return w


def rotate_kernel(order, nb, q_hbm, k_hbm, v_hbm, out_hbm, table, held, packed, sems, out_sems):
    x = lax.axis_index("x")
    frame_in_tile = lax.rem(x, 2) * 2 + lax.axis_index("core")
    slot = lax.axis_index("col") * 4 + lax.axis_index("half") * 2 + x // 2
    width = 2 * 3 * HD
    copies = []
    for part in range(4):
        for which, ref in enumerate((k_hbm, q_hbm, v_hbm)):
            columns = pl.ds(part * width, width)
            copies.append(
                pltpu.make_async_copy(
                    ref.at[:, columns], held.at[which, :, columns], sems.at[3 * part + which]
                )
            )
    for copy in copies:
        copy.start()
    w = plan(order, nb, table)
    edge = (w == 0) | (w == 7)
    factors = turns(order[slot], frame_in_tile, 1.0)
    outs = []
    for part in range(4):
        for which in range(3):
            copies[3 * part + which].wait()
        for g in range(2 * part, 2 * part + 2):
            at = [slice((3 * g + h) * HD, (3 * g + h + 1) * HD) for h in range(3)]
            key = [turned(held[0, :, a], factors) for a in at]
            query = [held[1, :, a] for a in at]
            value = [held[2, :, a] for a in at]
            for c in range(2):
                to = 2 * g + c
                mine = slice(32 * c, 32 * c + 32)
                shared = jnp.concatenate([key[2][mine], value[2][mine]])
                packed[to, ONE, :] = jnp.where(edge, key[c], shared)
                packed[to, MAIN, :] = jnp.where(edge, query[c], key[c])
                packed[to, VALUE, :] = value[c]
                packed[to, QUERY, :] = query[2][mine]
                packed[to, REST, :] = jnp.where(edge, shared, query[c])
        four = pl.ds(4 * part, 4)
        outs.append(
            pltpu.make_async_copy(packed.at[four], out_hbm.at[four], out_sems.at[part])
        )
        outs[-1].start()
    for out in outs:
        out.wait()


def early_kernel(table, two, one, own):
    w = table[AT_W]
    one[...] = two[:, ONE]

    @pl.when((w == 0) | (w == 7))
    def _():
        own[...] = two[:, REST]

    @pl.when((w != 0) & (w != 7))
    def _():
        own[...] = two[:, ONE]


def middle_kernel(table, order, two, q_head, q_shared, value_left, value_right):
    w = table[AT_W]
    edge = (w == 0) | (w == 7)
    col, core = lax.axis_index("col"), lax.axis_index("core")

    @pl.loop(0, 16)
    def _(source):
        scale = HD ** (-0.5) * 1.4426950408889634
        factors = turns(order[col * 4 + source // 4], lax.rem(source, 4), scale)
        held = two[source]
        q_head[source] = turned(jnp.where(edge, held[MAIN], held[REST]), factors)
        mine = [jnp.where(core == 0, f[0:32], f[32:64]) for f in factors]
        q_shared[source] = turned(held[QUERY], mine)

    for out, special in ((value_left, 1), (value_right, 6)):

        @pl.when(w == special)
        def _(out=out):
            out[:, 0:32] = q_shared[...]
            out[:, 32:64] = q_shared[...]

        @pl.when(w != special)
        def _(out=out):
            out[...] = two[:, VALUE]


def late_kernel(table, two, q_head, l1, r1, main_left, main_right, swap):
    w = table[AT_W]
    edge = (w == 0) | (w == 7)
    for out, special, source in ((main_left, 1, r1), (main_right, 6, l1)):

        @pl.when(w == special)
        def _(out=out, source=source):
            out[...] = source[...]

        @pl.when(edge)
        def _(out=out):
            out[...] = q_head[...]

        @pl.when((w != special) & jnp.logical_not(edge))
        def _(out=out):
            out[...] = two[:, MAIN]

    swap[0] = l1[...]
    swap[1] = r1[...]


def attend(q, kp, vp, picks):
    top = weights = acc = None
    for pick in picks:
        s = lax.dot_general(q, kp[pick], (((1,), (1,)), ((), ())), preferred_element_type=F32)
        high = jnp.max(s, axis=1, keepdims=True)
        new = high if top is None else jnp.maximum(top, high)
        p = jnp.exp2(s - new)
        part = jnp.dot(p.astype(BF), whole(vp, pick), preferred_element_type=F32)
        if top is None:
            weights, acc = p, part
        else:
            shrink = jnp.exp2(top - new)
            weights, acc = weights * shrink + p, acc * shrink + part
        top = new
    return (acc / jnp.sum(weights, axis=1, keepdims=True)).astype(BF)


def whole(ref, *index):
    return ref[index].reshape(-1, HD)


def attend_column(table, column, at, query, kp, vp, store):
    @pl.loop(0, 2)
    def _(p):
        fours = [pl.ds(table[AT_TILE + 4 * column + 2 * p + i] * 4, 4) for i in range(2)]
        picks = [table[at + (2 * column + p) * WIN + j] for j in range(WIN)]
        o = attend(jnp.concatenate([query(four) for four in fours]), kp, vp, picks)
        half = o.shape[0] // 2
        for i, four in enumerate(fours):
            store(four, o[i * half : (i + 1) * half].reshape(4, -1, HD))


def fill_shared(base, mine, other, k2, v2):
    for t in range(4):
        four = slice(4 * t, 4 * t + 4)
        for pool, part in ((k2, slice(0, 32)), (v2, slice(32, 64))):
            pool[base + t, 0:128] = mine(four, part)
            pool[base + t, 128:256] = other(four, part)


def value_kernel(two, l3, r3, vh):
    for t in range(4):
        four = slice(4 * t, 4 * t + 4)
        vh[t] = two[four, VALUE]
        vh[4 + t] = r3[four]
        vh[8 + t] = l3[four]


def forwarded_kernel(table, l2, r2, vh, out):
    del vh
    w = table[AT_W]

    @pl.when(w == 0)
    def _():
        out[...] = r2[...]

    @pl.when(w == 7)
    def _():
        out[...] = l2[...]


def first_kernel(table, two, q_head, l1, r1, l2, r2, vh, sent, o_oth, kh):
    w = table[AT_W]
    inner = (w == 1) | (w == 6)
    edge = (w == 0) | (w == 7)

    @pl.when(jnp.logical_not(edge))
    def _():
        for t in range(4):
            four = slice(4 * t, 4 * t + 4)
            kh[t] = whole(two, four, MAIN)
        for base, special, early, late in ((4, 6, r1, r2), (8, 1, l1, l2)):

            @pl.when(w == special)
            def _(base=base, early=early):
                for t in range(4):
                    kh[base + t] = whole(early, slice(4 * t, 4 * t + 4))

            @pl.when(w != special)
            def _(base=base, late=late):
                for t in range(4):
                    kh[base + t] = whole(late, slice(4 * t, 4 * t + 4))

    def to_other(four, o):
        o_oth[four] = o

    def to_sent(four, o):
        sent[four, 0:64] = o

    for special, source in ((1, l2), (6, r2)):

        @pl.when(w == special)
        def _(source=source):
            query = lambda four: whole(source, four)
            attend_column(table, OTHER, AT_HEAD, query, kh, vh, to_other)

    @pl.when(jnp.logical_not(inner | edge))
    def _():
        query = lambda four: whole(q_head, four)
        attend_column(table, THIS, AT_HEAD, query, kh, vh, to_sent)


def edge_kernel(table, two, l1, r1, l2, r2, l3, r3, s0, sw, se, oth_in, o_oth, k2, v2):
    del oth_in
    w = table[AT_W]

    def to_other(four, o):
        o_oth[four, 0:32] = o

    for special, near, far, asked, swapped_near in ((0, r1, r2, r3, 1), (7, l1, l2, l3, 0)):

        @pl.when(w == special)
        def _(near=near, far=far, asked=asked, swapped_near=swapped_near):
            own = lambda f, p: whole(two, f, slice(REST.start + p.start, REST.start + p.stop))
            fill_shared(0, own, lambda f, p: whole(s0, f, p), k2, v2)
            fill_shared(
                4, lambda f, p: whole(near, f, p), lambda f, p: whole(sw, swapped_near, f, p), k2, v2
            )
            fill_shared(8, lambda f, p: whole(far, f, p), lambda f, p: whole(se, f, p), k2, v2)
            query = lambda four: whole(asked, four, slice(0, 32))
            attend_column(table, OTHER, AT_SHARED, query, k2, v2, to_other)


def last_kernel(table, two, q_head, q_shared, l1, r1, s0, sw, kh, vh, k2, v2, sent_in, sent, k3, v3):
    del sent_in
    w = table[AT_W]
    inner = (w == 1) | (w == 6)
    edge = (w == 0) | (w == 7)

    def to_head(four, o):
        sent[four, 0:64] = o

    def to_shared(four, o):
        sent[four, 64:96] = o

    shared_query = lambda four: whole(q_shared, four)

    @pl.when(inner)
    def _():
        query = lambda four: whole(q_head, four)
        attend_column(table, THIS, AT_HEAD, query, kh, vh, to_head)

    @pl.when(edge)
    def _():
        attend_column(table, THIS, AT_SHARED, shared_query, k2, v2, to_shared)

    @pl.when(jnp.logical_not(inner | edge))
    def _():
        fill_shared(0, lambda f, p: whole(two, f, p), lambda f, p: whole(s0, f, p), k3, v3)
        fill_shared(4, lambda f, p: whole(r1, f, p), lambda f, p: whole(sw, 1, f, p), k3, v3)
        fill_shared(8, lambda f, p: whole(l1, f, p), lambda f, p: whole(sw, 0, f, p), k3, v3)
        attend_column(table, THIS, AT_SHARED, shared_query, k3, v3, to_shared)


def merge_kernel(table, o_left, o_right, sent_in, sent):
    del sent_in
    w = table[AT_W]

    @pl.when(w == 0)
    def _():
        sent[:, 0:64] = o_right[...]

    @pl.when(w == 7)
    def _():
        sent[:, 0:64] = o_left[...]

    @pl.when(w == 1)
    def _():
        sent[:, 64:96] = o_left[:, 0:32]

    @pl.when(w == 6)
    def _():
        sent[:, 64:96] = o_right[:, 0:32]


def unpack_kernel(in_ref, out_ref):
    for g in range(8):
        for h in range(2):
            out_ref[:, (3 * g + h) * HD : (3 * g + h + 1) * HD] = in_ref[2 * g + h, 0:64, :]
        last = slice((3 * g + 2) * HD, (3 * g + 3) * HD)
        out_ref[0:32, last] = in_ref[2 * g, 64:96, :]
        out_ref[32:64, last] = in_ref[2 * g + 1, 64:96, :]


def along_columns(block, distance):
    n = 2 * COLS
    return lax.ppermute(block, ("col", "half"), [(i, (i + 2 * distance) % n) for i in range(n)])


def swapped(block):
    return lax.ppermute(block, "core", [(0, 1), (1, 0)])


def exchanged(block):
    return lax.all_to_all(block, GROUP, split_axis=0, concat_axis=0, tiled=True)


SLOT = (16, 64, HD)
SENT = (16, 96, HD)
POOL = (12, TOK_TILE, HD)
PARTS = (12, 4, 64, HD)
FLOPS = 20_000_000_000


def kernel(body, name, outs, inputs, scratch=(), limit=32, aliases={}, flops=None, space=VMEM):
    return pl.pallas_call(
        body,
        out_shape=tuple(
            jax.ShapeDtypeStruct(shape, BF if len(shape) > 1 else jnp.int32) for shape in outs
        ),
        in_specs=[SMEM if i.dtype == jnp.int32 else space for i in inputs],
        out_specs=tuple(space if len(shape) > 1 else SMEM for shape in outs),
        scratch_shapes=list(scratch),
        input_output_aliases=aliases,
        compiler_params=pltpu.CompilerParams(vmem_limit_bytes=limit * MIB),
        cost_estimate=flops and pl.CostEstimate(flops=flops, bytes_accessed=0, transcendentals=0),
        name=name,
    )(*inputs)


def shards(queries, keys, values, order, nb):
    two, table = kernel(
        rotate_kernel,
        "rotate",
        ((16, 288, HD), (128,)),
        (order, nb.T, queries, keys, values),
        (
            pltpu.VMEM((3,) + queries.shape, BF),
            pltpu.VMEM((16, 288, HD), BF),
            pltpu.SemaphoreType.DMA((12,)),
            pltpu.SemaphoreType.DMA((4,)),
        ),
        limit=60,
        space=ANY,
    )
    two = exchanged(two)
    one, own = kernel(early_kernel, "early", (SLOT, SLOT), (table, two))
    l1, r1 = along_columns(one, 1), along_columns(one, -1)
    q_head, q_shared, value_left, value_right = kernel(
        middle_kernel, "middle", (SLOT, (16, 32, HD), SLOT, SLOT), (table, order, two), flops=FLOPS
    )
    l3, r3 = along_columns(value_right, 1), along_columns(value_left, -1)
    main_left, main_right, swap = kernel(
        late_kernel, "late", (SLOT, SLOT, (2,) + SLOT), (table, two, q_head, l1, r1)
    )
    l2, r2 = along_columns(main_right, 1), along_columns(main_left, -1)
    sw = swapped(swap)
    s0 = swapped(own)
    (vh,) = kernel(value_kernel, "values", (PARTS,), (two, l3, r3), flops=FLOPS)
    (se,) = kernel(forwarded_kernel, "forwarded", (SLOT,), (table, l2, r2, vh))
    se = swapped(se)
    sent, o_oth, kh = kernel(
        first_kernel,
        "attend_first",
        (SENT, SLOT, POOL),
        (table, two, q_head, l1, r1, l2, r2, vh),
        flops=FLOPS,
    )
    o_oth, k2, v2 = kernel(
        edge_kernel,
        "attend_edge",
        (SLOT, POOL, POOL),
        (table, two, l1, r1, l2, r2, l3, r3, s0, sw, se, o_oth),
        aliases={11: 0},
    )
    o_left, o_right = along_columns(o_oth, 1), along_columns(o_oth, -1)
    (sent,) = kernel(
        last_kernel,
        "attend_last",
        (SENT,),
        (table, two, q_head, q_shared, l1, r1, s0, sw, kh, vh, k2, v2, sent),
        (pltpu.VMEM(POOL, BF), pltpu.VMEM(POOL, BF)),
        aliases={12: 0},
    )
    (sent,) = kernel(merge_kernel, "merge", (SENT,), (table, o_left, o_right, sent), aliases={3: 0})
    return kernel(unpack_kernel, "unpack", (queries.shape,), (exchanged(sent),))[0]


def solution(mesh):
    blk, uly, dp = (mesh.shape[name] for name in ("blk", "uly", "dp"))
    fine = Mesh(
        mesh.devices.reshape(blk // 2, 2, uly // 2, 2, dp), ("col", "half", "x", "core", "dp")
    )
    tokens = ("dp", "col", "half", "x", "core")
    placed = (P(tokens, None), P(tokens, None), P(tokens, None), P("dp"), P("dp", None))
    return jax.shard_map(
        shards, mesh=fine, in_specs=placed, out_specs=P(tokens, None), check_vma=False
    )
```

```python
import jax
import jax.numpy as jnp
import numpy as np
from jax import lax
from jax.experimental import pallas as pl
from jax.experimental.pallas import tpu as pltpu
from jax.sharding import Mesh
from jax.sharding import PartitionSpec as P

HD = 128
TOK_TILE = 256
WIN = 9
COLS = 8
GROUP = ("half", "x", "core")
VMEM = pl.BlockSpec(memory_space=pltpu.VMEM)
SMEM = pl.BlockSpec(memory_space=pltpu.SMEM)
ANY = pl.BlockSpec(memory_space=pl.ANY)
BF = jnp.bfloat16
F32 = jnp.float32
MIB = 1024 * 1024
POWER = HD ** (-0.5) * 1.4426950408889634
ONE, MAIN, VALUE = slice(0, 64), slice(64, 128), slice(128, 192)
QUERY, REST = slice(192, 224), slice(224, 288)
AT_W, AT_TILE, AT_HEAD, AT_SHARED = 0, 8, 16, 64
OTHER, THIS = 0, 1


def frequency_rows():
    pair = lax.broadcasted_iota(jnp.int32, (8, HD), 1) // 2
    nt = (HD - 4 * (HD // 6)) // 2
    ns = HD // 6
    rows = []
    for first, count in ((0, nt), (nt, ns), (nt + ns, ns)):
        within = (pair - first).astype(F32)
        freq = jnp.exp(within * float(-np.log(10000.0) / count))
        rows.append(jnp.where((pair >= first) & (pair < first + count), freq, 0.0)[0:1])
    return rows


def turns(tile, frame_in_tile):
    frame = (tile // 32 * 4 + frame_in_tile).astype(F32)
    row0 = (tile // 8 % 4 * 8).astype(F32)
    col0 = (tile % 8 * 8).astype(F32)
    token = lax.broadcasted_iota(jnp.int32, (64, HD), 0)
    row = row0 + (token // 8).astype(F32)
    col = col0 + (token % 8).astype(F32)
    by_frame, by_row, by_col = frequency_rows()
    angle = frame * by_frame + row * by_row + col * by_col
    cosine = jnp.cos(angle)
    sine = jnp.sin(angle)
    even = lax.broadcasted_iota(jnp.int32, (64, HD), 1) % 2 == 0
    return cosine, jnp.where(even, -sine, 0.0), jnp.where(even, 0.0, sine)


def turned(x, factors):
    here, after, before = factors
    x = x.astype(F32)
    return (x * here + pltpu.roll(x, HD - 1, 1) * after + pltpu.roll(x, 1, 1) * before).astype(BF)


def plan(order, nb, table):
    k = lax.axis_index("col")
    w = lax.rem(order[k * 4], COLS)
    table[AT_W] = w
    k_oth = lax.rem(jnp.where((w == 1) | (w == 7), k + 7, k + 1), COLS)
    near = jnp.where(w == 7, 7, 1)
    for column, base in ((OTHER, k_oth), (THIS, k)):
        low, high = 0, 2
        first = [0, 0]
        for t in range(4):
            upper = lax.rem(order[base * 4 + t] // 8, 4) < 2
            table[AT_TILE + 4 * column + jnp.where(upper, low, high)] = t
            first = [jnp.where(upper, t, first[0]), jnp.where(upper, first[1], t)]
            low, high = low + upper.astype(jnp.int32), high + 1 - upper.astype(jnp.int32)
        for p in range(2):
            for j in range(WIN):
                n = nb[j, base * 4 + first[p]]
                d = lax.rem(n // 4 - k + COLS, COLS)
                t = lax.rem(n, 4)
                at = WIN * (2 * column + p) + j
                table[AT_HEAD + at] = jnp.where(d == 0, 0, jnp.where(d == 1, 4, 8)) + t
                table[AT_SHARED + at] = jnp.where(d == 0, 0, jnp.where(d == near, 4, 8)) + t
    return w


def rotate_kernel(order, nb, q_hbm, k_hbm, v_hbm, out_hbm, table, held, packed, sems, out_sems):
    x = lax.axis_index("x")
    frame_in_tile = lax.rem(x, 2) * 2 + lax.axis_index("core")
    slot = lax.axis_index("col") * 4 + lax.axis_index("half") * 2 + x // 2
    width = 2 * 3 * HD
    copies = []
    for part in range(4):
        for which, ref in enumerate((k_hbm, q_hbm, v_hbm)):
            columns = pl.ds(part * width, width)
            copies.append(
                pltpu.make_async_copy(
                    ref.at[:, columns], held.at[which, :, columns], sems.at[3 * part + which]
                )
            )
    for copy in copies:
        copy.start()
    w = plan(order, nb, table)
    edge = (w == 0) | (w == 7)
    factors = turns(order[slot], frame_in_tile)
    outs = []
    for part in range(4):
        for which in range(3):
            copies[3 * part + which].wait()
        for g in range(2 * part, 2 * part + 2):
            at = [slice((3 * g + h) * HD, (3 * g + h + 1) * HD) for h in range(3)]
            key = [turned(held[0, :, a], factors) for a in at]
            query = [held[1, :, a] for a in at]
            value = [held[2, :, a] for a in at]
            for c in range(2):
                to = 2 * g + c
                mine = slice(32 * c, 32 * c + 32)
                shared = jnp.concatenate([key[2][mine], value[2][mine]])
                packed[to, ONE, :] = jnp.where(edge, key[c], shared)
                packed[to, MAIN, :] = jnp.where(edge, query[c], key[c])
                packed[to, VALUE, :] = value[c]
                packed[to, QUERY, :] = query[2][mine]
                packed[to, REST, :] = jnp.where(edge, shared, query[c])
        four = pl.ds(4 * part, 4)
        outs.append(
            pltpu.make_async_copy(packed.at[four], out_hbm.at[four], out_sems.at[part])
        )
        outs[-1].start()
    for out in outs:
        out.wait()


def early_kernel(two, one):
    one[...] = two[:, ONE]


def middle_kernel(table, order, two, q_head, q_shared, value_left, value_right):
    w = table[AT_W]
    edge = (w == 0) | (w == 7)
    col, core = lax.axis_index("col"), lax.axis_index("core")

    @pl.loop(0, 16)
    def _(source):
        factors = turns(order[col * 4 + source // 4], lax.rem(source, 4))
        held = two[source]
        q_head[source] = turned(jnp.where(edge, held[MAIN], held[REST]), factors)
        mine = [jnp.where(core == 0, f[0:32], f[32:64]) for f in factors]
        q_shared[source] = turned(held[QUERY], mine)

    for out, special in ((value_left, 1), (value_right, 6)):

        @pl.when(w == special)
        def _(out=out):
            out[:, 0:32] = q_shared[...]
            out[:, 32:64] = q_shared[...]

        @pl.when(w != special)
        def _(out=out):
            out[...] = two[:, VALUE]


def late_kernel(table, two, q_head, l1, r1, main_left, main_right, swap):
    w = table[AT_W]
    edge = (w == 0) | (w == 7)
    for out, special, source in ((main_left, 1, r1), (main_right, 6, l1)):

        @pl.when(w == special)
        def _(out=out, source=source):
            out[...] = source[...]

        @pl.when(edge)
        def _(out=out):
            out[...] = q_head[...]

        @pl.when((w != special) & jnp.logical_not(edge))
        def _(out=out):
            out[...] = two[:, MAIN]

    @pl.when(edge)
    def _():
        swap[0] = two[:, REST]

    @pl.when(jnp.logical_not(edge))
    def _():
        swap[0] = two[:, ONE]

    swap[1] = l1[...]
    swap[2] = r1[...]


def attend(q, kp, vp, picks):
    top = weights = acc = None
    for pick in picks:
        s = lax.dot_general(q, kp[pick], (((1,), (1,)), ((), ())), preferred_element_type=F32)
        high = jnp.max(s, axis=1, keepdims=True)
        new = high if top is None else jnp.maximum(top, high)
        p = jnp.exp2((s - new) * POWER)
        part = jnp.dot(p.astype(BF), whole(vp, pick), preferred_element_type=F32)
        if top is None:
            weights, acc = p, part
        else:
            shrink = jnp.exp2((top - new) * POWER)
            weights, acc = weights * shrink + p, acc * shrink + part
        top = new
    return (acc / jnp.sum(weights, axis=1, keepdims=True)).astype(BF)


def whole(ref, *index):
    return ref[index].reshape(-1, HD)


def attend_column(table, column, at, query, kp, vp, store):
    @pl.loop(0, 2)
    def _(p):
        fours = [pl.ds(table[AT_TILE + 4 * column + 2 * p + i] * 4, 4) for i in range(2)]
        picks = [table[at + (2 * column + p) * WIN + j] for j in range(WIN)]
        o = attend(jnp.concatenate([query(four) for four in fours]), kp, vp, picks)
        half = o.shape[0] // 2
        for i, four in enumerate(fours):
            store(four, o[i * half : (i + 1) * half].reshape(4, -1, HD))


def fill_shared(base, mine, other, k2, v2):
    for t in range(4):
        four = slice(4 * t, 4 * t + 4)
        for pool, part in ((k2, slice(0, 32)), (v2, slice(32, 64))):
            pool[base + t, 0:128] = mine(four, part)
            pool[base + t, 128:256] = other(four, part)


def value_kernel(two, l3, r3, vh):
    for t in range(4):
        four = slice(4 * t, 4 * t + 4)
        vh[t] = two[four, VALUE]
        vh[4 + t] = r3[four]
        vh[8 + t] = l3[four]


def shared_kernel(table, two, l1, r1, sw, k2, v2):
    w = table[AT_W]
    edge = (w == 0) | (w == 7)
    left = (lambda f, p: whole(l1, f, p)), (lambda f, p: whole(sw, 1, f, p))
    right = (lambda f, p: whole(r1, f, p)), (lambda f, p: whole(sw, 2, f, p))

    def own(rows):
        mine = lambda f, p: whole(two, f, slice(rows.start + p.start, rows.start + p.stop))
        fill_shared(0, mine, lambda f, p: whole(sw, 0, f, p), k2, v2)

    @pl.when(jnp.logical_not(edge))
    def _():
        own(ONE)
        fill_shared(4, *right, k2, v2)
        fill_shared(8, *left, k2, v2)

    @pl.when(w == 0)
    def _():
        own(REST)
        fill_shared(4, *right, k2, v2)

    @pl.when(w == 7)
    def _():
        own(REST)
        fill_shared(4, *left, k2, v2)


def forwarded_kernel(table, l2, r2, vh, k2, out):
    del vh, k2
    w = table[AT_W]

    @pl.when(w == 0)
    def _():
        out[...] = r2[...]

    @pl.when(w == 7)
    def _():
        out[...] = l2[...]


def first_kernel(table, two, q_head, l1, r1, l2, r2, vh, sent, o_oth, kh):
    w = table[AT_W]
    inner = (w == 1) | (w == 6)
    edge = (w == 0) | (w == 7)

    @pl.when(jnp.logical_not(edge))
    def _():
        for t in range(4):
            four = slice(4 * t, 4 * t + 4)
            kh[t] = whole(two, four, MAIN)
        for base, special, early, late in ((4, 6, r1, r2), (8, 1, l1, l2)):

            @pl.when(w == special)
            def _(base=base, early=early):
                for t in range(4):
                    kh[base + t] = whole(early, slice(4 * t, 4 * t + 4))

            @pl.when(w != special)
            def _(base=base, late=late):
                for t in range(4):
                    kh[base + t] = whole(late, slice(4 * t, 4 * t + 4))

    def to_other(four, o):
        o_oth[four] = o

    def to_sent(four, o):
        sent[four, 0:64] = o

    for special, source in ((1, l2), (6, r2)):

        @pl.when(w == special)
        def _(source=source):
            query = lambda four: whole(source, four)
            attend_column(table, OTHER, AT_HEAD, query, kh, vh, to_other)

    @pl.when(jnp.logical_not(inner | edge))
    def _():
        query = lambda four: whole(q_head, four)
        attend_column(table, THIS, AT_HEAD, query, kh, vh, to_sent)


def edge_kernel(table, l2, r2, l3, r3, se, oth_in, k_in, v_in, o_oth, k2, v2):
    del oth_in, k_in, v_in
    w = table[AT_W]

    def to_other(four, o):
        o_oth[four, 0:32] = o

    for special, far, asked in ((0, r2, r3), (7, l2, l3)):

        @pl.when(w == special)
        def _(far=far, asked=asked):
            fill_shared(8, lambda f, p: whole(far, f, p), lambda f, p: whole(se, f, p), k2, v2)
            query = lambda four: whole(asked, four, slice(0, 32))
            attend_column(table, OTHER, AT_SHARED, query, k2, v2, to_other)


def last_kernel(table, q_head, q_shared, kh, vh, k2, v2, sent_in, sent):
    del sent_in
    w = table[AT_W]
    inner = (w == 1) | (w == 6)

    def to_head(four, o):
        sent[four, 0:64] = o

    def to_shared(four, o):
        sent[four, 64:96] = o

    @pl.when(inner)
    def _():
        query = lambda four: whole(q_head, four)
        attend_column(table, THIS, AT_HEAD, query, kh, vh, to_head)

    @pl.when(jnp.logical_not(inner))
    def _():
        query = lambda four: whole(q_shared, four)
        attend_column(table, THIS, AT_SHARED, query, k2, v2, to_shared)


def merge_kernel(table, o_left, o_right, sent_in, sent):
    del sent_in
    w = table[AT_W]

    @pl.when(w == 0)
    def _():
        sent[:, 0:64] = o_right[...]

    @pl.when(w == 7)
    def _():
        sent[:, 0:64] = o_left[...]

    @pl.when(w == 1)
    def _():
        sent[:, 64:96] = o_left[:, 0:32]

    @pl.when(w == 6)
    def _():
        sent[:, 64:96] = o_right[:, 0:32]


def unpack_kernel(in_ref, out_ref):
    for g in range(8):
        for h in range(2):
            out_ref[:, (3 * g + h) * HD : (3 * g + h + 1) * HD] = in_ref[2 * g + h, 0:64, :]
        last = slice((3 * g + 2) * HD, (3 * g + 3) * HD)
        out_ref[0:32, last] = in_ref[2 * g, 64:96, :]
        out_ref[32:64, last] = in_ref[2 * g + 1, 64:96, :]


def along_columns(block, distance):
    n = 2 * COLS
    return lax.ppermute(block, ("col", "half"), [(i, (i + 2 * distance) % n) for i in range(n)])


def swapped(block):
    return lax.ppermute(block, "core", [(0, 1), (1, 0)])


def exchanged(block):
    return lax.all_to_all(block, GROUP, split_axis=0, concat_axis=0, tiled=True)


SLOT = (16, 64, HD)
SENT = (16, 96, HD)
POOL = (12, TOK_TILE, HD)
PARTS = (12, 4, 64, HD)
FLOPS = 20_000_000_000


def kernel(body, name, outs, inputs, scratch=(), limit=32, aliases={}, flops=None, space=VMEM):
    return pl.pallas_call(
        body,
        out_shape=tuple(
            jax.ShapeDtypeStruct(shape, BF if len(shape) > 1 else jnp.int32) for shape in outs
        ),
        in_specs=[SMEM if i.dtype == jnp.int32 else space for i in inputs],
        out_specs=tuple(space if len(shape) > 1 else SMEM for shape in outs),
        scratch_shapes=list(scratch),
        input_output_aliases=aliases,
        compiler_params=pltpu.CompilerParams(vmem_limit_bytes=limit * MIB),
        cost_estimate=flops and pl.CostEstimate(flops=flops, bytes_accessed=0, transcendentals=0),
        name=name,
    )(*inputs)


def shards(queries, keys, values, order, nb):
    two, table = kernel(
        rotate_kernel,
        "rotate",
        ((16, 288, HD), (128,)),
        (order, nb.T, queries, keys, values),
        (
            pltpu.VMEM((3,) + queries.shape, BF),
            pltpu.VMEM((16, 288, HD), BF),
            pltpu.SemaphoreType.DMA((12,)),
            pltpu.SemaphoreType.DMA((4,)),
        ),
        limit=60,
        space=ANY,
    )
    two = exchanged(two)
    (one,) = kernel(early_kernel, "early", (SLOT,), (two,))
    l1, r1 = along_columns(one, 1), along_columns(one, -1)
    q_head, q_shared, value_left, value_right = kernel(
        middle_kernel, "middle", (SLOT, (16, 32, HD), SLOT, SLOT), (table, order, two), flops=FLOPS
    )
    l3, r3 = along_columns(value_right, 1), along_columns(value_left, -1)
    main_left, main_right, swap = kernel(
        late_kernel, "late", (SLOT, SLOT, (3,) + SLOT), (table, two, q_head, l1, r1)
    )
    l2, r2 = along_columns(main_right, 1), along_columns(main_left, -1)
    sw = swapped(swap)
    (vh,) = kernel(value_kernel, "values", (PARTS,), (two, l3, r3), flops=FLOPS)
    k2, v2 = kernel(shared_kernel, "shared", (POOL, POOL), (table, two, l1, r1, sw))
    (se,) = kernel(
        forwarded_kernel, "forwarded", (SLOT,), (table, l2, r2, vh, k2), space=VMEM
    )
    se = swapped(se)
    sent, o_oth, kh = kernel(
        first_kernel,
        "attend_first",
        (SENT, SLOT, POOL),
        (table, two, q_head, l1, r1, l2, r2, vh),
        flops=FLOPS,
    )
    o_oth, k2, v2 = kernel(
        edge_kernel,
        "attend_edge",
        (SLOT, POOL, POOL),
        (table, l2, r2, l3, r3, se, o_oth, k2, v2),
        aliases={6: 0, 7: 1, 8: 2},
    )
    o_left, o_right = along_columns(o_oth, 1), along_columns(o_oth, -1)
    (sent,) = kernel(
        last_kernel,
        "attend_last",
        (SENT,),
        (table, q_head, q_shared, kh, vh, k2, v2, sent),
        aliases={7: 0},
    )
    (sent,) = kernel(merge_kernel, "merge", (SENT,), (table, o_left, o_right, sent), aliases={3: 0})
    return kernel(unpack_kernel, "unpack", (queries.shape,), (exchanged(sent),))[0]


def solution(mesh):
    blk, uly, dp = (mesh.shape[name] for name in ("blk", "uly", "dp"))
    fine = Mesh(
        mesh.devices.reshape(blk // 2, 2, uly // 2, 2, dp), ("col", "half", "x", "core", "dp")
    )
    tokens = ("dp", "col", "half", "x", "core")
    placed = (P(tokens, None), P(tokens, None), P(tokens, None), P("dp"), P("dp", None))
    return jax.shard_map(
        shards, mesh=fine, in_specs=placed, out_specs=P(tokens, None), check_vma=False
    )
```

```python
import jax
import jax.numpy as jnp
import numpy as np
from jax import lax
from jax.experimental import pallas as pl
from jax.experimental.pallas import tpu as pltpu
from jax.sharding import Mesh
from jax.sharding import PartitionSpec as P

HD = 128
TOK_TILE = 256
WIN = 9
COLS = 8
GROUP = ("half", "x", "core")
VMEM = pl.BlockSpec(memory_space=pltpu.VMEM)
SMEM = pl.BlockSpec(memory_space=pltpu.SMEM)
ANY = pl.BlockSpec(memory_space=pl.ANY)
BF = jnp.bfloat16
F32 = jnp.float32
MIB = 1024 * 1024
POWER = HD ** (-0.5) * 1.4426950408889634
ONE, MAIN, VALUE = slice(0, 64), slice(64, 128), slice(128, 192)
QUERY, REST = slice(192, 224), slice(224, 288)
AT_W, AT_TILE, AT_HEAD, AT_SHARED = 0, 8, 16, 64
OTHER, THIS = 0, 1


def frequency_rows():
    pair = lax.broadcasted_iota(jnp.int32, (8, HD), 1) // 2
    nt = (HD - 4 * (HD // 6)) // 2
    ns = HD // 6
    rows = []
    for first, count in ((0, nt), (nt, ns), (nt + ns, ns)):
        within = (pair - first).astype(F32)
        freq = jnp.exp(within * float(-np.log(10000.0) / count))
        rows.append(jnp.where((pair >= first) & (pair < first + count), freq, 0.0)[0:1])
    return rows


def turns(tile, frame_in_tile):
    frame = (tile // 32 * 4 + frame_in_tile).astype(F32)
    row0 = (tile // 8 % 4 * 8).astype(F32)
    col0 = (tile % 8 * 8).astype(F32)
    token = lax.broadcasted_iota(jnp.int32, (64, HD), 0)
    row = row0 + (token // 8).astype(F32)
    col = col0 + (token % 8).astype(F32)
    by_frame, by_row, by_col = frequency_rows()
    angle = frame * by_frame + row * by_row + col * by_col
    cosine = jnp.cos(angle)
    sine = jnp.sin(angle)
    even = lax.broadcasted_iota(jnp.int32, (64, HD), 1) % 2 == 0
    return cosine, jnp.where(even, -sine, 0.0), jnp.where(even, 0.0, sine)


def turned(x, factors):
    here, after, before = factors
    x = x.astype(F32)
    return (x * here + pltpu.roll(x, HD - 1, 1) * after + pltpu.roll(x, 1, 1) * before).astype(BF)


def plan(order, nb, table):
    k = lax.axis_index("col")
    w = lax.rem(order[k * 4], COLS)
    table[AT_W] = w
    k_oth = lax.rem(jnp.where((w == 1) | (w == 7), k + 7, k + 1), COLS)
    near = jnp.where(w == 7, 7, 1)
    for column, base in ((OTHER, k_oth), (THIS, k)):
        low, high = 0, 2
        first = [0, 0]
        for t in range(4):
            upper = lax.rem(order[base * 4 + t] // 8, 4) < 2
            table[AT_TILE + 4 * column + jnp.where(upper, low, high)] = t
            first = [jnp.where(upper, t, first[0]), jnp.where(upper, first[1], t)]
            low, high = low + upper.astype(jnp.int32), high + 1 - upper.astype(jnp.int32)
        for p in range(2):
            counts = [0, 0, 0]
            for j in range(WIN):
                n = nb[j, base * 4 + first[p]]
                d = lax.rem(n // 4 - k + COLS, COLS)
                t = lax.rem(n, 4)
                at = WIN * (2 * column + p)
                table[AT_HEAD + at + j] = jnp.where(d == 0, 0, jnp.where(d == 1, 4, 8)) + t
                group = jnp.where(d == 0, 0, jnp.where(d == near, 1, 2))
                count = jnp.where(group == 0, counts[0], jnp.where(group == 1, counts[1], counts[2]))
                table[AT_SHARED + at + 3 * group + count] = 4 * group + t
                counts = [c + (group == g).astype(jnp.int32) for g, c in enumerate(counts)]
    return w


def rotate_kernel(order, nb, q_hbm, k_hbm, v_hbm, out_hbm, table, held, packed, sems, out_sems):
    x = lax.axis_index("x")
    frame_in_tile = lax.rem(x, 2) * 2 + lax.axis_index("core")
    slot = lax.axis_index("col") * 4 + lax.axis_index("half") * 2 + x // 2
    width = 2 * 3 * HD
    copies = []
    for part in range(4):
        for which, ref in enumerate((k_hbm, q_hbm, v_hbm)):
            columns = pl.ds(part * width, width)
            copies.append(
                pltpu.make_async_copy(
                    ref.at[:, columns], held.at[which, :, columns], sems.at[3 * part + which]
                )
            )
    for copy in copies:
        copy.start()
    w = plan(order, nb, table)
    edge = (w == 0) | (w == 7)
    factors = turns(order[slot], frame_in_tile)
    outs = []
    for part in range(4):
        for which in range(3):
            copies[3 * part + which].wait()
        for g in range(2 * part, 2 * part + 2):
            at = [slice((3 * g + h) * HD, (3 * g + h + 1) * HD) for h in range(3)]
            key = [turned(held[0, :, a], factors) for a in at]
            query = [held[1, :, a] for a in at]
            value = [held[2, :, a] for a in at]
            for c in range(2):
                to = 2 * g + c
                mine = slice(32 * c, 32 * c + 32)
                shared = jnp.concatenate([key[2][mine], value[2][mine]])
                packed[to, ONE, :] = jnp.where(edge, key[c], shared)
                packed[to, MAIN, :] = jnp.where(edge, query[c], key[c])
                packed[to, VALUE, :] = value[c]
                packed[to, QUERY, :] = query[2][mine]
                packed[to, REST, :] = jnp.where(edge, shared, query[c])
        four = pl.ds(4 * part, 4)
        outs.append(
            pltpu.make_async_copy(packed.at[four], out_hbm.at[four], out_sems.at[part])
        )
        outs[-1].start()
    for out in outs:
        out.wait()


def early_kernel(two, one):
    one[...] = two[:, ONE]


def middle_kernel(table, order, two, q_head, q_shared, main_left, main_right):
    w = table[AT_W]
    edge = (w == 0) | (w == 7)
    col, core = lax.axis_index("col"), lax.axis_index("core")

    @pl.loop(0, 16)
    def _(source):
        factors = turns(order[col * 4 + source // 4], lax.rem(source, 4))
        held = two[source]
        q_head[source] = turned(jnp.where(edge, held[MAIN], held[REST]), factors)
        mine = [jnp.where(core == 0, f[0:32], f[32:64]) for f in factors]
        q_shared[source] = turned(held[QUERY], mine)

    for out, special in ((main_left, 1), (main_right, 6)):

        @pl.when(w == special)
        def _(out=out):
            out[:, 0:32] = q_shared[...]
            out[:, 32:64] = q_shared[...]

        @pl.when(edge)
        def _(out=out):
            out[...] = q_head[...]

        @pl.when((w != special) & jnp.logical_not(edge))
        def _(out=out):
            out[...] = two[:, MAIN]


def late_kernel(table, two, l1, r1, value_left, value_right, swap):
    w = table[AT_W]
    edge = (w == 0) | (w == 7)
    for out, special, source in ((value_left, 1, r1), (value_right, 6, l1)):

        @pl.when(w == special)
        def _(out=out, source=source):
            out[...] = source[...]

        @pl.when(w != special)
        def _(out=out):
            out[...] = two[:, VALUE]

    @pl.when(edge)
    def _():
        swap[0] = two[:, REST]

    @pl.when(jnp.logical_not(edge))
    def _():
        swap[0] = two[:, ONE]

    swap[1] = l1[...]
    swap[2] = r1[...]


def steps(q, kp, vp, picks, state):
    top, weights, acc = state
    for pick in picks:
        s = lax.dot_general(q, kp[pick], (((1,), (1,)), ((), ())), preferred_element_type=F32)
        high = jnp.max(s, axis=1, keepdims=True)
        new = high if top is None else jnp.maximum(top, high)
        p = jnp.exp2((s - new) * POWER)
        part = jnp.dot(p.astype(BF), whole(vp, pick), preferred_element_type=F32)
        if top is None:
            weights, acc = p, part
        else:
            shrink = jnp.exp2((top - new) * POWER)
            weights, acc = weights * shrink + p, acc * shrink + part
        top = new
    return top, weights, acc


def finished(state):
    _, weights, acc = state
    return (acc / jnp.sum(weights, axis=1, keepdims=True)).astype(BF)


def whole(ref, *index):
    return ref[index].reshape(-1, HD)


def pair_of(table, column, at, p):
    fours = [pl.ds(table[AT_TILE + 4 * column + 2 * p + i] * 4, 4) for i in range(2)]
    return fours, [table[at + (2 * column + p) * WIN + j] for j in range(WIN)]


def store_pair(store, fours, o):
    half = o.shape[0] // 2
    for i, four in enumerate(fours):
        store(four, o[i * half : (i + 1) * half].reshape(4, -1, HD))


def attend_column(table, column, at, query, kp, vp, store):
    @pl.loop(0, 2)
    def _(p):
        fours, picks = pair_of(table, column, at, p)
        q = jnp.concatenate([query(four) for four in fours])
        store_pair(store, fours, finished(steps(q, kp, vp, picks, (None, None, None))))


def fill_shared(base, mine, other, k2, v2):
    for t in range(4):
        four = slice(4 * t, 4 * t + 4)
        for pool, part in ((k2, slice(0, 32)), (v2, slice(32, 64))):
            pool[base + t, 0:128] = mine(four, part)
            pool[base + t, 128:256] = other(four, part)


def scores_kernel(table, two, q_head, l1, r1, l3, r3, kh, prob, total, s_ref):
    w = table[AT_W]
    inner = (w == 1) | (w == 6)
    edge = (w == 0) | (w == 7)

    @pl.when(jnp.logical_not(edge))
    def _():
        for t in range(4):
            kh[t] = whole(two, slice(4 * t, 4 * t + 4), MAIN)
        for base, special, early, later in ((4, 6, r1, r3), (8, 1, l1, l3)):

            @pl.when(w == special)
            def _(base=base, early=early):
                for t in range(4):
                    kh[base + t] = whole(early, slice(4 * t, 4 * t + 4))

            @pl.when(w != special)
            def _(base=base, later=later):
                for t in range(4):
                    kh[base + t] = whole(later, slice(4 * t, 4 * t + 4))

    def weigh(column, query):
        @pl.loop(0, 2)
        def _(p):
            fours, picks = pair_of(table, column, AT_HEAD, p)
            for i, four in enumerate(fours):
                rows = slice(i * TOK_TILE, (i + 1) * TOK_TILE)
                q = query(four)
                top = None
                for j, pick in enumerate(picks):
                    s = lax.dot_general(
                        q, kh[pick], (((1,), (1,)), ((), ())), preferred_element_type=F32
                    )
                    s_ref[i, j] = s
                    top = s if top is None else jnp.maximum(top, s)
                top = jnp.max(top, axis=1, keepdims=True)
                sums = None
                for j in range(WIN):
                    weights = jnp.exp2((s_ref[i, j] - top) * POWER)
                    sums = weights if sums is None else sums + weights
                    prob[p, j, rows, :] = weights.astype(BF)
                sums = jnp.sum(sums, axis=1, keepdims=True)
                total[p, rows, :] = jnp.broadcast_to(sums, (TOK_TILE, HD))

    for special, source in ((1, l3), (6, r3)):

        @pl.when(w == special)
        def _(source=source):
            weigh(OTHER, lambda four: whole(source, four))

    @pl.when(jnp.logical_not(inner | edge))
    def _():
        weigh(THIS, lambda four: whole(q_head, four))


def shared_kernel(table, two, l1, r1, l3, r3, sw, k2, v2, tops, weights, accs):
    w = table[AT_W]
    edge = (w == 0) | (w == 7)
    left = (lambda f, p: whole(l1, f, p)), (lambda f, p: whole(sw, 1, f, p))
    right = (lambda f, p: whole(r1, f, p)), (lambda f, p: whole(sw, 2, f, p))

    def own(rows):
        mine = lambda f, p: whole(two, f, slice(rows.start + p.start, rows.start + p.stop))
        fill_shared(0, mine, lambda f, p: whole(sw, 0, f, p), k2, v2)

    @pl.when(jnp.logical_not(edge))
    def _():
        own(ONE)
        fill_shared(4, *right, k2, v2)
        fill_shared(8, *left, k2, v2)

    for special, near, asked in ((0, right, r3), (7, left, l3)):

        @pl.when(w == special)
        def _(near=near, asked=asked):
            own(REST)
            fill_shared(4, *near, k2, v2)

            @pl.loop(0, 2)
            def _(p):
                fours, picks = pair_of(table, OTHER, AT_SHARED, p)
                q = jnp.concatenate([whole(asked, four, slice(0, 32)) for four in fours])
                top, sums, acc = steps(q, k2, v2, picks[0:6], (None, None, None))
                tops[p] = jnp.broadcast_to(top, acc.shape)
                weights[p] = sums
                accs[p] = acc


def forwarded_kernel(table, l2, r2, kh, k2, out):
    del kh, k2
    w = table[AT_W]

    @pl.when(w == 0)
    def _():
        out[...] = r2[...]

    @pl.when(w == 7)
    def _():
        out[...] = l2[...]


def first_kernel(table, two, l2, r2, prob, total, sent, o_oth, vh):
    w = table[AT_W]
    inner = (w == 1) | (w == 6)
    edge = (w == 0) | (w == 7)

    @pl.when(jnp.logical_not(edge))
    def _():
        for t in range(4):
            four = slice(4 * t, 4 * t + 4)
            vh[t] = two[four, VALUE]
            vh[4 + t] = r2[four]
            vh[8 + t] = l2[four]

    def gather(column, store):
        @pl.loop(0, 2)
        def _(p):
            fours, picks = pair_of(table, column, AT_HEAD, p)
            acc = None
            for j, pick in enumerate(picks):
                part = jnp.dot(prob[p, j], whole(vh, pick), preferred_element_type=F32)
                acc = part if acc is None else acc + part
            store_pair(store, fours, (acc / total[p]).astype(BF))

    def to_other(four, o):
        o_oth[four] = o

    def to_sent(four, o):
        sent[four, 0:64] = o

    @pl.when(inner)
    def _():
        gather(OTHER, to_other)

    @pl.when(jnp.logical_not(inner | edge))
    def _():
        gather(THIS, to_sent)


def edge_kernel(
    table, l2, r2, l3, r3, se, tops, weights, accs, oth_in, k_in, v_in, o_oth, k2, v2
):
    del oth_in, k_in, v_in
    w = table[AT_W]

    def to_other(four, o):
        o_oth[four, 0:32] = o

    for special, far, asked in ((0, r2, r3), (7, l2, l3)):

        @pl.when(w == special)
        def _(far=far, asked=asked):
            fill_shared(8, lambda f, p: whole(far, f, p), lambda f, p: whole(se, f, p), k2, v2)

            @pl.loop(0, 2)
            def _(p):
                fours, picks = pair_of(table, OTHER, AT_SHARED, p)
                q = jnp.concatenate([whole(asked, four, slice(0, 32)) for four in fours])
                state = tops[p, :, 0:1], weights[p], accs[p]
                store_pair(to_other, fours, finished(steps(q, k2, v2, picks[6:9], state)))


def last_kernel(table, q_head, q_shared, kh, vh, k2, v2, sent_in, sent):
    del sent_in
    w = table[AT_W]
    inner = (w == 1) | (w == 6)

    def to_head(four, o):
        sent[four, 0:64] = o

    def to_shared(four, o):
        sent[four, 64:96] = o

    @pl.when(inner)
    def _():
        query = lambda four: whole(q_head, four)
        attend_column(table, THIS, AT_HEAD, query, kh, vh, to_head)

    @pl.when(jnp.logical_not(inner))
    def _():
        query = lambda four: whole(q_shared, four)
        attend_column(table, THIS, AT_SHARED, query, k2, v2, to_shared)


def merge_kernel(table, o_left, o_right, sent_in, sent):
    del sent_in
    w = table[AT_W]

    @pl.when(w == 0)
    def _():
        sent[:, 0:64] = o_right[...]

    @pl.when(w == 7)
    def _():
        sent[:, 0:64] = o_left[...]

    @pl.when(w == 1)
    def _():
        sent[:, 64:96] = o_left[:, 0:32]

    @pl.when(w == 6)
    def _():
        sent[:, 64:96] = o_right[:, 0:32]


def unpack_kernel(in_ref, out_ref):
    for g in range(8):
        for h in range(2):
            out_ref[:, (3 * g + h) * HD : (3 * g + h + 1) * HD] = in_ref[2 * g + h, 0:64, :]
        last = slice((3 * g + 2) * HD, (3 * g + 3) * HD)
        out_ref[0:32, last] = in_ref[2 * g, 64:96, :]
        out_ref[32:64, last] = in_ref[2 * g + 1, 64:96, :]


def along_columns(block, distance):
    n = 2 * COLS
    return lax.ppermute(block, ("col", "half"), [(i, (i + 2 * distance) % n) for i in range(n)])


def swapped(block):
    return lax.ppermute(block, "core", [(0, 1), (1, 0)])


def exchanged(block):
    return lax.all_to_all(block, GROUP, split_axis=0, concat_axis=0, tiled=True)


SLOT = (16, 64, HD)
SENT = (16, 96, HD)
POOL = (12, TOK_TILE, HD)
PARTS = (12, 4, 64, HD)
FLOPS = 20_000_000_000


def kernel(body, name, outs, inputs, scratch=(), limit=32, aliases={}, flops=None, space=VMEM):
    outs = [
        out
        if isinstance(out, jax.ShapeDtypeStruct)
        else jax.ShapeDtypeStruct(out, BF if len(out) > 1 else jnp.int32)
        for out in outs
    ]
    return pl.pallas_call(
        body,
        out_shape=tuple(outs),
        in_specs=[SMEM if i.dtype == jnp.int32 else space for i in inputs],
        out_specs=tuple(SMEM if out.dtype == jnp.int32 else space for out in outs),
        scratch_shapes=list(scratch),
        input_output_aliases=aliases,
        compiler_params=pltpu.CompilerParams(vmem_limit_bytes=limit * MIB),
        cost_estimate=flops and pl.CostEstimate(flops=flops, bytes_accessed=0, transcendentals=0),
        name=name,
    )(*inputs)


def shards(queries, keys, values, order, nb):
    two, table = kernel(
        rotate_kernel,
        "rotate",
        ((16, 288, HD), (128,)),
        (order, nb.T, queries, keys, values),
        (
            pltpu.VMEM((3,) + queries.shape, BF),
            pltpu.VMEM((16, 288, HD), BF),
            pltpu.SemaphoreType.DMA((12,)),
            pltpu.SemaphoreType.DMA((4,)),
        ),
        limit=60,
        space=ANY,
    )
    two = exchanged(two)
    (one,) = kernel(early_kernel, "early", (SLOT,), (two,))
    l1, r1 = along_columns(one, 1), along_columns(one, -1)
    q_head, q_shared, main_left, main_right = kernel(
        middle_kernel, "middle", (SLOT, (16, 32, HD), SLOT, SLOT), (table, order, two), flops=FLOPS
    )
    l3, r3 = along_columns(main_right, 1), along_columns(main_left, -1)
    value_left, value_right, swap = kernel(
        late_kernel, "late", (SLOT, SLOT, (3,) + SLOT), (table, two, l1, r1)
    )
    l2, r2 = along_columns(value_right, 1), along_columns(value_left, -1)
    sw = swapped(swap)
    kh, prob, total = kernel(
        scores_kernel,
        "scores",
        (POOL, (2, WIN, 512, TOK_TILE), jax.ShapeDtypeStruct((2, 512, HD), F32)),
        (table, two, q_head, l1, r1, l3, r3),
        (pltpu.VMEM((2, WIN, TOK_TILE, TOK_TILE), F32),),
        flops=FLOPS,
    )
    state = [jax.ShapeDtypeStruct((2, TOK_TILE, n), F32) for n in (HD, TOK_TILE, HD)]
    k2, v2, *state = kernel(
        shared_kernel, "shared", (POOL, POOL, *state), (table, two, l1, r1, l3, r3, sw)
    )
    (se,) = kernel(forwarded_kernel, "forwarded", (SLOT,), (table, l2, r2, kh, k2))
    se = swapped(se)
    sent, o_oth, vh = kernel(
        first_kernel,
        "attend_first",
        (SENT, SLOT, PARTS),
        (table, two, l2, r2, prob, total),
        flops=FLOPS,
    )
    o_oth, k2, v2 = kernel(
        edge_kernel,
        "attend_edge",
        (SLOT, POOL, POOL),
        (table, l2, r2, l3, r3, se, *state, o_oth, k2, v2),
        aliases={9: 0, 10: 1, 11: 2},
    )
    o_left, o_right = along_columns(o_oth, 1), along_columns(o_oth, -1)
    (sent,) = kernel(
        last_kernel,
        "attend_last",
        (SENT,),
        (table, q_head, q_shared, kh, vh, k2, v2, sent),
        aliases={7: 0},
    )
    (sent,) = kernel(merge_kernel, "merge", (SENT,), (table, o_left, o_right, sent), aliases={3: 0})
    return kernel(unpack_kernel, "unpack", (queries.shape,), (exchanged(sent),))[0]


def solution(mesh):
    blk, uly, dp = (mesh.shape[name] for name in ("blk", "uly", "dp"))
    fine = Mesh(
        mesh.devices.reshape(blk // 2, 2, uly // 2, 2, dp), ("col", "half", "x", "core", "dp")
    )
    tokens = ("dp", "col", "half", "x", "core")
    placed = (P(tokens, None), P(tokens, None), P(tokens, None), P("dp"), P("dp", None))
    return jax.shard_map(
        shards, mesh=fine, in_specs=placed, out_specs=P(tokens, None), check_vma=False
    )
```

```python
import jax
import jax.numpy as jnp
import numpy as np
from jax import lax
from jax.experimental import pallas as pl
from jax.experimental.pallas import tpu as pltpu
from jax.sharding import Mesh
from jax.sharding import PartitionSpec as P

HD = 128
TOK_TILE = 256
WIN = 9
COLS = 8
GROUP = ("half", "x", "core")
VMEM = pl.BlockSpec(memory_space=pltpu.VMEM)
SMEM = pl.BlockSpec(memory_space=pltpu.SMEM)
ANY = pl.BlockSpec(memory_space=pl.ANY)
BF = jnp.bfloat16
F32 = jnp.float32
MIB = 1024 * 1024
POWER = HD ** (-0.5) * 1.4426950408889634
ONE, MAIN, VALUE = slice(0, 64), slice(64, 128), slice(128, 192)
QUERY, REST = slice(192, 224), slice(224, 288)
AT_W, AT_TILE, AT_HEAD, AT_SHARED = 0, 8, 16, 64
OTHER, THIS = 0, 1


def frequency_rows():
    pair = lax.broadcasted_iota(jnp.int32, (8, HD), 1) // 2
    nt = (HD - 4 * (HD // 6)) // 2
    ns = HD // 6
    rows = []
    for first, count in ((0, nt), (nt, ns), (nt + ns, ns)):
        within = (pair - first).astype(F32)
        freq = jnp.exp(within * float(-np.log(10000.0) / count))
        rows.append(jnp.where((pair >= first) & (pair < first + count), freq, 0.0)[0:1])
    return rows


def turns(tile, frame_in_tile):
    frame = (tile // 32 * 4 + frame_in_tile).astype(F32)
    row0 = (tile // 8 % 4 * 8).astype(F32)
    col0 = (tile % 8 * 8).astype(F32)
    token = lax.broadcasted_iota(jnp.int32, (64, HD), 0)
    row = row0 + (token // 8).astype(F32)
    col = col0 + (token % 8).astype(F32)
    by_frame, by_row, by_col = frequency_rows()
    angle = frame * by_frame + row * by_row + col * by_col
    cosine = jnp.cos(angle)
    sine = jnp.sin(angle)
    even = lax.broadcasted_iota(jnp.int32, (64, HD), 1) % 2 == 0
    return cosine, jnp.where(even, -sine, 0.0), jnp.where(even, 0.0, sine)


def turned(x, factors):
    here, after, before = factors
    x = x.astype(F32)
    return (x * here + pltpu.roll(x, HD - 1, 1) * after + pltpu.roll(x, 1, 1) * before).astype(BF)


def plan(order, nb, table):
    k = lax.axis_index("col")
    w = lax.rem(order[k * 4], COLS)
    table[AT_W] = w
    k_oth = lax.rem(jnp.where((w == 1) | (w == 7), k + 7, k + 1), COLS)
    near = jnp.where(w == 7, 7, 1)
    for column, base in ((OTHER, k_oth), (THIS, k)):
        low, high = 0, 2
        first = [0, 0]
        for t in range(4):
            upper = lax.rem(order[base * 4 + t] // 8, 4) < 2
            table[AT_TILE + 4 * column + jnp.where(upper, low, high)] = t
            first = [jnp.where(upper, t, first[0]), jnp.where(upper, first[1], t)]
            low, high = low + upper.astype(jnp.int32), high + 1 - upper.astype(jnp.int32)
        for p in range(2):
            counts = [0, 0, 0]
            for j in range(WIN):
                n = nb[j, base * 4 + first[p]]
                d = lax.rem(n // 4 - k + COLS, COLS)
                t = lax.rem(n, 4)
                at = WIN * (2 * column + p)
                table[AT_HEAD + at + j] = jnp.where(d == 0, 0, jnp.where(d == 1, 4, 8)) + t
                group = jnp.where(d == 0, 0, jnp.where(d == near, 1, 2))
                count = jnp.where(group == 0, counts[0], jnp.where(group == 1, counts[1], counts[2]))
                table[AT_SHARED + at + 3 * group + count] = 4 * group + t
                counts = [c + (group == g).astype(jnp.int32) for g, c in enumerate(counts)]
    return w


def rotate_kernel(order, nb, q_hbm, k_hbm, v_hbm, out_hbm, table, held, packed, sems, out_sems):
    x = lax.axis_index("x")
    frame_in_tile = lax.rem(x, 2) * 2 + lax.axis_index("core")
    slot = lax.axis_index("col") * 4 + lax.axis_index("half") * 2 + x // 2
    width = 2 * 3 * HD
    copies = []
    for part in range(4):
        for which, ref in enumerate((k_hbm, q_hbm, v_hbm)):
            columns = pl.ds(part * width, width)
            copies.append(
                pltpu.make_async_copy(
                    ref.at[:, columns], held.at[which, :, columns], sems.at[3 * part + which]
                )
            )
    for copy in copies:
        copy.start()
    w = plan(order, nb, table)
    edge = (w == 0) | (w == 7)
    factors = turns(order[slot], frame_in_tile)
    outs = []
    for part in range(4):
        for which in range(3):
            copies[3 * part + which].wait()
        for g in range(2 * part, 2 * part + 2):
            at = [slice((3 * g + h) * HD, (3 * g + h + 1) * HD) for h in range(3)]
            key = [turned(held[0, :, a], factors) for a in at]
            query = [held[1, :, a] for a in at]
            value = [held[2, :, a] for a in at]
            for c in range(2):
                to = 2 * g + c
                mine = slice(32 * c, 32 * c + 32)
                shared = jnp.concatenate([key[2][mine], value[2][mine]])
                packed[to, ONE, :] = jnp.where(edge, key[c], shared)
                packed[to, MAIN, :] = jnp.where(edge, query[c], key[c])
                packed[to, VALUE, :] = value[c]
                packed[to, QUERY, :] = query[2][mine]
                packed[to, REST, :] = jnp.where(edge, shared, query[c])
        four = pl.ds(4 * part, 4)
        outs.append(
            pltpu.make_async_copy(packed.at[four], out_hbm.at[four], out_sems.at[part])
        )
        outs[-1].start()
    for out in outs:
        out.wait()


def early_kernel(two, one):
    one[...] = two[:, ONE]


def middle_kernel(table, order, two, q_head, q_shared, main_left, main_right):
    w = table[AT_W]
    edge = (w == 0) | (w == 7)
    col, core = lax.axis_index("col"), lax.axis_index("core")

    @pl.loop(0, 16)
    def _(source):
        factors = turns(order[col * 4 + source // 4], lax.rem(source, 4))
        held = two[source]
        q_head[source] = turned(jnp.where(edge, held[MAIN], held[REST]), factors)
        mine = [jnp.where(core == 0, f[0:32], f[32:64]) for f in factors]
        q_shared[source] = turned(held[QUERY], mine)

    for out, special in ((main_left, 1), (main_right, 6)):

        @pl.when(w == special)
        def _(out=out):
            out[:, 0:32] = q_shared[...]
            out[:, 32:64] = q_shared[...]

        @pl.when(edge)
        def _(out=out):
            out[...] = q_head[...]

        @pl.when((w != special) & jnp.logical_not(edge))
        def _(out=out):
            out[...] = two[:, MAIN]


def late_kernel(table, two, l1, r1, value_left, value_right, swap):
    w = table[AT_W]
    edge = (w == 0) | (w == 7)
    for out, special, source in ((value_left, 1, r1), (value_right, 6, l1)):

        @pl.when(w == special)
        def _(out=out, source=source):
            out[...] = source[...]

        @pl.when(w != special)
        def _(out=out):
            out[...] = two[:, VALUE]

    @pl.when(edge)
    def _():
        swap[0] = two[:, REST]

    @pl.when(jnp.logical_not(edge))
    def _():
        swap[0] = two[:, ONE]

    swap[1] = l1[...]
    swap[2] = r1[...]


def steps(q, kp, vp, picks, state):
    top, weights, acc = state
    for pick in picks:
        s = lax.dot_general(q, kp[pick], (((1,), (1,)), ((), ())), preferred_element_type=F32)
        high = jnp.max(s, axis=1, keepdims=True)
        new = high if top is None else jnp.maximum(top, high)
        p = jnp.exp2((s - new) * POWER)
        part = jnp.dot(p.astype(BF), whole(vp, pick), preferred_element_type=F32)
        if top is None:
            weights, acc = p, part
        else:
            shrink = jnp.exp2((top - new) * POWER)
            weights, acc = weights * shrink + p, acc * shrink + part
        top = new
    return top, weights, acc


def finished(state):
    _, weights, acc = state
    return (acc / jnp.sum(weights, axis=1, keepdims=True)).astype(BF)


def whole(ref, *index):
    return ref[index].reshape(-1, HD)


def pair_of(table, column, at, p, only=None):
    tiles = range(2) if only is None else (only,)
    fours = [pl.ds(table[AT_TILE + 4 * column + 2 * p + i] * 4, 4) for i in tiles]
    return fours, [table[at + (2 * column + p) * WIN + j] for j in range(WIN)]


def store_pair(store, fours, o):
    half = o.shape[0] // 2
    for i, four in enumerate(fours):
        store(four, o[i * half : (i + 1) * half].reshape(4, -1, HD))


def attend_column(table, column, at, query, kp, vp, store):
    @pl.loop(0, 2)
    def _(p):
        fours, picks = pair_of(table, column, at, p)
        q = jnp.concatenate([query(four) for four in fours])
        store_pair(store, fours, finished(steps(q, kp, vp, picks, (None, None, None))))


def fill_shared(base, mine, other, k2, v2):
    for t in range(4):
        four = slice(4 * t, 4 * t + 4)
        for pool, part in ((k2, slice(0, 32)), (v2, slice(32, 64))):
            pool[base + t, 0:128] = mine(four, part)
            pool[base + t, 128:256] = other(four, part)


def scores_kernel(table, two, q_head, l1, r1, l3, r3, kh, prob, total, s_ref):
    w = table[AT_W]
    inner = (w == 1) | (w == 6)
    edge = (w == 0) | (w == 7)

    @pl.when(jnp.logical_not(edge))
    def _():
        for t in range(4):
            kh[t] = whole(two, slice(4 * t, 4 * t + 4), MAIN)
        for base, special, early, later in ((4, 6, r1, r3), (8, 1, l1, l3)):

            @pl.when(w == special)
            def _(base=base, early=early):
                for t in range(4):
                    kh[base + t] = whole(early, slice(4 * t, 4 * t + 4))

            @pl.when(w != special)
            def _(base=base, later=later):
                for t in range(4):
                    kh[base + t] = whole(later, slice(4 * t, 4 * t + 4))

    @pl.when(jnp.logical_not(edge))
    def _():
        column = jnp.where(inner, OTHER, THIS)

        @pl.loop(0, 4)
        def _(n):
            p, i = n // 2, lax.rem(n, 2)
            fours, picks = pair_of(table, column, AT_HEAD, p, i)
            four = fours[0]
            q = jnp.where(w == 1, whole(l3, four), jnp.where(w == 6, whole(r3, four), whole(q_head, four)))
            rows = pl.ds(pl.multiple_of(i * TOK_TILE, TOK_TILE), TOK_TILE)
            top = None
            for j, pick in enumerate(picks):
                s = lax.dot_general(q, kh[pick], (((1,), (1,)), ((), ())), preferred_element_type=F32)
                s_ref[j] = s
                top = s if top is None else jnp.maximum(top, s)
            top = jnp.max(top, axis=1, keepdims=True)
            sums = None
            for j in range(WIN):
                weights = jnp.exp2((s_ref[j] - top) * POWER)
                sums = weights if sums is None else sums + weights
                prob[p, j, rows, :] = weights.astype(BF)
            sums = jnp.sum(sums, axis=1, keepdims=True)
            total[p, rows, :] = jnp.broadcast_to(sums, (TOK_TILE, HD))


def shared_kernel(table, two, l1, r1, l3, r3, sw, k2, v2, tops, weights, accs):
    w = table[AT_W]
    edge = (w == 0) | (w == 7)
    left = (lambda f, p: whole(l1, f, p)), (lambda f, p: whole(sw, 1, f, p))
    right = (lambda f, p: whole(r1, f, p)), (lambda f, p: whole(sw, 2, f, p))

    def own(rows):
        mine = lambda f, p: whole(two, f, slice(rows.start + p.start, rows.start + p.stop))
        fill_shared(0, mine, lambda f, p: whole(sw, 0, f, p), k2, v2)

    @pl.when(jnp.logical_not(edge))
    def _():
        own(ONE)
        fill_shared(4, *right, k2, v2)
        fill_shared(8, *left, k2, v2)

    @pl.when(edge)
    def _():
        own(REST)
        for special, near in ((0, right), (7, left)):

            @pl.when(w == special)
            def _(near=near):
                fill_shared(4, *near, k2, v2)

        @pl.loop(0, 2)
        def _(p):
            fours, picks = pair_of(table, OTHER, AT_SHARED, p)
            top, sums, acc = steps(asked(w, l3, r3, fours), k2, v2, picks[0:6], (None, None, None))
            tops[p] = jnp.broadcast_to(top, acc.shape)
            weights[p] = sums
            accs[p] = acc


def asked(w, l3, r3, fours):
    half = slice(0, 32)
    return jnp.concatenate(
        [jnp.where(w == 7, whole(l3, four, half), whole(r3, four, half)) for four in fours]
    )


def forwarded_kernel(table, l2, r2, kh, k2, out):
    del kh, k2
    w = table[AT_W]

    @pl.when(w == 0)
    def _():
        out[...] = r2[...]

    @pl.when(w == 7)
    def _():
        out[...] = l2[...]


def first_kernel(table, two, l2, r2, prob, total, sent, o_oth, vh):
    w = table[AT_W]
    inner = (w == 1) | (w == 6)
    edge = (w == 0) | (w == 7)

    @pl.when(jnp.logical_not(edge))
    def _():
        for t in range(4):
            four = slice(4 * t, 4 * t + 4)
            vh[t] = two[four, VALUE]
            vh[4 + t] = r2[four]
            vh[8 + t] = l2[four]

        column = jnp.where(inner, OTHER, THIS)

        @pl.loop(0, 2)
        def _(p):
            fours, picks = pair_of(table, column, AT_HEAD, p)
            acc = None
            for j, pick in enumerate(picks):
                part = jnp.dot(prob[p, j], whole(vh, pick), preferred_element_type=F32)
                acc = part if acc is None else acc + part

            def store(four, o):
                o_oth[four] = o
                sent[four, 0:64] = o

            store_pair(store, fours, (acc / total[p]).astype(BF))


def edge_kernel(table, far, l3, r3, se, tops, weights, accs, oth_in, k_in, v_in, o_oth, k2, v2):
    del oth_in, k_in, v_in
    w = table[AT_W]

    def to_other(four, o):
        o_oth[four, 0:32] = o

    @pl.when((w == 0) | (w == 7))
    def _():
        fill_shared(8, lambda f, p: whole(far, f, p), lambda f, p: whole(se, f, p), k2, v2)

        @pl.loop(0, 2)
        def _(p):
            fours, picks = pair_of(table, OTHER, AT_SHARED, p)
            state = tops[p, :, 0:1], weights[p], accs[p]
            q = asked(w, l3, r3, fours)
            store_pair(to_other, fours, finished(steps(q, k2, v2, picks[6:9], state)))


def last_kernel(table, q_head, q_shared, kh, vh, k2, v2, sent_in, sent):
    del sent_in
    w = table[AT_W]
    inner = (w == 1) | (w == 6)

    def to_head(four, o):
        sent[four, 0:64] = o

    def to_shared(four, o):
        sent[four, 64:96] = o

    @pl.when(inner)
    def _():
        query = lambda four: whole(q_head, four)
        attend_column(table, THIS, AT_HEAD, query, kh, vh, to_head)

    @pl.when(jnp.logical_not(inner))
    def _():
        query = lambda four: whole(q_shared, four)
        attend_column(table, THIS, AT_SHARED, query, k2, v2, to_shared)


def merge_kernel(table, o_left, o_right, sent_in, sent):
    del sent_in
    w = table[AT_W]

    @pl.when(w == 0)
    def _():
        sent[:, 0:64] = o_right[...]

    @pl.when(w == 7)
    def _():
        sent[:, 0:64] = o_left[...]

    @pl.when(w == 1)
    def _():
        sent[:, 64:96] = o_left[:, 0:32]

    @pl.when(w == 6)
    def _():
        sent[:, 64:96] = o_right[:, 0:32]


def unpack_kernel(in_ref, out_ref):
    for g in range(8):
        for h in range(2):
            out_ref[:, (3 * g + h) * HD : (3 * g + h + 1) * HD] = in_ref[2 * g + h, 0:64, :]
        last = slice((3 * g + 2) * HD, (3 * g + 3) * HD)
        out_ref[0:32, last] = in_ref[2 * g, 64:96, :]
        out_ref[32:64, last] = in_ref[2 * g + 1, 64:96, :]


def along_columns(block, distance):
    n = 2 * COLS
    return lax.ppermute(block, ("col", "half"), [(i, (i + 2 * distance) % n) for i in range(n)])


def swapped(block):
    return lax.ppermute(block, "core", [(0, 1), (1, 0)])


def exchanged(block):
    return lax.all_to_all(block, GROUP, split_axis=0, concat_axis=0, tiled=True)


SLOT = (16, 64, HD)
SENT = (16, 96, HD)
POOL = (12, TOK_TILE, HD)
PARTS = (12, 4, 64, HD)
FLOPS = 20_000_000_000


def kernel(body, name, outs, inputs, scratch=(), limit=32, aliases={}, flops=None, space=VMEM):
    outs = [
        out
        if isinstance(out, jax.ShapeDtypeStruct)
        else jax.ShapeDtypeStruct(out, BF if len(out) > 1 else jnp.int32)
        for out in outs
    ]
    return pl.pallas_call(
        body,
        out_shape=tuple(outs),
        in_specs=[SMEM if i.dtype == jnp.int32 else space for i in inputs],
        out_specs=tuple(SMEM if out.dtype == jnp.int32 else space for out in outs),
        scratch_shapes=list(scratch),
        input_output_aliases=aliases,
        compiler_params=pltpu.CompilerParams(vmem_limit_bytes=limit * MIB),
        cost_estimate=flops and pl.CostEstimate(flops=flops, bytes_accessed=0, transcendentals=0),
        name=name,
    )(*inputs)


def shards(queries, keys, values, order, nb):
    two, table = kernel(
        rotate_kernel,
        "rotate",
        ((16, 288, HD), (128,)),
        (order, nb.T, queries, keys, values),
        (
            pltpu.VMEM((3,) + queries.shape, BF),
            pltpu.VMEM((16, 288, HD), BF),
            pltpu.SemaphoreType.DMA((12,)),
            pltpu.SemaphoreType.DMA((4,)),
        ),
        limit=60,
        space=ANY,
    )
    two = exchanged(two)
    (one,) = kernel(early_kernel, "early", (SLOT,), (two,))
    l1, r1 = along_columns(one, 1), along_columns(one, -1)
    q_head, q_shared, main_left, main_right = kernel(
        middle_kernel, "middle", (SLOT, (16, 32, HD), SLOT, SLOT), (table, order, two), flops=FLOPS
    )
    l3, r3 = along_columns(main_right, 1), along_columns(main_left, -1)
    value_left, value_right, swap = kernel(
        late_kernel, "late", (SLOT, SLOT, (3,) + SLOT), (table, two, l1, r1)
    )
    l2, r2 = along_columns(value_right, 1), along_columns(value_left, -1)
    sw = swapped(swap)
    kh, prob, total = kernel(
        scores_kernel,
        "scores",
        (POOL, (2, WIN, 512, TOK_TILE), jax.ShapeDtypeStruct((2, 512, HD), F32)),
        (table, two, q_head, l1, r1, l3, r3),
        (pltpu.VMEM((WIN, TOK_TILE, TOK_TILE), F32),),
        flops=FLOPS,
    )
    state = [jax.ShapeDtypeStruct((2, TOK_TILE, n), F32) for n in (HD, TOK_TILE, HD)]
    k2, v2, *state = kernel(
        shared_kernel, "shared", (POOL, POOL, *state), (table, two, l1, r1, l3, r3, sw)
    )
    (far,) = kernel(forwarded_kernel, "forwarded", (SLOT,), (table, l2, r2, kh, k2))
    se = swapped(far)
    sent, o_oth, vh = kernel(
        first_kernel,
        "attend_first",
        (SENT, SLOT, PARTS),
        (table, two, l2, r2, prob, total),
        flops=FLOPS,
    )
    o_oth, k2, v2 = kernel(
        edge_kernel,
        "attend_edge",
        (SLOT, POOL, POOL),
        (table, far, l3, r3, se, *state, o_oth, k2, v2),
        aliases={8: 0, 9: 1, 10: 2},
    )
    o_left, o_right = along_columns(o_oth, 1), along_columns(o_oth, -1)
    (sent,) = kernel(
        last_kernel,
        "attend_last",
        (SENT,),
        (table, q_head, q_shared, kh, vh, k2, v2, sent),
        aliases={7: 0},
    )
    (sent,) = kernel(merge_kernel, "merge", (SENT,), (table, o_left, o_right, sent), aliases={3: 0})
    return kernel(unpack_kernel, "unpack", (queries.shape,), (exchanged(sent),))[0]


def solution(mesh):
    blk, uly, dp = (mesh.shape[name] for name in ("blk", "uly", "dp"))
    fine = Mesh(
        mesh.devices.reshape(blk // 2, 2, uly // 2, 2, dp), ("col", "half", "x", "core", "dp")
    )
    tokens = ("dp", "col", "half", "x", "core")
    placed = (P(tokens, None), P(tokens, None), P(tokens, None), P("dp"), P("dp", None))
    return jax.shard_map(
        shards, mesh=fine, in_specs=placed, out_specs=P(tokens, None), check_vma=False
    )
```

```python
import jax
import jax.numpy as jnp
import numpy as np
from jax import lax
from jax.experimental import pallas as pl
from jax.experimental.pallas import tpu as pltpu
from jax.sharding import Mesh
from jax.sharding import PartitionSpec as P

HD = 128
TOK_TILE = 256
WIN = 9
COLS = 8
GROUP = ("half", "x", "core")
VMEM = pl.BlockSpec(memory_space=pltpu.VMEM)
SMEM = pl.BlockSpec(memory_space=pltpu.SMEM)
ANY = pl.BlockSpec(memory_space=pl.ANY)
BF = jnp.bfloat16
F32 = jnp.float32
MIB = 1024 * 1024
POWER = HD ** (-0.5) * 1.4426950408889634
ONE, MAIN, VALUE = slice(0, 64), slice(64, 128), slice(128, 192)
QUERY, REST = slice(192, 224), slice(224, 288)
AT_W, AT_TILE, AT_HEAD, AT_SHARED = 0, 8, 16, 64
OTHER, THIS = 0, 1


def frequency_rows():
    pair = lax.broadcasted_iota(jnp.int32, (8, HD), 1) // 2
    nt = (HD - 4 * (HD // 6)) // 2
    ns = HD // 6
    rows = []
    for first, count in ((0, nt), (nt, ns), (nt + ns, ns)):
        within = (pair - first).astype(F32)
        freq = jnp.exp(within * float(-np.log(10000.0) / count))
        rows.append(jnp.where((pair >= first) & (pair < first + count), freq, 0.0)[0:1])
    return rows


def turns(tile, frame_in_tile):
    frame = (tile // 32 * 4 + frame_in_tile).astype(F32)
    row0 = (tile // 8 % 4 * 8).astype(F32)
    col0 = (tile % 8 * 8).astype(F32)
    token = lax.broadcasted_iota(jnp.int32, (64, HD), 0)
    row = row0 + (token // 8).astype(F32)
    col = col0 + (token % 8).astype(F32)
    by_frame, by_row, by_col = frequency_rows()
    angle = frame * by_frame + row * by_row + col * by_col
    cosine = jnp.cos(angle)
    sine = jnp.sin(angle)
    even = lax.broadcasted_iota(jnp.int32, (64, HD), 1) % 2 == 0
    return cosine, jnp.where(even, -sine, 0.0), jnp.where(even, 0.0, sine)


def turned(x, factors):
    here, after, before = factors
    x = x.astype(F32)
    return (x * here + pltpu.roll(x, HD - 1, 1) * after + pltpu.roll(x, 1, 1) * before).astype(BF)


def plan(order, nb, table):
    k = lax.axis_index("col")
    w = lax.rem(order[k * 4], COLS)
    table[AT_W] = w
    k_oth = lax.rem(jnp.where((w == 1) | (w == 7), k + 7, k + 1), COLS)
    near = jnp.where(w == 7, 7, 1)
    for column, base in ((OTHER, k_oth), (THIS, k)):
        low, high = 0, 2
        first = [0, 0]
        for t in range(4):
            upper = lax.rem(order[base * 4 + t] // 8, 4) < 2
            table[AT_TILE + 4 * column + jnp.where(upper, low, high)] = t
            first = [jnp.where(upper, t, first[0]), jnp.where(upper, first[1], t)]
            low, high = low + upper.astype(jnp.int32), high + 1 - upper.astype(jnp.int32)
        for p in range(2):
            counts = [0, 0, 0]
            for j in range(WIN):
                n = nb[j, base * 4 + first[p]]
                d = lax.rem(n // 4 - k + COLS, COLS)
                t = lax.rem(n, 4)
                at = WIN * (2 * column + p)
                table[AT_HEAD + at + j] = jnp.where(d == 0, 0, jnp.where(d == 1, 4, 8)) + t
                group = jnp.where(d == 0, 0, jnp.where(d == near, 1, 2))
                count = jnp.where(group == 0, counts[0], jnp.where(group == 1, counts[1], counts[2]))
                table[AT_SHARED + at + 3 * group + count] = 4 * group + t
                counts = [c + (group == g).astype(jnp.int32) for g, c in enumerate(counts)]
    return w


def rotate_kernel(order, nb, q_hbm, k_hbm, v_hbm, out_hbm, table, held, packed, sems, out_sems):
    x = lax.axis_index("x")
    frame_in_tile = lax.rem(x, 2) * 2 + lax.axis_index("core")
    slot = lax.axis_index("col") * 4 + lax.axis_index("half") * 2 + x // 2
    width = 2 * 3 * HD
    copies = []
    for part in range(4):
        for which, ref in enumerate((k_hbm, q_hbm, v_hbm)):
            columns = pl.ds(part * width, width)
            copies.append(
                pltpu.make_async_copy(
                    ref.at[:, columns], held.at[which, :, columns], sems.at[3 * part + which]
                )
            )
    for copy in copies:
        copy.start()
    w = plan(order, nb, table)
    edge = (w == 0) | (w == 7)
    factors = turns(order[slot], frame_in_tile)
    outs = []
    for part in range(4):
        for which in range(3):
            copies[3 * part + which].wait()
        for g in range(2 * part, 2 * part + 2):
            at = [slice((3 * g + h) * HD, (3 * g + h + 1) * HD) for h in range(3)]
            key = [turned(held[0, :, a], factors) for a in at]
            query = [held[1, :, a] for a in at]
            value = [held[2, :, a] for a in at]
            for c in range(2):
                to = 2 * g + c
                mine = slice(32 * c, 32 * c + 32)
                shared = jnp.concatenate([key[2][mine], value[2][mine]])
                packed[to, ONE, :] = jnp.where(edge, key[c], shared)
                packed[to, MAIN, :] = jnp.where(edge, query[c], key[c])
                packed[to, VALUE, :] = value[c]
                packed[to, QUERY, :] = query[2][mine]
                packed[to, REST, :] = jnp.where(edge, shared, query[c])
        four = pl.ds(4 * part, 4)
        outs.append(
            pltpu.make_async_copy(packed.at[four], out_hbm.at[four], out_sems.at[part])
        )
        outs[-1].start()
    for out in outs:
        out.wait()


def early_kernel(two, one):
    one[...] = two[:, ONE]


def middle_kernel(table, order, two, q_head, q_shared, main_left, main_right):
    w = table[AT_W]
    edge = (w == 0) | (w == 7)
    col, core = lax.axis_index("col"), lax.axis_index("core")

    @pl.loop(0, 16)
    def _(source):
        factors = turns(order[col * 4 + source // 4], lax.rem(source, 4))
        held = two[source]
        q_head[source] = turned(jnp.where(edge, held[MAIN], held[REST]), factors)
        mine = [jnp.where(core == 0, f[0:32], f[32:64]) for f in factors]
        q_shared[source] = turned(held[QUERY], mine)

    for out, special in ((main_left, 1), (main_right, 6)):

        @pl.when(w == special)
        def _(out=out):
            out[:, 0:32] = q_shared[...]
            out[:, 32:64] = q_shared[...]

        @pl.when(edge)
        def _(out=out):
            out[...] = q_head[...]

        @pl.when((w != special) & jnp.logical_not(edge))
        def _(out=out):
            out[...] = two[:, MAIN]


def late_kernel(table, two, l1, r1, value_left, value_right, swap):
    w = table[AT_W]
    edge = (w == 0) | (w == 7)
    for out, special, source in ((value_left, 1, r1), (value_right, 6, l1)):

        @pl.when(w == special)
        def _(out=out, source=source):
            out[...] = source[...]

        @pl.when(w != special)
        def _(out=out):
            out[...] = two[:, VALUE]

    @pl.when(edge)
    def _():
        swap[0] = two[:, REST]

    @pl.when(jnp.logical_not(edge))
    def _():
        swap[0] = two[:, ONE]

    swap[1] = l1[...]
    swap[2] = r1[...]


def steps(q, kp, vp, picks, state, at_once=1):
    top, weights, acc = state
    for start in range(0, len(picks), at_once):
        some = picks[start : start + at_once]
        scores = [
            lax.dot_general(q, kp[pick], (((1,), (1,)), ((), ())), preferred_element_type=F32)
            for pick in some
        ]
        high = scores[0]
        for s in scores[1:]:
            high = jnp.maximum(high, s)
        high = jnp.max(high, axis=1, keepdims=True)
        new = high if top is None else jnp.maximum(top, high)
        sums = part = None
        for pick, s in zip(some, scores):
            p = jnp.exp2((s - new) * POWER)
            product = jnp.dot(p.astype(BF), whole(vp, pick), preferred_element_type=F32)
            sums = p if sums is None else sums + p
            part = product if part is None else part + product
        if top is None:
            weights, acc = sums, part
        else:
            shrink = jnp.exp2((top - new) * POWER)
            weights, acc = weights * shrink + sums, acc * shrink + part
        top = new
    return top, weights, acc


def finished(state):
    _, weights, acc = state
    return (acc / jnp.sum(weights, axis=1, keepdims=True)).astype(BF)


def whole(ref, *index):
    return ref[index].reshape(-1, HD)


def pair_of(table, column, at, p, only=None):
    tiles = range(2) if only is None else (only,)
    fours = [pl.ds(table[AT_TILE + 4 * column + 2 * p + i] * 4, 4) for i in tiles]
    return fours, [table[at + (2 * column + p) * WIN + j] for j in range(WIN)]


def store_pair(store, fours, o):
    half = o.shape[0] // 2
    for i, four in enumerate(fours):
        store(four, o[i * half : (i + 1) * half].reshape(4, -1, HD))


def attend_column(table, column, at, query, kp, vp, store):
    @pl.loop(0, 2)
    def _(p):
        fours, picks = pair_of(table, column, at, p)
        q = jnp.concatenate([query(four) for four in fours])
        store_pair(store, fours, finished(steps(q, kp, vp, picks, (None, None, None))))


def fill_shared(base, mine, other, k2, v2):
    for t in range(4):
        four = slice(4 * t, 4 * t + 4)
        for pool, part in ((k2, slice(0, 32)), (v2, slice(32, 64))):
            pool[base + t, 0:128] = mine(four, part)
            pool[base + t, 128:256] = other(four, part)


def scores_kernel(table, two, q_head, l1, r1, l3, r3, kh, prob, total, s_ref):
    w = table[AT_W]
    inner = (w == 1) | (w == 6)
    edge = (w == 0) | (w == 7)

    @pl.when(jnp.logical_not(edge))
    def _():
        for t in range(4):
            kh[t] = whole(two, slice(4 * t, 4 * t + 4), MAIN)
        for base, special, early, later in ((4, 6, r1, r3), (8, 1, l1, l3)):

            @pl.when(w == special)
            def _(base=base, early=early):
                for t in range(4):
                    kh[base + t] = whole(early, slice(4 * t, 4 * t + 4))

            @pl.when(w != special)
            def _(base=base, later=later):
                for t in range(4):
                    kh[base + t] = whole(later, slice(4 * t, 4 * t + 4))

    @pl.when(jnp.logical_not(edge))
    def _():
        column = jnp.where(inner, OTHER, THIS)

        @pl.loop(0, 4)
        def _(n):
            p, i = n // 2, lax.rem(n, 2)
            fours, picks = pair_of(table, column, AT_HEAD, p, i)
            four = fours[0]
            q = jnp.where(w == 1, whole(l3, four), jnp.where(w == 6, whole(r3, four), whole(q_head, four)))
            rows = pl.ds(pl.multiple_of(i * TOK_TILE, TOK_TILE), TOK_TILE)
            top = None
            for j, pick in enumerate(picks):
                s = lax.dot_general(q, kh[pick], (((1,), (1,)), ((), ())), preferred_element_type=F32)
                s_ref[j] = s
                top = s if top is None else jnp.maximum(top, s)
            top = jnp.max(top, axis=1, keepdims=True)
            sums = None
            for j in range(WIN):
                weights = jnp.exp2((s_ref[j] - top) * POWER)
                sums = weights if sums is None else sums + weights
                prob[p, j, rows, :] = weights.astype(BF)
            sums = jnp.sum(sums, axis=1, keepdims=True)
            total[p, rows, :] = jnp.broadcast_to(sums, (TOK_TILE, HD))


def shared_kernel(table, two, l1, r1, l3, r3, sw, k2, v2, tops, weights, accs):
    w = table[AT_W]
    edge = (w == 0) | (w == 7)
    left = (lambda f, p: whole(l1, f, p)), (lambda f, p: whole(sw, 1, f, p))
    right = (lambda f, p: whole(r1, f, p)), (lambda f, p: whole(sw, 2, f, p))

    def own(rows):
        mine = lambda f, p: whole(two, f, slice(rows.start + p.start, rows.start + p.stop))
        fill_shared(0, mine, lambda f, p: whole(sw, 0, f, p), k2, v2)

    @pl.when(jnp.logical_not(edge))
    def _():
        own(ONE)
        fill_shared(4, *right, k2, v2)
        fill_shared(8, *left, k2, v2)

    @pl.when(edge)
    def _():
        own(REST)
        for special, near in ((0, right), (7, left)):

            @pl.when(w == special)
            def _(near=near):
                fill_shared(4, *near, k2, v2)

        @pl.loop(0, 2)
        def _(p):
            fours, picks = pair_of(table, OTHER, AT_SHARED, p)
            top, sums, acc = steps(asked(w, l3, r3, fours), k2, v2, picks[0:6], (None, None, None))
            tops[p] = jnp.broadcast_to(top, acc.shape)
            weights[p] = sums
            accs[p] = acc


def asked(w, l3, r3, fours):
    half = slice(0, 32)
    return jnp.concatenate(
        [jnp.where(w == 7, whole(l3, four, half), whole(r3, four, half)) for four in fours]
    )


def forwarded_kernel(table, l2, r2, kh, k2, out):
    del kh, k2
    w = table[AT_W]

    @pl.when(w == 0)
    def _():
        out[...] = r2[...]

    @pl.when(w == 7)
    def _():
        out[...] = l2[...]


def first_kernel(table, two, l2, r2, prob, total, sent, o_oth, vh):
    w = table[AT_W]
    inner = (w == 1) | (w == 6)
    edge = (w == 0) | (w == 7)

    @pl.when(jnp.logical_not(edge))
    def _():
        for t in range(4):
            four = slice(4 * t, 4 * t + 4)
            vh[t] = two[four, VALUE]
            vh[4 + t] = r2[four]
            vh[8 + t] = l2[four]

        column = jnp.where(inner, OTHER, THIS)

        @pl.loop(0, 2)
        def _(p):
            fours, picks = pair_of(table, column, AT_HEAD, p)
            acc = None
            for j, pick in enumerate(picks):
                part = jnp.dot(prob[p, j], whole(vh, pick), preferred_element_type=F32)
                acc = part if acc is None else acc + part

            def store(four, o):
                o_oth[four] = o
                sent[four, 0:64] = o

            store_pair(store, fours, (acc / total[p]).astype(BF))


def edge_kernel(table, far, l3, r3, se, tops, weights, accs, oth_in, k_in, v_in, o_oth, k2, v2):
    del oth_in, k_in, v_in
    w = table[AT_W]

    def to_other(four, o):
        o_oth[four, 0:32] = o

    @pl.when((w == 0) | (w == 7))
    def _():
        fill_shared(8, lambda f, p: whole(far, f, p), lambda f, p: whole(se, f, p), k2, v2)

        done = []
        for p in range(2):
            fours, picks = pair_of(table, OTHER, AT_SHARED, p)
            state = tops[p, :, 0:1], weights[p], accs[p]
            q = asked(w, l3, r3, fours)
            done.append((fours, finished(steps(q, k2, v2, picks[6:9], state, 3))))
        for fours, o in done:
            store_pair(to_other, fours, o)


def last_kernel(table, q_head, q_shared, kh, vh, k2, v2, sent_in, sent):
    del sent_in
    w = table[AT_W]
    inner = (w == 1) | (w == 6)

    def to_head(four, o):
        sent[four, 0:64] = o

    def to_shared(four, o):
        sent[four, 64:96] = o

    @pl.when(inner)
    def _():
        query = lambda four: whole(q_head, four)
        attend_column(table, THIS, AT_HEAD, query, kh, vh, to_head)

    @pl.when(jnp.logical_not(inner))
    def _():
        query = lambda four: whole(q_shared, four)
        attend_column(table, THIS, AT_SHARED, query, k2, v2, to_shared)


def merge_kernel(table, o_left, o_right, sent_in, sent):
    del sent_in
    w = table[AT_W]

    @pl.when(w == 0)
    def _():
        sent[:, 0:64] = o_right[...]

    @pl.when(w == 7)
    def _():
        sent[:, 0:64] = o_left[...]

    @pl.when(w == 1)
    def _():
        sent[:, 64:96] = o_left[:, 0:32]

    @pl.when(w == 6)
    def _():
        sent[:, 64:96] = o_right[:, 0:32]


def unpack_kernel(in_ref, out_ref):
    for g in range(8):
        for h in range(2):
            out_ref[:, (3 * g + h) * HD : (3 * g + h + 1) * HD] = in_ref[2 * g + h, 0:64, :]
        last = slice((3 * g + 2) * HD, (3 * g + 3) * HD)
        out_ref[0:32, last] = in_ref[2 * g, 64:96, :]
        out_ref[32:64, last] = in_ref[2 * g + 1, 64:96, :]


def along_columns(block, distance):
    n = 2 * COLS
    return lax.ppermute(block, ("col", "half"), [(i, (i + 2 * distance) % n) for i in range(n)])


def swapped(block):
    return lax.ppermute(block, "core", [(0, 1), (1, 0)])


def exchanged(block):
    return lax.all_to_all(block, GROUP, split_axis=0, concat_axis=0, tiled=True)


SLOT = (16, 64, HD)
SENT = (16, 96, HD)
POOL = (12, TOK_TILE, HD)
PARTS = (12, 4, 64, HD)
FLOPS = 20_000_000_000


def kernel(body, name, outs, inputs, scratch=(), limit=32, aliases={}, flops=None, space=VMEM):
    outs = [
        out
        if isinstance(out, jax.ShapeDtypeStruct)
        else jax.ShapeDtypeStruct(out, BF if len(out) > 1 else jnp.int32)
        for out in outs
    ]
    return pl.pallas_call(
        body,
        out_shape=tuple(outs),
        in_specs=[SMEM if i.dtype == jnp.int32 else space for i in inputs],
        out_specs=tuple(SMEM if out.dtype == jnp.int32 else space for out in outs),
        scratch_shapes=list(scratch),
        input_output_aliases=aliases,
        compiler_params=pltpu.CompilerParams(vmem_limit_bytes=limit * MIB),
        cost_estimate=flops and pl.CostEstimate(flops=flops, bytes_accessed=0, transcendentals=0),
        name=name,
    )(*inputs)


def shards(queries, keys, values, order, nb):
    two, table = kernel(
        rotate_kernel,
        "rotate",
        ((16, 288, HD), (128,)),
        (order, nb.T, queries, keys, values),
        (
            pltpu.VMEM((3,) + queries.shape, BF),
            pltpu.VMEM((16, 288, HD), BF),
            pltpu.SemaphoreType.DMA((12,)),
            pltpu.SemaphoreType.DMA((4,)),
        ),
        limit=60,
        space=ANY,
    )
    two = exchanged(two)
    (one,) = kernel(early_kernel, "early", (SLOT,), (two,))
    l1, r1 = along_columns(one, 1), along_columns(one, -1)
    q_head, q_shared, main_left, main_right = kernel(
        middle_kernel, "middle", (SLOT, (16, 32, HD), SLOT, SLOT), (table, order, two), flops=FLOPS
    )
    l3, r3 = along_columns(main_right, 1), along_columns(main_left, -1)
    value_left, value_right, swap = kernel(
        late_kernel, "late", (SLOT, SLOT, (3,) + SLOT), (table, two, l1, r1)
    )
    l2, r2 = along_columns(value_right, 1), along_columns(value_left, -1)
    sw = swapped(swap)
    kh, prob, total = kernel(
        scores_kernel,
        "scores",
        (POOL, (2, WIN, 512, TOK_TILE), jax.ShapeDtypeStruct((2, 512, HD), F32)),
        (table, two, q_head, l1, r1, l3, r3),
        (pltpu.VMEM((WIN, TOK_TILE, TOK_TILE), F32),),
        flops=FLOPS,
    )
    state = [jax.ShapeDtypeStruct((2, TOK_TILE, n), F32) for n in (HD, TOK_TILE, HD)]
    k2, v2, *state = kernel(
        shared_kernel, "shared", (POOL, POOL, *state), (table, two, l1, r1, l3, r3, sw)
    )
    (far,) = kernel(forwarded_kernel, "forwarded", (SLOT,), (table, l2, r2, kh, k2))
    se = swapped(far)
    sent, o_oth, vh = kernel(
        first_kernel,
        "attend_first",
        (SENT, SLOT, PARTS),
        (table, two, l2, r2, prob, total),
        flops=FLOPS,
    )
    o_oth, k2, v2 = kernel(
        edge_kernel,
        "attend_edge",
        (SLOT, POOL, POOL),
        (table, far, l3, r3, se, *state, o_oth, k2, v2),
        aliases={8: 0, 9: 1, 10: 2},
    )
    o_left, o_right = along_columns(o_oth, 1), along_columns(o_oth, -1)
    (sent,) = kernel(
        last_kernel,
        "attend_last",
        (SENT,),
        (table, q_head, q_shared, kh, vh, k2, v2, sent),
        aliases={7: 0},
    )
    (sent,) = kernel(merge_kernel, "merge", (SENT,), (table, o_left, o_right, sent), aliases={3: 0})
    return kernel(unpack_kernel, "unpack", (queries.shape,), (exchanged(sent),))[0]


def solution(mesh):
    blk, uly, dp = (mesh.shape[name] for name in ("blk", "uly", "dp"))
    fine = Mesh(
        mesh.devices.reshape(blk // 2, 2, uly // 2, 2, dp), ("col", "half", "x", "core", "dp")
    )
    tokens = ("dp", "col", "half", "x", "core")
    placed = (P(tokens, None), P(tokens, None), P(tokens, None), P("dp"), P("dp", None))
    return jax.shard_map(
        shards, mesh=fine, in_specs=placed, out_specs=P(tokens, None), check_vma=False
    )
```

```python
import jax
import jax.numpy as jnp
import numpy as np
from jax import lax
from jax.experimental import pallas as pl
from jax.experimental.pallas import tpu as pltpu
from jax.sharding import Mesh
from jax.sharding import PartitionSpec as P

HD = 128
TOK_TILE = 256
WIN = 9
COLS = 8
GROUP = ("half", "x", "core")
VMEM = pl.BlockSpec(memory_space=pltpu.VMEM)
SMEM = pl.BlockSpec(memory_space=pltpu.SMEM)
ANY = pl.BlockSpec(memory_space=pl.ANY)
BF = jnp.bfloat16
F32 = jnp.float32
MIB = 1024 * 1024
POWER = HD ** (-0.5) * 1.4426950408889634
ONE, MAIN, VALUE = slice(0, 64), slice(64, 128), slice(128, 192)
QUERY, REST = slice(192, 224), slice(224, 288)
AT_W, AT_TILE, AT_HEAD, AT_SHARED = 0, 8, 16, 64
OTHER, THIS = 0, 1


def frequency_rows():
    pair = lax.broadcasted_iota(jnp.int32, (8, HD), 1) // 2
    nt = (HD - 4 * (HD // 6)) // 2
    ns = HD // 6
    rows = []
    for first, count in ((0, nt), (nt, ns), (nt + ns, ns)):
        within = (pair - first).astype(F32)
        freq = jnp.exp(within * float(-np.log(10000.0) / count))
        rows.append(jnp.where((pair >= first) & (pair < first + count), freq, 0.0)[0:1])
    return rows


def turns(tile, frames):
    row0 = (tile // 8 % 4 * 8).astype(F32)
    col0 = (tile % 8 * 8).astype(F32)
    token = lax.broadcasted_iota(jnp.int32, (64, HD), 0)
    row = row0 + (token // 8).astype(F32)
    col = col0 + (token % 8).astype(F32)
    by_frame, by_row, by_col = frequency_rows()
    angle = row * by_row + col * by_col
    cosine, sine = jnp.cos(angle), jnp.sin(angle)
    even = lax.broadcasted_iota(jnp.int32, (64, HD), 1) % 2 == 0
    found = []
    for frame in frames:
        turn = (tile // 32 * 4 + frame).astype(F32) * by_frame
        c, s = cosine * jnp.cos(turn), sine + jnp.sin(turn)
        found.append((c, jnp.where(even, -s, 0.0), jnp.where(even, 0.0, s)))
    return found


def turned(x, factors):
    here, after, before = factors
    x = x.astype(F32)
    return (x * here + pltpu.roll(x, HD - 1, 1) * after + pltpu.roll(x, 1, 1) * before).astype(BF)


def plan(order, nb, table):
    k = lax.axis_index("col")
    w = lax.rem(order[k * 4], COLS)
    table[AT_W] = w
    k_oth = lax.rem(jnp.where((w == 1) | (w == 7), k + 7, k + 1), COLS)
    near = jnp.where(w == 7, 7, 1)
    for column, base in ((OTHER, k_oth), (THIS, k)):
        low, high = 0, 2
        first = [0, 0]
        for t in range(4):
            upper = lax.rem(order[base * 4 + t] // 8, 4) < 2
            table[AT_TILE + 4 * column + jnp.where(upper, low, high)] = t
            first = [jnp.where(upper, t, first[0]), jnp.where(upper, first[1], t)]
            low, high = low + upper.astype(jnp.int32), high + 1 - upper.astype(jnp.int32)
        for p in range(2):
            counts = [0, 0, 0]
            for j in range(WIN):
                n = nb[j, base * 4 + first[p]]
                d = lax.rem(n // 4 - k + COLS, COLS)
                t = lax.rem(n, 4)
                at = WIN * (2 * column + p)
                table[AT_HEAD + at + j] = jnp.where(d == 0, 0, jnp.where(d == 1, 4, 8)) + t
                group = jnp.where(d == 0, 0, jnp.where(d == near, 1, 2))
                count = jnp.where(group == 0, counts[0], jnp.where(group == 1, counts[1], counts[2]))
                table[AT_SHARED + at + 3 * group + count] = 4 * group + t
                counts = [c + (group == g).astype(jnp.int32) for g, c in enumerate(counts)]
    return w


def rotate_kernel(order, nb, q_hbm, k_hbm, v_hbm, out_hbm, table, held, packed, sems, out_sems):
    x = lax.axis_index("x")
    frame_in_tile = lax.rem(x, 2) * 2 + lax.axis_index("core")
    slot = lax.axis_index("col") * 4 + lax.axis_index("half") * 2 + x // 2
    width = 2 * 3 * HD
    copies = []
    for part in range(4):
        for which, ref in enumerate((k_hbm, q_hbm, v_hbm)):
            columns = pl.ds(part * width, width)
            copies.append(
                pltpu.make_async_copy(
                    ref.at[:, columns], held.at[which, :, columns], sems.at[3 * part + which]
                )
            )
    for copy in copies:
        copy.start()
    w = plan(order, nb, table)
    edge = (w == 0) | (w == 7)
    (factors,) = turns(order[slot], [frame_in_tile])
    outs = []
    for part in range(4):
        for which in range(3):
            copies[3 * part + which].wait()
        for g in range(2 * part, 2 * part + 2):
            at = [slice((3 * g + h) * HD, (3 * g + h + 1) * HD) for h in range(3)]
            key = [turned(held[0, :, a], factors) for a in at]
            query = [held[1, :, a] for a in at]
            value = [held[2, :, a] for a in at]
            for c in range(2):
                to = 2 * g + c
                mine = slice(32 * c, 32 * c + 32)
                shared = jnp.concatenate([key[2][mine], value[2][mine]])
                packed[to, ONE, :] = jnp.where(edge, key[c], shared)
                packed[to, MAIN, :] = jnp.where(edge, query[c], key[c])
                packed[to, VALUE, :] = value[c]
                packed[to, QUERY, :] = query[2][mine]
                packed[to, REST, :] = jnp.where(edge, shared, query[c])
        four = pl.ds(4 * part, 4)
        outs.append(
            pltpu.make_async_copy(packed.at[four], out_hbm.at[four], out_sems.at[part])
        )
        outs[-1].start()
    for out in outs:
        out.wait()


def early_kernel(two, one):
    one[...] = two[:, ONE]


def middle_kernel(table, order, two, q_head, q_shared, main_left, main_right):
    w = table[AT_W]
    edge = (w == 0) | (w == 7)
    col, core = lax.axis_index("col"), lax.axis_index("core")

    @pl.loop(0, 4)
    def _(t):
        for frame, factors in enumerate(turns(order[col * 4 + t], range(4))):
            source = t * 4 + frame
            held = two[source]
            q_head[source] = turned(jnp.where(edge, held[MAIN], held[REST]), factors)
            mine = [jnp.where(core == 0, f[0:32], f[32:64]) for f in factors]
            q_shared[source] = turned(held[QUERY], mine)

    for out, special in ((main_left, 1), (main_right, 6)):

        @pl.when(w == special)
        def _(out=out):
            out[:, 0:32] = q_shared[...]
            out[:, 32:64] = q_shared[...]

        @pl.when(edge)
        def _(out=out):
            out[...] = q_head[...]

        @pl.when((w != special) & jnp.logical_not(edge))
        def _(out=out):
            out[...] = two[:, MAIN]


def late_kernel(table, two, l1, r1, value_left, value_right, swap):
    w = table[AT_W]
    edge = (w == 0) | (w == 7)
    for out, special, source in ((value_left, 1, r1), (value_right, 6, l1)):

        @pl.when(w == special)
        def _(out=out, source=source):
            out[...] = source[...]

        @pl.when(w != special)
        def _(out=out):
            out[...] = two[:, VALUE]

    @pl.when(edge)
    def _():
        swap[0] = two[:, REST]

    @pl.when(jnp.logical_not(edge))
    def _():
        swap[0] = two[:, ONE]

    swap[1] = l1[...]
    swap[2] = r1[...]


def steps(q, kp, vp, picks, state, at_once=1):
    top, weights, acc = state
    for start in range(0, len(picks), at_once):
        some = picks[start : start + at_once]
        scores = [
            lax.dot_general(q, kp[pick], (((1,), (1,)), ((), ())), preferred_element_type=F32)
            for pick in some
        ]
        high = scores[0]
        for s in scores[1:]:
            high = jnp.maximum(high, s)
        high = jnp.max(high, axis=1, keepdims=True)
        new = high if top is None else jnp.maximum(top, high)
        sums = part = None
        for pick, s in zip(some, scores):
            p = jnp.exp2((s - new) * POWER)
            product = jnp.dot(p.astype(BF), whole(vp, pick), preferred_element_type=F32)
            sums = p if sums is None else sums + p
            part = product if part is None else part + product
        if top is None:
            weights, acc = sums, part
        else:
            shrink = jnp.exp2((top - new) * POWER)
            weights, acc = weights * shrink + sums, acc * shrink + part
        top = new
    return top, weights, acc


def finished(state):
    _, weights, acc = state
    return (acc / jnp.sum(weights, axis=1, keepdims=True)).astype(BF)


def whole(ref, *index):
    return ref[index].reshape(-1, HD)


def pair_of(table, column, at, p, only=None):
    tiles = range(2) if only is None else (only,)
    fours = [pl.ds(table[AT_TILE + 4 * column + 2 * p + i] * 4, 4) for i in tiles]
    return fours, [table[at + (2 * column + p) * WIN + j] for j in range(WIN)]


def store_pair(store, fours, o):
    half = o.shape[0] // 2
    for i, four in enumerate(fours):
        store(four, o[i * half : (i + 1) * half].reshape(4, -1, HD))


def attend_column(table, column, at, query, kp, vp, store):
    @pl.loop(0, 2)
    def _(p):
        fours, picks = pair_of(table, column, at, p)
        q = jnp.concatenate([query(four) for four in fours])
        store_pair(store, fours, finished(steps(q, kp, vp, picks, (None, None, None))))


def fill_shared(base, mine, other, k2, v2):
    for t in range(4):
        four = slice(4 * t, 4 * t + 4)
        for pool, part in ((k2, slice(0, 32)), (v2, slice(32, 64))):
            pool[base + t, 0:128] = mine(four, part)
            pool[base + t, 128:256] = other(four, part)


def scores_kernel(table, two, q_head, l1, r1, l3, r3, kh, prob, total, s_ref):
    w = table[AT_W]
    inner = (w == 1) | (w == 6)
    edge = (w == 0) | (w == 7)

    @pl.when(jnp.logical_not(edge))
    def _():
        for t in range(4):
            kh[t] = whole(two, slice(4 * t, 4 * t + 4), MAIN)
        for base, special, early, later in ((4, 6, r1, r3), (8, 1, l1, l3)):

            @pl.when(w == special)
            def _(base=base, early=early):
                for t in range(4):
                    kh[base + t] = whole(early, slice(4 * t, 4 * t + 4))

            @pl.when(w != special)
            def _(base=base, later=later):
                for t in range(4):
                    kh[base + t] = whole(later, slice(4 * t, 4 * t + 4))

    @pl.when(jnp.logical_not(edge))
    def _():
        column = jnp.where(inner, OTHER, THIS)

        @pl.loop(0, 4)
        def _(n):
            p, i = n // 2, lax.rem(n, 2)
            fours, picks = pair_of(table, column, AT_HEAD, p, i)
            four = fours[0]
            q = jnp.where(w == 1, whole(l3, four), jnp.where(w == 6, whole(r3, four), whole(q_head, four)))
            rows = pl.ds(pl.multiple_of(i * TOK_TILE, TOK_TILE), TOK_TILE)
            top = None
            for j, pick in enumerate(picks):
                s = lax.dot_general(q, kh[pick], (((1,), (1,)), ((), ())), preferred_element_type=F32)
                s_ref[j] = s
                top = s if top is None else jnp.maximum(top, s)
            top = jnp.max(top, axis=1, keepdims=True)
            sums = None
            for j in range(WIN):
                weights = jnp.exp2((s_ref[j] - top) * POWER)
                sums = weights if sums is None else sums + weights
                prob[p, j, rows, :] = weights.astype(BF)
            sums = jnp.sum(sums, axis=1, keepdims=True)
            total[p, rows, :] = jnp.broadcast_to(sums, (TOK_TILE, HD))


def shared_kernel(table, two, l1, r1, l3, r3, sw, k2, v2, tops, weights, accs):
    w = table[AT_W]
    edge = (w == 0) | (w == 7)
    left = (lambda f, p: whole(l1, f, p)), (lambda f, p: whole(sw, 1, f, p))
    right = (lambda f, p: whole(r1, f, p)), (lambda f, p: whole(sw, 2, f, p))

    def own(rows):
        mine = lambda f, p: whole(two, f, slice(rows.start + p.start, rows.start + p.stop))
        fill_shared(0, mine, lambda f, p: whole(sw, 0, f, p), k2, v2)

    @pl.when(jnp.logical_not(edge))
    def _():
        own(ONE)
        fill_shared(4, *right, k2, v2)
        fill_shared(8, *left, k2, v2)

    @pl.when(edge)
    def _():
        own(REST)
        for special, near in ((0, right), (7, left)):

            @pl.when(w == special)
            def _(near=near):
                fill_shared(4, *near, k2, v2)

        @pl.loop(0, 2)
        def _(p):
            fours, picks = pair_of(table, OTHER, AT_SHARED, p)
            top, sums, acc = steps(asked(w, l3, r3, fours), k2, v2, picks[0:6], (None, None, None))
            tops[p] = jnp.broadcast_to(top, acc.shape)
            weights[p] = sums
            accs[p] = acc


def asked(w, l3, r3, fours):
    half = slice(0, 32)
    return jnp.concatenate(
        [jnp.where(w == 7, whole(l3, four, half), whole(r3, four, half)) for four in fours]
    )


def forwarded_kernel(table, l2, r2, kh, k2, out):
    del kh, k2
    w = table[AT_W]

    @pl.when(w == 0)
    def _():
        out[...] = r2[...]

    @pl.when(w == 7)
    def _():
        out[...] = l2[...]


def first_kernel(table, two, l2, r2, prob, total, sent, o_oth, vh):
    w = table[AT_W]
    inner = (w == 1) | (w == 6)
    edge = (w == 0) | (w == 7)

    @pl.when(jnp.logical_not(edge))
    def _():
        for t in range(4):
            four = slice(4 * t, 4 * t + 4)
            vh[t] = two[four, VALUE]
            vh[4 + t] = r2[four]
            vh[8 + t] = l2[four]

        column = jnp.where(inner, OTHER, THIS)

        @pl.loop(0, 2)
        def _(p):
            fours, picks = pair_of(table, column, AT_HEAD, p)
            acc = None
            for j, pick in enumerate(picks):
                part = jnp.dot(prob[p, j], whole(vh, pick), preferred_element_type=F32)
                acc = part if acc is None else acc + part

            def store(four, o):
                o_oth[four] = o
                sent[four, 0:64] = o

            store_pair(store, fours, (acc / total[p]).astype(BF))


def edge_kernel(table, far, l3, r3, se, tops, weights, accs, oth_in, k_in, v_in, o_oth, k2, v2):
    del oth_in, k_in, v_in
    w = table[AT_W]

    def to_other(four, o):
        o_oth[four, 0:32] = o

    @pl.when((w == 0) | (w == 7))
    def _():
        fill_shared(8, lambda f, p: whole(far, f, p), lambda f, p: whole(se, f, p), k2, v2)

        done = []
        for p in range(2):
            fours, picks = pair_of(table, OTHER, AT_SHARED, p)
            state = tops[p, :, 0:1], weights[p], accs[p]
            q = asked(w, l3, r3, fours)
            done.append((fours, finished(steps(q, k2, v2, picks[6:9], state, 3))))
        for fours, o in done:
            store_pair(to_other, fours, o)


def last_kernel(table, q_head, q_shared, kh, vh, k2, v2, sent_in, sent):
    del sent_in
    w = table[AT_W]
    inner = (w == 1) | (w == 6)

    def to_head(four, o):
        sent[four, 0:64] = o

    def to_shared(four, o):
        sent[four, 64:96] = o

    @pl.when(inner)
    def _():
        query = lambda four: whole(q_head, four)
        attend_column(table, THIS, AT_HEAD, query, kh, vh, to_head)

    @pl.when(jnp.logical_not(inner))
    def _():
        query = lambda four: whole(q_shared, four)
        attend_column(table, THIS, AT_SHARED, query, k2, v2, to_shared)


def merge_kernel(table, o_left, o_right, sent_in, sent):
    del sent_in
    w = table[AT_W]

    @pl.when(w == 0)
    def _():
        sent[:, 0:64] = o_right[...]

    @pl.when(w == 7)
    def _():
        sent[:, 0:64] = o_left[...]

    @pl.when(w == 1)
    def _():
        sent[:, 64:96] = o_left[:, 0:32]

    @pl.when(w == 6)
    def _():
        sent[:, 64:96] = o_right[:, 0:32]


def unpack_kernel(in_ref, out_ref):
    for g in range(8):
        for h in range(2):
            out_ref[:, (3 * g + h) * HD : (3 * g + h + 1) * HD] = in_ref[2 * g + h, 0:64, :]
        last = slice((3 * g + 2) * HD, (3 * g + 3) * HD)
        out_ref[0:32, last] = in_ref[2 * g, 64:96, :]
        out_ref[32:64, last] = in_ref[2 * g + 1, 64:96, :]


def along_columns(block, distance):
    n = 2 * COLS
    return lax.ppermute(block, ("col", "half"), [(i, (i + 2 * distance) % n) for i in range(n)])


def swapped(block):
    return lax.ppermute(block, "core", [(0, 1), (1, 0)])


def exchanged(block):
    return lax.all_to_all(block, GROUP, split_axis=0, concat_axis=0, tiled=True)


SLOT = (16, 64, HD)
SENT = (16, 96, HD)
POOL = (12, TOK_TILE, HD)
PARTS = (12, 4, 64, HD)
FLOPS = 20_000_000_000


def kernel(body, name, outs, inputs, scratch=(), limit=32, aliases={}, flops=None, space=VMEM):
    outs = [
        out
        if isinstance(out, jax.ShapeDtypeStruct)
        else jax.ShapeDtypeStruct(out, BF if len(out) > 1 else jnp.int32)
        for out in outs
    ]
    return pl.pallas_call(
        body,
        out_shape=tuple(outs),
        in_specs=[SMEM if i.dtype == jnp.int32 else space for i in inputs],
        out_specs=tuple(SMEM if out.dtype == jnp.int32 else space for out in outs),
        scratch_shapes=list(scratch),
        input_output_aliases=aliases,
        compiler_params=pltpu.CompilerParams(vmem_limit_bytes=limit * MIB),
        cost_estimate=flops and pl.CostEstimate(flops=flops, bytes_accessed=0, transcendentals=0),
        name=name,
    )(*inputs)


def shards(queries, keys, values, order, nb):
    two, table = kernel(
        rotate_kernel,
        "rotate",
        ((16, 288, HD), (128,)),
        (order, nb.T, queries, keys, values),
        (
            pltpu.VMEM((3,) + queries.shape, BF),
            pltpu.VMEM((16, 288, HD), BF),
            pltpu.SemaphoreType.DMA((12,)),
            pltpu.SemaphoreType.DMA((4,)),
        ),
        limit=60,
        space=ANY,
    )
    two = exchanged(two)
    (one,) = kernel(early_kernel, "early", (SLOT,), (two,))
    l1, r1 = along_columns(one, 1), along_columns(one, -1)
    q_head, q_shared, main_left, main_right = kernel(
        middle_kernel, "middle", (SLOT, (16, 32, HD), SLOT, SLOT), (table, order, two), flops=FLOPS
    )
    l3, r3 = along_columns(main_right, 1), along_columns(main_left, -1)
    value_left, value_right, swap = kernel(
        late_kernel, "late", (SLOT, SLOT, (3,) + SLOT), (table, two, l1, r1)
    )
    l2, r2 = along_columns(value_right, 1), along_columns(value_left, -1)
    sw = swapped(swap)
    kh, prob, total = kernel(
        scores_kernel,
        "scores",
        (POOL, (2, WIN, 512, TOK_TILE), jax.ShapeDtypeStruct((2, 512, HD), F32)),
        (table, two, q_head, l1, r1, l3, r3),
        (pltpu.VMEM((WIN, TOK_TILE, TOK_TILE), F32),),
        flops=FLOPS,
    )
    state = [jax.ShapeDtypeStruct((2, TOK_TILE, n), F32) for n in (HD, TOK_TILE, HD)]
    k2, v2, *state = kernel(
        shared_kernel, "shared", (POOL, POOL, *state), (table, two, l1, r1, l3, r3, sw)
    )
    (far,) = kernel(forwarded_kernel, "forwarded", (SLOT,), (table, l2, r2, kh, k2))
    se = swapped(far)
    sent, o_oth, vh = kernel(
        first_kernel,
        "attend_first",
        (SENT, SLOT, PARTS),
        (table, two, l2, r2, prob, total),
        flops=FLOPS,
    )
    o_oth, k2, v2 = kernel(
        edge_kernel,
        "attend_edge",
        (SLOT, POOL, POOL),
        (table, far, l3, r3, se, *state, o_oth, k2, v2),
        aliases={8: 0, 9: 1, 10: 2},
    )
    o_left, o_right = along_columns(o_oth, 1), along_columns(o_oth, -1)
    (sent,) = kernel(
        last_kernel,
        "attend_last",
        (SENT,),
        (table, q_head, q_shared, kh, vh, k2, v2, sent),
        aliases={7: 0},
    )
    (sent,) = kernel(merge_kernel, "merge", (SENT,), (table, o_left, o_right, sent), aliases={3: 0})
    return kernel(unpack_kernel, "unpack", (queries.shape,), (exchanged(sent),))[0]


def solution(mesh):
    blk, uly, dp = (mesh.shape[name] for name in ("blk", "uly", "dp"))
    fine = Mesh(
        mesh.devices.reshape(blk // 2, 2, uly // 2, 2, dp), ("col", "half", "x", "core", "dp")
    )
    tokens = ("dp", "col", "half", "x", "core")
    placed = (P(tokens, None), P(tokens, None), P(tokens, None), P("dp"), P("dp", None))
    return jax.shard_map(
        shards, mesh=fine, in_specs=placed, out_specs=P(tokens, None), check_vma=False
    )
```
